128 devices in a mesh: prow: 16 (over y, x), pcol: 8 (over z, core).
Axes of the slice: x: 4, y: 4, z: 4, core: 2. Of those that a mesh axis runs over, the one named last changes fastest.
Arguments:
- front: float32 [2, 4096, 4, 2048], P(None, 'prow', None, 'pcol')
- partials: float32 [128, 128, 8, 256], P(('prow', 'pcol')), may hold values from -6 to 6
- targets: int32 [128, 128, 8], P(('prow', 'pcol')), may hold values from 0 to 2047
- counts: int32 [128, 128], P(('prow', 'pcol')), may hold values from 0 to 8, as said below
- local_picks: int32 [2, 16, 256], replicated, may hold values from 0 to 511, as said below
- level_picks: int32 [2, 4, 16, 256], replicated, may hold values from 0 to 511, as said below
- order: int32 [2, 256], replicated, may hold values from 0 to 255, as said below
Outputs:
- factored: float32 [2, 4096, 4, 2048], P(None, 'prow', None, 'pcol')
The draws below stay inside these ranges and needn't reach their ends.
Inputs may be any that keep to these rules, and one draw needn't show every extreme that they name: `targets`: code c names local row c // 4 and local tile column c % 4 of the owner's block; codes of unused slots are arbitrary and ignored. `counts`: in every draw some owner receives 8 rows from every source. For panel k, row p of local_picks names 256 different local rows of prow index p, none of them a winner of an earlier panel. `level_picks`: each list names 256 different positions; at level l the lists of indices that differ only in bits 0 .. l are equal. `order`: each row is a permutation.
All inputs are finite; a program needn't handle non-finite values.
Results may differ from the reference program's by a relative error of at most 0.0001.
Values sent between devices are 32-bit elements; how exact they have to be, the bound alone decides.
No kernel may reach another device: no remote copies, remote signals or barrier semaphores. Data moves between devices by JAX's collectives and lax.ppermute only.
A program may use at most 64 MiB of HBM per device.

```python
import jax
import jax.numpy as jnp
from jax import lax

B = 256
NF = 8192
PANELS = 2
SLOT = 8
LEVELS = 4
RTD = 2
CTD = 4
N_PROW = 16
N_PCOL = 8
DEVICES = 128


def winner_rows_drawn(chosen_rows, levels, final_order):
    device_ids = jnp.arange(N_PROW, dtype=jnp.int32)
    candidates = (chosen_rows // B * N_PROW + device_ids[:, None]) * B + chosen_rows % B
    for level_id in range(LEVELS):
        partner = device_ids ^ 1 << level_id
        lower_side = jnp.minimum(device_ids, partner)
        upper_side = jnp.maximum(device_ids, partner)
        joined = jnp.concatenate([candidates[lower_side], candidates[upper_side]], axis=1)
        candidates = jnp.take_along_axis(joined, levels[level_id], axis=1)
    return candidates[0][final_order]


def tournament_draw(key):
    base_key = jax.random.fold_in(key, 11)
    rows_local = RTD * B
    taken = jnp.zeros((N_PROW, rows_local), jnp.int32)
    device_ids = jnp.arange(N_PROW, dtype=jnp.int32)
    local_list = []
    level_list = []
    order_list = []
    for panel_id in range(PANELS):
        panel_key = jax.random.fold_in(base_key, panel_id)
        subkeys = jax.random.split(jax.random.fold_in(panel_key, 1), N_PROW)
        ranking = jax.vmap(lambda subkey: jax.random.permutation(subkey, rows_local))(subkeys).astype(jnp.int32)
        scores = ranking + taken * (2 * rows_local)
        chosen_rows = jnp.argsort(scores, axis=1, stable=True)[:, :B].astype(jnp.int32)
        level_keys = jax.random.split(jax.random.fold_in(panel_key, 2), LEVELS * N_PROW)
        raw_picks = jax.vmap(lambda subkey: jax.random.permutation(subkey, 2 * B)[:B])(level_keys).astype(jnp.int32).reshape(LEVELS, N_PROW, B)
        levels = jnp.stack([raw_picks[level_id][device_ids >> level_id + 1] for level_id in range(LEVELS)]).astype(jnp.int32)
        final_order = jax.random.permutation(jax.random.fold_in(panel_key, 3), B).astype(jnp.int32)
        winners = winner_rows_drawn(chosen_rows, levels, final_order)
        owner_row = winners // B % N_PROW
        local_rows = winners // (N_PROW * B) * B + winners % B
        taken = taken.at[owner_row, local_rows].set(1)
        local_list.append(chosen_rows)
        level_list.append(levels)
        order_list.append(final_order)
    return (jnp.stack(local_list), jnp.stack(level_list), jnp.stack(order_list))


def draw_local_picks(key, part):
    return tournament_draw(key)[0]


def draw_level_picks(key, part):
    return tournament_draw(key)[1]


def draw_order(key, part):
    return tournament_draw(key)[2]


def draw_counts(key, part):
    used = jax.random.randint(jax.random.fold_in(key, 31), (DEVICES, DEVICES), 0, SLOT + 1)
    filled = jax.random.randint(jax.random.fold_in(key, 32), (), 0, DEVICES)
    return jnp.where(jnp.arange(DEVICES)[None, :] == filled, SLOT, used).astype(jnp.int32)


def draw_front(key, part):
    chosen, levels, final_order = tournament_draw(key)
    float_key = jax.random.fold_in(key, 21)
    draws_base = jax.random.truncated_normal(float_key, -6.0, 6.0, (NF, NF), jnp.float32)
    panel_of = jnp.full((NF,), PANELS, jnp.int32)
    position = jnp.zeros((NF,), jnp.int32)
    for panel_id in range(PANELS):
        winners = winner_rows_drawn(chosen[panel_id], levels[panel_id], final_order[panel_id])
        panel_of = panel_of.at[winners].set(panel_id)
        position = position.at[winners].set(jnp.arange(B, dtype=jnp.int32))
    columns = jnp.arange(NF, dtype=jnp.int32)
    col_panel = columns // B
    unscaled = col_panel[None, :] >= panel_of[:, None]
    factor = jnp.where((col_panel[None, :] < PANELS) & jnp.logical_not(unscaled), 4.0, 1.0)
    diag_hit = (col_panel[None, :] == panel_of[:, None]) & ((columns % B)[None, :] == position[:, None])
    magnitude = jax.random.uniform(jax.random.fold_in(key, 22), (NF,), jnp.float32, 7.5, 11.25) * jnp.sqrt(jnp.float32(B))
    diag_sign = jnp.where(jax.random.bernoulli(jax.random.fold_in(key, 23), 0.5, (NF,)), 1.0, -1.0)
    entries = draws_base * factor + jnp.where(diag_hit, (magnitude * diag_sign)[:, None], 0.0)
    return entries.astype(jnp.float32).reshape(RTD, N_PROW * B, CTD, N_PCOL * B)


def place_ends(drawn, rng, least, top_value):
    longest = drawn.shape.index(max(drawn.shape))
    spots = []
    for shift in (0, 1):
        where = [jax.random.randint(jax.random.fold_in(rng, axis), (), 0, length) for axis, length in enumerate(drawn.shape)]
        where[longest] = (where[longest] + shift) % drawn.shape[longest]
        spots.append(tuple(where))
    return drawn.at[spots[0]].set(least).at[spots[1]].set(top_value)


def steps_of(key, dims, pieces, least, top_value):
    def one(axis_at, blocks):
        heights = jax.random.uniform(jax.random.fold_in(jax.random.fold_in(key, 6), axis_at), (blocks,), jnp.float32, least / len(pieces), top_value / len(pieces))
        return jnp.repeat(jnp.exp(heights), dims[axis_at] // blocks).reshape((-1,) + (1,) * (len(dims) - axis_at - 1))

    factor_of = one(*pieces[0])
    for cut in pieces[1:]:
        factor_of = factor_of * one(*cut)
    return factor_of


def noise(rng, extent, width, bound, pieces=(), kind=jnp.bfloat16):
    gain = steps_of(rng, extent, pieces, -0.22, 0.18) if pieces else 1.0
    result = jax.random.normal(rng, extent, jnp.float32) * width * gain
    return jnp.minimum(jnp.maximum(result, -bound), bound).astype(kind)


def setup_inputs(seed: int = 0) -> dict:
    splits = jax.random.split(jax.random.key(seed), 8)
    front = draw_front(jax.random.fold_in(splits[7], 71), 0)
    partials = noise(splits[1], (DEVICES, DEVICES, SLOT, B), 1.0, 6.0, ((0, 128),), jnp.float32)
    targets = place_ends(jax.random.randint(splits[2], (DEVICES, DEVICES, SLOT), 0, RTD * B * CTD), jax.random.fold_in(splits[2], 1), 0, (RTD * B * CTD) - 1).astype(jnp.int32)
    counts = draw_counts(jax.random.fold_in(splits[7], 71), 0)
    local_picks = draw_local_picks(jax.random.fold_in(splits[7], 71), 0)
    level_picks = draw_level_picks(jax.random.fold_in(splits[7], 71), 0)
    order = draw_order(jax.random.fold_in(splits[7], 71), 0)
    return {"front": front, "partials": partials, "targets": targets, "counts": counts, "local_picks": local_picks, "level_picks": level_picks, "order": order}


def winner_rows(chosen_rows, levels, final_order):
    device_ids = jnp.arange(N_PROW, dtype=jnp.int32)
    candidates = ((chosen_rows // B) * N_PROW + device_ids[:, None]) * B + chosen_rows % B
    for level_id in range(LEVELS):
        partner = device_ids ^ (1 << level_id)
        lower_side = jnp.minimum(device_ids, partner)
        upper_side = jnp.maximum(device_ids, partner)
        joined = jnp.concatenate([candidates[lower_side], candidates[upper_side]], axis=1)
        candidates = jnp.take_along_axis(joined, levels[level_id], axis=1)
    return candidates[0][final_order]


def newton_inverse(diag_block):
    identity = jnp.eye(diag_block.shape[0], dtype=jnp.float32)
    approx = identity / jnp.diagonal(diag_block)[:, None]
    for refine in range(2):
        approx = jnp.dot(approx, 2.0 * identity - jnp.dot(diag_block, approx, precision=lax.Precision.HIGHEST), precision=lax.Precision.HIGHEST)
    return approx


def reference(front, partials, targets, counts, local_picks, level_picks, order):
    matrix = front.reshape(NF, NF)
    occupied = jnp.arange(SLOT, dtype=jnp.int32)[None, None, :] < counts[:, :, None]
    owner_ids = jnp.arange(DEVICES, dtype=jnp.int32)[None, :, None]
    prow_of = owner_ids // N_PCOL
    pcol_of = owner_ids % N_PCOL
    local_row = targets // CTD
    tile_col = targets % CTD
    global_row = ((local_row // B) * N_PROW + prow_of) * B + local_row % B
    global_cols = ((tile_col * N_PCOL + pcol_of) * B)[..., None] + jnp.arange(B, dtype=jnp.int32)
    partial_rows = jnp.where(occupied[..., None], partials, jnp.float32(0.0))
    matrix = matrix.at[global_row[..., None], global_cols].add(partial_rows)
    retired = jnp.zeros((NF,), dtype=bool)
    for panel_id in range(PANELS):
        winners = winner_rows(local_picks[panel_id], level_picks[panel_id], order[panel_id])
        retired = retired.at[winners].set(True)
        left = panel_id * B
        right = (panel_id + 1) * B
        inverse = newton_inverse(matrix[winners, left:right])
        multipliers = jnp.dot(matrix[:, left:right], inverse, precision=lax.Precision.HIGHEST)
        pivot_rows = matrix[winners, right:]
        updated = matrix[:, right:] - jnp.dot(multipliers, pivot_rows, precision=lax.Precision.HIGHEST)
        frozen = retired[:, None]
        matrix = matrix.at[:, left:right].set(jnp.where(frozen, matrix[:, left:right], multipliers))
        matrix = matrix.at[:, right:].set(jnp.where(frozen, matrix[:, right:], updated))
    return matrix.reshape(RTD, N_PROW * B, CTD, N_PCOL * B)
```

```python
import functools

import jax
import jax.numpy as jnp
from jax import lax
from jax.experimental import pallas as pl
from jax.experimental.pallas import tpu as pltpu
from jax.sharding import PartitionSpec as P

F32 = jnp.float32
BF16 = jnp.bfloat16
VM = pl.BlockSpec(memory_space=pltpu.VMEM)
SM = pl.BlockSpec(memory_space=pltpu.SMEM)
B = 256
PARAMS = dict(compiler_params=pltpu.CompilerParams(vmem_limit_bytes=56 * 1024 * 1024))


def iota(shape, dim):
    return lax.broadcasted_iota(jnp.int32, shape, dim)


def dot(a, b):
    return jnp.dot(a, b, preferred_element_type=F32)


def halves(x):
    high = x.astype(BF16)
    return high, (x - high.astype(F32)).astype(BF16)


def dot3(a, b):
    ah, al = a
    bh, bl = b
    return dot(ah, bh) + (dot(ah, bl) + dot(al, bh))


def pick(onehot, x):
    high, low = halves(x)
    return dot(onehot, high) + dot(onehot, low)


def lookup(table, d, pos):
    n = pos.shape[1]
    hot = (iota((B, n), 0) == pos).astype(F32).astype(BF16)
    high = table // 256
    low = table - high * 256
    both = jnp.concatenate([high, low], axis=0).astype(F32).astype(BF16)
    got = dot(both, hot).astype(jnp.int32)
    rows = table.shape[0]
    values = got[:rows] * 256 + got[rows:]
    return jnp.sum(jnp.where(iota((rows, n), 0) == d, values, 0), axis=0, keepdims=True)


def index_kernel(place, local_picks, level_picks, order, own_out, active_out):
    rows = active_out.shape[1]
    p = place[0]
    retired = jnp.zeros((rows, 1), F32)
    for k in range(order.shape[0]):
        pos = order[k : k + 1, :]
        d = jnp.zeros_like(pos)
        for level in range(level_picks.shape[1] - 1, -1, -1):
            j = lookup(level_picks[k, level], d, pos)
            bit = 1 << level
            d = (d & ~bit) | jnp.where(j >= B, bit, 0)
            pos = j & (B - 1)
        r = lookup(local_picks[k], d, pos)
        own = jnp.where(d == p, r, -1)
        own_out[k * B : (k + 1) * B, :] = jnp.broadcast_to(own, (128, B)).T
        hit = (iota((rows, B), 0) == own).astype(F32)
        retired = jnp.maximum(retired, jnp.max(hit, axis=1, keepdims=True))
        active_out[k] = jnp.broadcast_to(1.0 - retired, (rows, 128))


def assemble_kernel(payload, front, own, matrix_out, pivots_out):
    sources = payload.shape[0] // 17
    groups = sources // 16
    left, right, codes = [], [], []
    for g in range(groups):
        row = jnp.zeros((1, 128), F32)
        for s in range(16 * g, 16 * g + 16):
            left.append(payload[17 * s : 17 * s + 8, :])
            right.append(payload[17 * s + 8 : 17 * s + 16, :])
            row = row + payload[17 * s + 16 : 17 * s + 17, :]
        codes.append(row)
    values = jnp.concatenate([jnp.concatenate(left, axis=0), jnp.concatenate(right, axis=0)], axis=1)
    high, low = halves(values)
    code = jnp.concatenate(codes, axis=1).astype(jnp.int32)
    rows = front.shape[0]
    count = code.shape[1]
    pivot_hot = (own[:, 0:1] == iota((own.shape[0], rows), 1)).astype(F32).astype(BF16)
    for u in range(4):
        hot = (code == iota((rows, count), 0) * 4 + u).astype(F32).astype(BF16)
        tile = front[:, u * B : (u + 1) * B] + (dot(hot, high) + dot(hot, low))
        matrix_out[:, u * B : (u + 1) * B] = tile
        pivots_out[:, u * B : (u + 1) * B] = pick(pivot_hot, tile)


def inverse_of(diag):
    eye = iota((B, B), 0) == iota((B, B), 1)
    only = jnp.where(eye, diag, 0.0)
    by_row = 1.0 / jnp.sum(only, axis=1, keepdims=True)
    by_col = 1.0 / jnp.sum(only, axis=0, keepdims=True)
    two = jnp.where(eye, 2.0, 0.0)
    x = by_row * (two - diag * by_col)
    xs = halves(x)
    return dot3(xs, halves(two - dot3(halves(diag), xs)))


def panel_kernel(place, w_own, w_other, r_own, r_other, active, half_out, tile_out):
    even = place[1] % 2 == 0
    w0 = jnp.where(even, w_own[...], w_other[...])
    w1 = jnp.where(even, w_other[...], w_own[...])
    r0 = jnp.where(even, r_own[...], r_other[...])
    r1 = jnp.where(even, r_other[...], r_own[...])
    act0 = active[0][:, 0:1]
    act1 = active[1][:, 0:1]
    inv0 = halves(inverse_of(w0[:B]))
    m0w = dot3(halves(w0[B:]), inv0)
    m0w_s = halves(m0w)
    p01 = halves(w1[:B])
    inv1 = halves(inverse_of(w1[B:] - dot3(m0w_s, p01)))
    m0 = dot3(halves(r0), inv0)
    m0a = jnp.where(act0 > 0, m0, 0.0)
    r1 = r1 - dot3(halves(m0a), p01)
    m1 = dot3(halves(r1), inv1)
    n1 = jnp.where(act1 > 0, m1, 0.0)
    n0 = m0a - dot3(halves(n1), m0w_s)
    half_out[...] = jnp.where(even, n0, n1)
    tile_out[...] = jnp.where(even, jnp.where(act0 > 0, m0, r0), jnp.where(act1 > 0, m1, r1))


def update_kernel(place, matrix, pivots, n_own, n_other, tile, out):
    even = place[1] % 2 == 0
    n0 = halves(jnp.where(even, n_own[...], n_other[...]))
    n1 = halves(jnp.where(even, n_other[...], n_own[...]))
    for u in range(4):
        cols = slice(u * B, (u + 1) * B)
        new = matrix[:, cols] - (
            dot3(n0, halves(pivots[:B, cols])) + dot3(n1, halves(pivots[B:, cols]))
        )
        if u == 0:
            new = jnp.where(place[1] < 2, tile[...], new)
        out[:, cols] = new


def call(kernel, outs, n_in, scalars=1, flops=0, moved=0):
    return pl.pallas_call(
        kernel,
        out_shape=outs,
        in_specs=[SM] * scalars + [VM] * (n_in - scalars),
        out_specs=jax.tree.map(lambda _: VM, outs),
        cost_estimate=pl.CostEstimate(flops=flops, bytes_accessed=moved, transcendentals=0),
        **PARAMS,
    )


def shaped(*shape, dtype=F32):
    return jax.ShapeDtypeStruct(shape, dtype)


def core_swap(x):
    return lax.ppermute(x, "pcol", [(i, i ^ 1) for i in range(lax.axis_size("pcol"))])


def spread_z(x, z):
    one = lax.ppermute(x, "pcol", [(0, 2), (1, 3)])
    three = lax.ppermute(x, "pcol", [(0, 6), (1, 7)])
    two = lax.ppermute(x, "pcol", [(0, 4), (1, 5)])
    return jnp.where(z == 0, x, jnp.where(z == 1, one, jnp.where(z == 2, two, three)))


def body(front, partials, targets, counts, local_picks, level_picks, order):
    rows = front.shape[0] * front.shape[1]
    cols = front.shape[2] * front.shape[3]
    p = lax.axis_index("prow")
    q = lax.axis_index("pcol")
    me = p * lax.axis_size("pcol") + q
    place = jnp.stack([p, q]).astype(jnp.int32)
    sources = partials.shape[1]
    slots = partials.shape[2]

    used = iota((sources, slots), 1) < counts[0][:, None]
    codes = jnp.where(used, targets[0], -1)
    lanes = jnp.tile(codes, (1, 16))
    code_row = jnp.where(iota((sources, 128), 1) // slots == me % 16, lanes, 0).astype(F32)
    values = partials[0].reshape(sources, slots, 2, 128).transpose(0, 2, 1, 3).reshape(sources, 16, 128)
    payload = jnp.concatenate([values, code_row[:, None, :]], axis=1).reshape(sources * 17, 1, 128)
    payload = lax.all_to_all(payload, ("prow", "pcol"), 0, 0, tiled=True).reshape(sources * 17, 128)

    own, active = call(
        index_kernel, (shaped(2 * B, 128, dtype=jnp.int32), shaped(2, rows, 128)), 4, flops=10**9, moved=10**6
    )(place, local_picks, level_picks, order)

    matrix, pivots = call(
        assemble_kernel, (shaped(rows, cols), shaped(2 * B, cols)), 3, scalars=0, flops=4 * 10**9, moved=8 * 10**6
    )(payload, front.reshape(rows, cols), own)

    r_own = matrix[:, :B]
    r_other = core_swap(r_own)
    pivots = lax.psum(pivots, "prow")
    w_own = pivots[:, :B]
    w_other = core_swap(w_own)
    half, tile = call(
        panel_kernel, (shaped(rows, B), shaped(rows, B)), 6, flops=2 * 10**9, moved=4 * 10**6
    )(place, w_own, w_other, r_own, r_other, active)
    n_own = spread_z(half, q // 2)
    n_other = core_swap(n_own)
    out = call(
        update_kernel, shaped(rows, cols), 6, flops=2 * 10**9, moved=8 * 10**6
    )(place, matrix, pivots, n_own, n_other, tile)
    return out.reshape(front.shape)


def solution(mesh):
    placed = (
        P(None, "prow", None, "pcol"),
        P(("prow", "pcol"), None, None, None),
        P(("prow", "pcol"), None, None),
        P(("prow", "pcol"), None),
        P(),
        P(),
        P(),
    )
    return jax.shard_map(
        body, mesh=mesh, in_specs=placed, out_specs=P(None, "prow", None, "pcol"), check_vma=False
    )
```

```python
import functools

import jax
import jax.numpy as jnp
from jax import lax
from jax.experimental import pallas as pl
from jax.experimental.pallas import tpu as pltpu
from jax.sharding import PartitionSpec as P

F32 = jnp.float32
BF16 = jnp.bfloat16
VM = pl.BlockSpec(memory_space=pltpu.VMEM)
SM = pl.BlockSpec(memory_space=pltpu.SMEM)
B = 256
KEEP = 48
PARAMS = dict(compiler_params=pltpu.CompilerParams(vmem_limit_bytes=56 * 1024 * 1024))


def iota(shape, dim):
    return lax.broadcasted_iota(jnp.int32, shape, dim)


def dot(a, b):
    return jnp.dot(a, b, preferred_element_type=F32)


def halves(x):
    high = x.astype(BF16)
    return high, (x - high.astype(F32)).astype(BF16)


def dot3(a, b):
    ah, al = a
    bh, bl = b
    return dot(ah, bh) + (dot(ah, bl) + dot(al, bh))


def pick(onehot, x):
    high, low = halves(x)
    return dot(onehot, high) + dot(onehot, low)


def lookup(table, d, pos):
    n = pos.shape[1]
    hot = (iota((B, n), 0) == pos).astype(F32).astype(BF16)
    high = table // 256
    low = table - high * 256
    both = jnp.concatenate([high, low], axis=0).astype(F32).astype(BF16)
    got = dot(both, hot).astype(jnp.int32)
    rows = table.shape[0]
    values = got[:rows] * 256 + got[rows:]
    return jnp.sum(jnp.where(iota((rows, n), 0) == d, values, 0), axis=0, keepdims=True)


def index_kernel(place, local_picks, level_picks, order, own_out, active_out, give_out, slot_out, fits_out):
    rows = active_out.shape[1]
    keep = give_out.shape[0]
    p = place[0]
    retired = jnp.zeros((rows, 1), F32)
    owners, locals_ = [], []
    for k in range(order.shape[0]):
        pos = order[k : k + 1, :]
        d = jnp.zeros_like(pos)
        for level in range(level_picks.shape[1] - 1, -1, -1):
            j = lookup(level_picks[k, level], d, pos)
            bit = 1 << level
            d = (d & ~bit) | jnp.where(j >= B, bit, 0)
            pos = j & (B - 1)
        r = lookup(local_picks[k], d, pos)
        own = jnp.where(d == p, r, -1)
        own_out[k * B : (k + 1) * B, :] = jnp.broadcast_to(own, (128, B)).T
        hit = (iota((rows, B), 0) == own).astype(F32)
        retired = jnp.maximum(retired, jnp.max(hit, axis=1, keepdims=True))
        active_out[k] = jnp.broadcast_to(1.0 - retired, (rows, 128))
        owners.append(d)
        locals_.append(r)
    d = jnp.concatenate(owners, axis=1)
    r = jnp.concatenate(locals_, axis=1)
    n = d.shape[1]
    d_col = jnp.broadcast_to(d, (128, n)).T[:, 0:1]
    before = (d_col == d) & (iota((n, n), 0) < iota((n, n), 1))
    rank = jnp.sum(before.astype(jnp.int32), axis=0, keepdims=True)
    fits_out[0] = (jnp.max(rank) < keep).astype(jnp.int32)
    slot_out[...] = jnp.broadcast_to(d * keep + rank, (128, n)).T
    mine = (iota((keep, n), 0) == rank) & (d == p)
    give = jnp.sum(jnp.where(mine, r + 1, 0), axis=1, keepdims=True) - 1
    give_out[...] = jnp.broadcast_to(give, (keep, 128))


def unpack(payload):
    sources = payload.shape[0] // 17
    left, right, codes = [], [], []
    for g in range(sources // 16):
        row = jnp.zeros((1, 128), F32)
        for s in range(16 * g, 16 * g + 16):
            left.append(payload[17 * s : 17 * s + 8, :])
            right.append(payload[17 * s + 8 : 17 * s + 16, :])
            row = row + payload[17 * s + 16 : 17 * s + 17, :]
        codes.append(row)
    values = jnp.concatenate([jnp.concatenate(left, axis=0), jnp.concatenate(right, axis=0)], axis=1)
    return halves(values), jnp.concatenate(codes, axis=1).astype(jnp.int32)


def hot_of(code, rows, u):
    return (code == iota((rows, code.shape[1]), 0) * 4 + u).astype(F32).astype(BF16)


def rows_hot(chosen, rows):
    return (chosen[:, 0:1] == iota((chosen.shape[0], rows), 1)).astype(F32).astype(BF16)


def assemble_kernel(payload, front, own, matrix_out, pivots_out):
    (high, low), code = unpack(payload)
    rows = front.shape[0]
    pivot_hot = rows_hot(own, rows)
    for u in range(4):
        cols = slice(u * B, (u + 1) * B)
        hot = hot_of(code, rows, u)
        tile = front[:, cols] + (dot(hot, high) + dot(hot, low))
        matrix_out[:, cols] = tile
        pivots_out[:, cols] = pick(pivot_hot, tile)


def first_kernel(payload, front, give, tile_out, send_out, high_out, low_out, code_out):
    (high, low), code = unpack(payload)
    high_out[...] = high
    low_out[...] = low
    code_out[...] = jnp.broadcast_to(code, code_out.shape)
    rows = front.shape[0]
    hot = hot_of(code, rows, 0)
    tile = front[:, :B] + (dot(hot, high) + dot(hot, low))
    tile_out[...] = tile
    sent = pick(rows_hot(give, rows), tile)
    for i in range(send_out.shape[0] // sent.shape[0]):
        send_out[i * sent.shape[0] : (i + 1) * sent.shape[0], :] = sent


def rest_kernel(high, low, code, front, give, rest_out, send_out):
    rows = front.shape[0]
    give_hot = rows_hot(give, rows)
    keep = give.shape[0]
    for u in range(1, 4):
        hot = hot_of(code[0:1, :], rows, u)
        tile = front[:, u * B : (u + 1) * B] + (dot(hot, high[...]) + dot(hot, low[...]))
        cols = slice((u - 1) * B, u * B)
        rest_out[:, cols] = tile
        sent = pick(give_hot, tile)
        for i in range(send_out.shape[0] // keep):
            send_out[i * keep : (i + 1) * keep, cols] = sent


def inverse_of(diag):
    eye = iota((B, B), 0) == iota((B, B), 1)
    only = jnp.where(eye, diag, 0.0)
    by_row = 1.0 / jnp.sum(only, axis=1, keepdims=True)
    by_col = 1.0 / jnp.sum(only, axis=0, keepdims=True)
    two = jnp.where(eye, 2.0, 0.0)
    x = by_row * (two - diag * by_col)
    xs = halves(x)
    return dot3(xs, halves(two - dot3(halves(diag), xs)))


def panel_slots_kernel(place, slot, w_own, w_other, r_own, r_other, active, half_out, tile_out):
    hot = rows_hot(slot, w_own.shape[0])
    panel_kernel(place, pick(hot, w_own[...]), pick(hot, w_other[...]), r_own, r_other, active, half_out, tile_out)


def panel_kernel(place, w_own, w_other, r_own, r_other, active, half_out, tile_out):
    even = place[1] % 2 == 0
    w0 = jnp.where(even, w_own[...], w_other[...])
    w1 = jnp.where(even, w_other[...], w_own[...])
    r0 = jnp.where(even, r_own[...], r_other[...])
    r1 = jnp.where(even, r_other[...], r_own[...])
    act0 = active[0][:, 0:1]
    act1 = active[1][:, 0:1]
    inv0 = halves(inverse_of(w0[:B]))
    m0w = dot3(halves(w0[B:]), inv0)
    m0w_s = halves(m0w)
    p01 = halves(w1[:B])
    inv1 = halves(inverse_of(w1[B:] - dot3(m0w_s, p01)))
    m0 = dot3(halves(r0), inv0)
    m0a = jnp.where(act0 > 0, m0, 0.0)
    r1 = r1 - dot3(halves(m0a), p01)
    m1 = dot3(halves(r1), inv1)
    n1 = jnp.where(act1 > 0, m1, 0.0)
    n0 = m0a - dot3(halves(n1), m0w_s)
    half_out[...] = jnp.where(even, n0, n1)
    tile_out[...] = jnp.where(even, jnp.where(act0 > 0, m0, r0), jnp.where(act1 > 0, m1, r1))


def update_kernel(place, matrix, pivots, n_own, n_other, tile, out):
    even = place[1] % 2 == 0
    n0 = halves(jnp.where(even, n_own[...], n_other[...]))
    n1 = halves(jnp.where(even, n_other[...], n_own[...]))
    for u in range(4):
        cols = slice(u * B, (u + 1) * B)
        new = matrix[:, cols] - (
            dot3(n0, halves(pivots[:B, cols])) + dot3(n1, halves(pivots[B:, cols]))
        )
        if u == 0:
            new = jnp.where(place[1] < 2, tile[...], new)
        out[:, cols] = new


def spread_kernel(place, slot, n_own, n_other, high_out, low_out):
    even = place[1] % 2 == 0
    hot = rows_hot(slot, high_out.shape[1])
    h0, l0 = halves(jnp.where(even, n_own[...], n_other[...]))
    h1, l1 = halves(jnp.where(even, n_other[...], n_own[...]))
    high_out[...] = (dot(h0, hot[:B]) + dot(h1, hot[B:])).astype(BF16)
    low_out[...] = (dot(l0, hot[:B]) + dot(l1, hot[B:])).astype(BF16)


def finish_kernel(place, first, rest, w_first, w_rest, high, low, tile, out):
    n = (high[...], low[...])
    half = out.shape[1]
    for u in range(4):
        if u == 0:
            new = first[...] - dot3(n, halves(w_first[...]))
            new = jnp.where(place[1] < 2, tile[...], new)
        else:
            cols = slice((u - 1) * B, u * B)
            new = rest[:, cols] - dot3(n, halves(w_rest[:, cols]))
        for t in range(out.shape[0]):
            out[t, :, u, :] = new[t * half : (t + 1) * half]


def call(kernel, outs, n_in, scalars=1, outs_in_smem=0, flops=0, moved=0):
    specs = jax.tree.map(lambda _: VM, outs)
    if outs_in_smem:
        specs = specs[:-outs_in_smem] + (SM,) * outs_in_smem
    return pl.pallas_call(
        kernel,
        out_shape=outs,
        in_specs=[SM] * scalars + [VM] * (n_in - scalars),
        out_specs=specs,
        cost_estimate=pl.CostEstimate(flops=flops, bytes_accessed=moved, transcendentals=0),
        **PARAMS,
    )


def shaped(*shape, dtype=F32):
    return jax.ShapeDtypeStruct(shape, dtype)


def core_swap(x):
    return lax.ppermute(x, "pcol", [(i, i ^ 1) for i in range(lax.axis_size("pcol"))])


def spread_z(x, z):
    one = lax.ppermute(x, "pcol", [(0, 2), (1, 3)])
    three = lax.ppermute(x, "pcol", [(0, 6), (1, 7)])
    two = lax.ppermute(x, "pcol", [(0, 4), (1, 5)])
    return jnp.where(z == 0, x, jnp.where(z == 1, one, jnp.where(z == 2, two, three)))


def body(front, partials, targets, counts, local_picks, level_picks, order):
    rows = front.shape[0] * front.shape[1]
    cols = front.shape[2] * front.shape[3]
    p = lax.axis_index("prow")
    q = lax.axis_index("pcol")
    me = p * lax.axis_size("pcol") + q
    place = jnp.stack([p, q]).astype(jnp.int32)
    sources = partials.shape[1]
    slots = partials.shape[2]

    used = iota((sources, slots), 1) < counts[0][:, None]
    codes = jnp.where(used, targets[0], -1)
    lanes = jnp.tile(codes, (1, 16))
    code_row = jnp.where(iota((sources, 128), 1) // slots == me % 16, lanes, 0).astype(F32)
    values = partials[0].reshape(sources, slots, 2, 128).transpose(0, 2, 1, 3).reshape(sources, 16, 128)
    payload = jnp.concatenate([values, code_row[:, None, :]], axis=1).reshape(sources * 17, 1, 128)
    payload = lax.all_to_all(payload, ("prow", "pcol"), 0, 0, tiled=True).reshape(sources * 17, 128)

    own, active, give, slot, fits = call(
        index_kernel,
        (
            shaped(2 * B, 128, dtype=jnp.int32),
            shaped(2, rows, 128),
            shaped(KEEP, 128, dtype=jnp.int32),
            shaped(2 * B, 128, dtype=jnp.int32),
            shaped(1, dtype=jnp.int32),
        ),
        4,
        outs_in_smem=1,
        flops=10**9,
        moved=10**6,
    )(place, local_picks, level_picks, order)
    front, own = lax.optimization_barrier((front, own))
    flat = front.reshape(rows, cols)
    copies = lax.axis_size("prow") * KEEP

    def gather(payload, flat, own, active, give, slot, place):
        first, send, high, low, code = call(
            first_kernel,
            (
                shaped(rows, B),
                shaped(copies, B),
                shaped(sources * slots, B, dtype=BF16),
                shaped(sources * slots, B, dtype=BF16),
                shaped(8, sources * slots, dtype=jnp.int32),
            ),
            3,
            scalars=0,
            flops=10**9,
            moved=4 * 10**6,
        )(payload, flat, give)
        w_first = lax.all_to_all(send, "prow", 0, 0, tiled=True)
        r_other = core_swap(first)
        rest, send = call(
            rest_kernel, (shaped(rows, cols - B), shaped(copies, cols - B)), 5, scalars=0, flops=3 * 10**9, moved=8 * 10**6
        )(high, low, code, flat, give)
        w_rest = lax.all_to_all(send, "prow", 0, 0, tiled=True)
        w_other = core_swap(w_first)
        half, tile = call(
            panel_slots_kernel, (shaped(rows, B), shaped(rows, B)), 7, flops=2 * 10**9, moved=4 * 10**6
        )(place, slot, w_first, w_other, first, r_other, active)
        n_own = spread_z(half, place[1] // 2)
        n_other = core_swap(n_own)
        high, low = call(
            spread_kernel, (shaped(rows, copies, dtype=BF16), shaped(rows, copies, dtype=BF16)), 4, flops=10**9, moved=2 * 10**6
        )(place, slot, n_own, n_other)
        return call(finish_kernel, shaped(*front.shape), 8, flops=4 * 10**9, moved=8 * 10**6)(
            place, first, rest, w_first, w_rest, high, low, tile
        )

    def add_up(payload, flat, own, active, give, slot, place):
        matrix, pivots = call(
            assemble_kernel, (shaped(rows, cols), shaped(2 * B, cols)), 3, scalars=0, flops=4 * 10**9, moved=8 * 10**6
        )(payload, flat, own)
        r_own = matrix[:, :B]
        r_other = core_swap(r_own)
        pivots = lax.psum(pivots, "prow")
        w_own = pivots[:, :B]
        w_other = core_swap(w_own)
        half, tile = call(
            panel_kernel, (shaped(rows, B), shaped(rows, B)), 6, flops=2 * 10**9, moved=4 * 10**6
        )(place, w_own, w_other, r_own, r_other, active)
        n_own = spread_z(half, place[1] // 2)
        n_other = core_swap(n_own)
        out = call(update_kernel, shaped(rows, cols), 6, flops=2 * 10**9, moved=8 * 10**6)(
            place, matrix, pivots, n_own, n_other, tile
        )
        return out.reshape(front.shape)

    return lax.cond(fits[0] == 1, gather, add_up, payload, flat, own, active, give, slot, place)


def solution(mesh):
    placed = (
        P(None, "prow", None, "pcol"),
        P(("prow", "pcol"), None, None, None),
        P(("prow", "pcol"), None, None),
        P(("prow", "pcol"), None),
        P(),
        P(),
        P(),
    )
    return jax.shard_map(
        body, mesh=mesh, in_specs=placed, out_specs=P(None, "prow", None, "pcol"), check_vma=False
    )
```

```python
import functools

import jax
import jax.numpy as jnp
from jax import lax
from jax.experimental import pallas as pl
from jax.experimental.pallas import tpu as pltpu
from jax.sharding import PartitionSpec as P

F32 = jnp.float32
BF16 = jnp.bfloat16
VM = pl.BlockSpec(memory_space=pltpu.VMEM)
SM = pl.BlockSpec(memory_space=pltpu.SMEM)
B = 256
KEEP = 48
PARAMS = dict(compiler_params=pltpu.CompilerParams(vmem_limit_bytes=24 * 1024 * 1024))


def iota(shape, dim):
    return lax.broadcasted_iota(jnp.int32, shape, dim)


def dot(a, b):
    return jnp.dot(a, b, preferred_element_type=F32)


def halves(x):
    high = x.astype(BF16)
    return high, (x - high.astype(F32)).astype(BF16)


def dot3(a, b):
    ah, al = a
    bh, bl = b
    return dot(ah, bh) + (dot(ah, bl) + dot(al, bh))


def pick(onehot, x):
    high, low = halves(x)
    return dot(onehot, high) + dot(onehot, low)


def lookup(table, d, pos):
    n = pos.shape[1]
    hot = (iota((B, n), 0) == pos).astype(F32).astype(BF16)
    high = table // 256
    low = table - high * 256
    both = jnp.concatenate([high, low], axis=0).astype(F32).astype(BF16)
    got = dot(both, hot).astype(jnp.int32)
    rows = table.shape[0]
    values = got[:rows] * 256 + got[rows:]
    return jnp.sum(jnp.where(iota((rows, n), 0) == d, values, 0), axis=0, keepdims=True)


def index_kernel(place, local_picks, level_picks, order, own_out, active_out, give_out, slot_out, fits_out):
    rows = active_out.shape[1]
    keep = give_out.shape[0]
    p = place[0]
    retired = jnp.zeros((rows, 1), F32)
    owners, locals_ = [], []
    for k in range(order.shape[0]):
        pos = order[k : k + 1, :]
        d = jnp.zeros_like(pos)
        for level in range(level_picks.shape[1] - 1, -1, -1):
            j = lookup(level_picks[k, level], d, pos)
            bit = 1 << level
            d = (d & ~bit) | jnp.where(j >= B, bit, 0)
            pos = j & (B - 1)
        r = lookup(local_picks[k], d, pos)
        own = jnp.where(d == p, r, -1)
        own_out[k * B : (k + 1) * B, :] = jnp.broadcast_to(own, (128, B)).T
        hit = (iota((rows, B), 0) == own).astype(F32)
        retired = jnp.maximum(retired, jnp.max(hit, axis=1, keepdims=True))
        active_out[k] = jnp.broadcast_to(1.0 - retired, (rows, 128))
        owners.append(d)
        locals_.append(r)
    d = jnp.concatenate(owners, axis=1)
    r = jnp.concatenate(locals_, axis=1)
    n = d.shape[1]
    d_col = jnp.broadcast_to(d, (128, n)).T[:, 0:1]
    before = (d_col == d) & (iota((n, n), 0) < iota((n, n), 1))
    rank = jnp.sum(before.astype(jnp.int32), axis=0, keepdims=True)
    fits_out[0] = (jnp.max(rank) < keep).astype(jnp.int32)
    slot_out[...] = jnp.broadcast_to(d * keep + rank, (128, n)).T
    mine = (iota((keep, n), 0) == rank) & (d == p)
    give = jnp.sum(jnp.where(mine, r + 1, 0), axis=1, keepdims=True) - 1
    give_out[...] = jnp.broadcast_to(give, (keep, 128))


def pack_kernel(place, partials, targets, counts, out):
    sources, slots = targets.shape
    limit = jnp.broadcast_to(counts[...], (sources, sources)).T
    lane = iota((sources, 128), 1)
    row = jnp.full((sources, 128), -1, jnp.int32)
    for j in range(slots):
        row = jnp.where((lane % slots == j) & (limit > j), jnp.broadcast_to(targets[:, j : j + 1], (sources, 128)), row)
    row = jnp.where(lane // slots == place[2] % 16, row, 0).astype(F32)
    for s in range(sources):
        out[17 * s : 17 * s + 8, :] = partials[s, :, :128]
        out[17 * s + 8 : 17 * s + 16, :] = partials[s, :, 128:]
        out[17 * s + 16 : 17 * s + 17, :] = row[s : s + 1, :]


def unpack(payload):
    sources = payload.shape[0] // 17
    left, right, codes = [], [], []
    for g in range(sources // 16):
        row = jnp.zeros((1, 128), F32)
        for s in range(16 * g, 16 * g + 16):
            left.append(payload[17 * s : 17 * s + 8, :])
            right.append(payload[17 * s + 8 : 17 * s + 16, :])
            row = row + payload[17 * s + 16 : 17 * s + 17, :]
        codes.append(row)
    values = jnp.concatenate([jnp.concatenate(left, axis=0), jnp.concatenate(right, axis=0)], axis=1)
    return halves(values), jnp.concatenate(codes, axis=1).astype(jnp.int32)


def hot_of(code, rows, u):
    return (code == iota((rows, code.shape[1]), 0) * 4 + u).astype(F32).astype(BF16)


def rows_hot(chosen, rows):
    return (chosen[:, 0:1] == iota((chosen.shape[0], rows), 1)).astype(F32).astype(BF16)


def assemble_kernel(payload, front, own, matrix_out, pivots_out):
    (high, low), code = unpack(payload)
    rows = front.shape[0]
    pivot_hot = rows_hot(own, rows)
    for u in range(4):
        cols = slice(u * B, (u + 1) * B)
        hot = hot_of(code, rows, u)
        tile = front[:, cols] + (dot(hot, high) + dot(hot, low))
        matrix_out[:, cols] = tile
        pivots_out[:, cols] = pick(pivot_hot, tile)


def first_kernel(payload, front, give, tile_out, send_out, high_out, low_out, code_out):
    (high, low), code = unpack(payload)
    high_out[...] = high
    low_out[...] = low
    code_out[...] = jnp.broadcast_to(code, code_out.shape)
    rows = front.shape[0]
    hot = hot_of(code, rows, 0)
    tile = front[:, :B] + (dot(hot, high) + dot(hot, low))
    tile_out[...] = tile
    sent = pick(rows_hot(give, rows), tile)
    for i in range(send_out.shape[0] // sent.shape[0]):
        send_out[i * sent.shape[0] : (i + 1) * sent.shape[0], :] = sent


def rest_kernel(high, low, code, front, give, rest_out, send_out, done_out):
    rows = front.shape[0]
    give_hot = rows_hot(give, rows)
    for u in range(1, 4):
        hot = hot_of(code[0:1, :], rows, u)
        tile = front[:, u * B : (u + 1) * B] + (dot(hot, high[...]) + dot(hot, low[...]))
        cols = slice((u - 1) * B, u * B)
        rest_out[:, cols] = tile
        send_out[:, cols] = pick(give_hot, tile)
    done_out[...] = jnp.zeros_like(done_out)


def sort_kernel(slot, gathered, done, out):
    out[...] = pick(rows_hot(slot, gathered.shape[0]), gathered[...])


def inverse_of(diag):
    eye = iota((B, B), 0) == iota((B, B), 1)
    only = jnp.where(eye, diag, 0.0)
    by_row = 1.0 / jnp.sum(only, axis=1, keepdims=True)
    by_col = 1.0 / jnp.sum(only, axis=0, keepdims=True)
    two = jnp.where(eye, 2.0, 0.0)
    x = by_row * (two - diag * by_col)
    xs = halves(x)
    return dot3(xs, halves(two - dot3(halves(diag), xs)))


def panel_kernel(place, w_own, w_other, r_own, r_other, active, half_out, tile_out):
    even = place[1] % 2 == 0
    w0 = jnp.where(even, w_own[...], w_other[...])
    w1 = jnp.where(even, w_other[...], w_own[...])
    r0 = jnp.where(even, r_own[...], r_other[...])
    r1 = jnp.where(even, r_other[...], r_own[...])
    act0 = active[0][:, 0:1]
    act1 = active[1][:, 0:1]
    inv0 = halves(inverse_of(w0[:B]))
    m0w = dot3(halves(w0[B:]), inv0)
    m0w_s = halves(m0w)
    p01 = halves(w1[:B])
    inv1 = halves(inverse_of(w1[B:] - dot3(m0w_s, p01)))
    m0 = dot3(halves(r0), inv0)
    m0a = jnp.where(act0 > 0, m0, 0.0)
    r1 = r1 - dot3(halves(m0a), p01)
    m1 = dot3(halves(r1), inv1)
    n1 = jnp.where(act1 > 0, m1, 0.0)
    n0 = m0a - dot3(halves(n1), m0w_s)
    half_out[...] = jnp.where(even, n0, n1)
    tile_out[...] = jnp.where(even, jnp.where(act0 > 0, m0, r0), jnp.where(act1 > 0, m1, r1))


def update_kernel(place, matrix, pivots, n_own, n_other, tile, out):
    even = place[1] % 2 == 0
    n0 = halves(jnp.where(even, n_own[...], n_other[...]))
    n1 = halves(jnp.where(even, n_other[...], n_own[...]))
    for u in range(4):
        cols = slice(u * B, (u + 1) * B)
        new = matrix[:, cols] - (
            dot3(n0, halves(pivots[:B, cols])) + dot3(n1, halves(pivots[B:, cols]))
        )
        if u == 0:
            new = jnp.where(place[1] < 2, tile[...], new)
        out[:, cols] = new


def spread_kernel(place, slot, n_early, n_late, o_early, o_late, first, w_first, tile, high_out, low_out, first_out):
    q = place[1]
    even = q % 2 == 0
    n_own = jnp.where((q < 3) | (q == 7), n_early[...], n_late[...])
    n_other = jnp.where((q < 2) | (q == 3) | (q == 6), o_early[...], o_late[...])
    hot = rows_hot(slot, high_out.shape[1])
    h0, l0 = halves(jnp.where(even, n_own, n_other))
    h1, l1 = halves(jnp.where(even, n_other, n_own))
    high_out[...] = (dot(h0, hot[:B]) + dot(h1, hot[B:])).astype(BF16)
    low_out[...] = (dot(l0, hot[:B]) + dot(l1, hot[B:])).astype(BF16)
    new = first[...] - (dot3((h0, l0), halves(w_first[:B])) + dot3((h1, l1), halves(w_first[B:])))
    first_out[...] = jnp.where(q < 2, tile[...], new)


def finish_kernel(first, rest, w_rest, high, low, out):
    n = (high[...], low[...])
    half = out.shape[1]
    for u in range(4):
        if u == 0:
            new = first[...]
        else:
            cols = slice((u - 1) * B, u * B)
            new = rest[:, cols] - dot3(n, halves(w_rest[:, cols]))
        for t in range(out.shape[0]):
            out[t, :, u, :] = new[t * half : (t + 1) * half]


def call(kernel, outs, n_in, scalars=1, outs_in_smem=0, flops=0, moved=0):
    specs = jax.tree.map(lambda _: VM, outs)
    if outs_in_smem:
        specs = specs[:-outs_in_smem] + (SM,) * outs_in_smem
    return pl.pallas_call(
        kernel,
        out_shape=outs,
        in_specs=[SM] * scalars + [VM] * (n_in - scalars),
        out_specs=specs,
        cost_estimate=pl.CostEstimate(flops=flops, bytes_accessed=moved, transcendentals=0),
        **PARAMS,
    )


def shaped(*shape, dtype=F32):
    return jax.ShapeDtypeStruct(shape, dtype)


def core_swap(x):
    return lax.ppermute(x, "pcol", [(i, i ^ 1) for i in range(lax.axis_size("pcol"))])


def spread_z(x, z):
    one = lax.ppermute(x, "pcol", [(0, 2), (1, 3)])
    three = lax.ppermute(x, "pcol", [(0, 6), (1, 7)])
    two = lax.ppermute(x, "pcol", [(0, 4), (1, 5)])
    return jnp.where(z == 0, x, jnp.where(z == 1, one, jnp.where(z == 2, two, three)))


def body(front, partials, targets, counts, local_picks, level_picks, order):
    rows = front.shape[0] * front.shape[1]
    cols = front.shape[2] * front.shape[3]
    p = lax.axis_index("prow")
    q = lax.axis_index("pcol")
    me = p * lax.axis_size("pcol") + q
    place = jnp.stack([p, q, me]).astype(jnp.int32)
    sources = partials.shape[1]
    slots = partials.shape[2]

    payload = call(pack_kernel, shaped(sources * 17, 128), 4, flops=10**6, moved=2 * 10**6)(
        place, partials[0], targets[0], counts
    ).reshape(sources * 17, 1, 128)
    payload = lax.all_to_all(payload, ("prow", "pcol"), 0, 0, tiled=True).reshape(sources * 17, 128)

    own, active, give, slot, fits = call(
        index_kernel,
        (
            shaped(2 * B, 128, dtype=jnp.int32),
            shaped(2, rows, 128),
            shaped(KEEP, 128, dtype=jnp.int32),
            shaped(2 * B, 128, dtype=jnp.int32),
            shaped(1, dtype=jnp.int32),
        ),
        4,
        outs_in_smem=1,
        flops=10**9,
        moved=10**6,
    )(place, local_picks, level_picks, order)
    front, own = lax.optimization_barrier((front, own))
    flat = front.reshape(rows, cols)
    copies = lax.axis_size("prow") * KEEP

    def gather(payload, flat, own, active, give, slot, place):
        first, send, high, low, code = call(
            first_kernel,
            (
                shaped(rows, B),
                shaped(copies, B),
                shaped(sources * slots, B, dtype=BF16),
                shaped(sources * slots, B, dtype=BF16),
                shaped(8, sources * slots, dtype=jnp.int32),
            ),
            3,
            scalars=0,
            flops=10**9,
            moved=4 * 10**6,
        )(payload, flat, give)
        w_first = lax.all_to_all(send, "prow", 0, 0, tiled=True)
        r_other = core_swap(first)
        rest, send, done = call(
            rest_kernel,
            (shaped(rows, cols - B), shaped(KEEP, cols - B), shaped(8, 128)),
            5,
            scalars=0,
            flops=3 * 10**9,
            moved=6 * 10**6,
        )(high, low, code, flat, give)
        w_rest = lax.all_gather(send, "prow", axis=0, tiled=True)
        w_first = call(sort_kernel, shaped(2 * B, B), 3, scalars=0, flops=10**9, moved=10**6)(slot, w_first, done)
        w_other = core_swap(w_first)
        half, tile = call(
            panel_kernel, (shaped(rows, B), shaped(rows, B)), 6, flops=2 * 10**9, moved=4 * 10**6
        )(place, w_first, w_other, first, r_other, active)
        q = place[1]
        step = lax.ppermute(half, "pcol", [(0, 2), (1, 7)])
        n_early = jnp.where((q == 2) | (q == 7), step, half)
        n_late = lax.ppermute(n_early, "pcol", [(1, 3), (0, 6), (2, 4), (7, 5)])
        o_early = lax.ppermute(n_early, "pcol", [(0, 1), (1, 0), (2, 3), (7, 6)])
        o_late = lax.ppermute(n_late, "pcol", [(3, 2), (6, 7), (4, 5), (5, 4)])
        high, low, first = call(
            spread_kernel,
            (shaped(rows, copies, dtype=BF16), shaped(rows, copies, dtype=BF16), shaped(rows, B)),
            9,
            flops=10**9,
            moved=4 * 10**6,
        )(place, slot, n_early, n_late, o_early, o_late, first, w_first, tile)
        return call(finish_kernel, shaped(*front.shape), 5, scalars=0, flops=4 * 10**9, moved=8 * 10**6)(
            first, rest, w_rest, high, low
        )

    def add_up(payload, flat, own, active, give, slot, place):
        matrix, pivots = call(
            assemble_kernel, (shaped(rows, cols), shaped(2 * B, cols)), 3, scalars=0, flops=4 * 10**9, moved=8 * 10**6
        )(payload, flat, own)
        r_own = matrix[:, :B]
        r_other = core_swap(r_own)
        pivots = lax.psum(pivots, "prow")
        w_own = pivots[:, :B]
        w_other = core_swap(w_own)
        half, tile = call(
            panel_kernel, (shaped(rows, B), shaped(rows, B)), 6, flops=2 * 10**9, moved=4 * 10**6
        )(place, w_own, w_other, r_own, r_other, active)
        n_own = spread_z(half, place[1] // 2)
        n_other = core_swap(n_own)
        out = call(update_kernel, shaped(rows, cols), 6, flops=2 * 10**9, moved=8 * 10**6)(
            place, matrix, pivots, n_own, n_other, tile
        )
        return out.reshape(front.shape)

    return lax.cond(fits[0] == 1, gather, add_up, payload, flat, own, active, give, slot, place)


def solution(mesh):
    placed = (
        P(None, "prow", None, "pcol"),
        P(("prow", "pcol"), None, None, None),
        P(("prow", "pcol"), None, None),
        P(("prow", "pcol"), None),
        P(),
        P(),
        P(),
    )
    return jax.shard_map(
        body, mesh=mesh, in_specs=placed, out_specs=P(None, "prow", None, "pcol"), check_vma=False
    )
```

```python
import functools

import jax
import jax.numpy as jnp
from jax import lax
from jax.experimental import pallas as pl
from jax.experimental.pallas import tpu as pltpu
from jax.sharding import PartitionSpec as P

F32 = jnp.float32
BF16 = jnp.bfloat16
VM = pl.BlockSpec(memory_space=pltpu.VMEM)
SM = pl.BlockSpec(memory_space=pltpu.SMEM)
B = 256
KEEP = 48
PARAMS = dict(compiler_params=pltpu.CompilerParams(vmem_limit_bytes=14 * 1024 * 1024))


def iota(shape, dim):
    return lax.broadcasted_iota(jnp.int32, shape, dim)


def dot(a, b):
    return jnp.dot(a, b, preferred_element_type=F32)


def halves(x):
    high = x.astype(BF16)
    return high, (x - high.astype(F32)).astype(BF16)


def dot3(a, b):
    ah, al = a
    bh, bl = b
    return dot(ah, bh) + (dot(ah, bl) + dot(al, bh))


def pick(onehot, x):
    high, low = halves(x)
    return dot(onehot, high) + dot(onehot, low)


def lookup(table, d, pos):
    n = pos.shape[1]
    hot = (iota((B, n), 0) == pos).astype(F32).astype(BF16)
    high = table // 256
    low = table - high * 256
    both = jnp.concatenate([high, low], axis=0).astype(F32).astype(BF16)
    got = dot(both, hot).astype(jnp.int32)
    rows = table.shape[0]
    values = got[:rows] * 256 + got[rows:]
    return jnp.sum(jnp.where(iota((rows, n), 0) == d, values, 0), axis=0, keepdims=True)


def index_kernel(place, local_picks, level_picks, order, own_out, active_out, give_out, slot_out, fits_out):
    rows = active_out.shape[1]
    keep = give_out.shape[0]
    p = place[0]
    retired = jnp.zeros((rows, 1), F32)
    owners, locals_ = [], []
    for k in range(order.shape[0]):
        pos = order[k : k + 1, :]
        d = jnp.zeros_like(pos)
        for level in range(level_picks.shape[1] - 1, -1, -1):
            j = lookup(level_picks[k, level], d, pos)
            bit = 1 << level
            d = (d & ~bit) | jnp.where(j >= B, bit, 0)
            pos = j & (B - 1)
        r = lookup(local_picks[k], d, pos)
        own = jnp.where(d == p, r, -1)
        own_out[k * B : (k + 1) * B, :] = jnp.broadcast_to(own, (128, B)).T
        hit = (iota((rows, B), 0) == own).astype(F32)
        retired = jnp.maximum(retired, jnp.max(hit, axis=1, keepdims=True))
        active_out[k] = jnp.broadcast_to(1.0 - retired, (rows, 128))
        owners.append(d)
        locals_.append(r)
    d = jnp.concatenate(owners, axis=1)
    r = jnp.concatenate(locals_, axis=1)
    n = d.shape[1]
    d_col = jnp.broadcast_to(d, (128, n)).T[:, 0:1]
    before = (d_col == d) & (iota((n, n), 0) < iota((n, n), 1))
    rank = jnp.sum(before.astype(jnp.int32), axis=0, keepdims=True)
    fits_out[0] = (jnp.max(rank) < keep).astype(jnp.int32)
    slot_out[...] = jnp.broadcast_to(d * keep + rank, (128, n)).T
    mine = (iota((keep, n), 0) == rank) & (d == p)
    give = jnp.sum(jnp.where(mine, r + 2, 0), axis=1, keepdims=True) - 2
    give_out[...] = jnp.broadcast_to(give, (keep, 128))


def pack_kernel(place, partials, targets, counts, out):
    slots, sources = targets.shape
    codes = jnp.where(iota((slots, sources), 0) < counts[...], targets[...], -1)
    codes = jnp.concatenate([codes] * (128 // slots), axis=0)
    codes = jnp.where(iota(codes.shape, 0) // slots == place[2] % (128 // slots), codes, 0)
    row = codes.astype(F32).T
    for s in range(sources):
        out[17 * s : 17 * s + 8, :] = partials[s, :, :128]
        out[17 * s + 8 : 17 * s + 16, :] = partials[s, :, 128:]
        out[17 * s + 16 : 17 * s + 17, :] = row[s : s + 1, :]


def unpack(payload):
    sources = payload.shape[0] // 17
    left, right, codes = [], [], []
    for g in range(sources // 16):
        row = jnp.zeros((1, 128), F32)
        for s in range(16 * g, 16 * g + 16):
            left.append(payload[17 * s : 17 * s + 8, :])
            right.append(payload[17 * s + 8 : 17 * s + 16, :])
            row = row + payload[17 * s + 16 : 17 * s + 17, :]
        codes.append(row)
    values = jnp.concatenate([jnp.concatenate(left, axis=0), jnp.concatenate(right, axis=0)], axis=1)
    return halves(values), jnp.concatenate(codes, axis=1).astype(jnp.int32)


def hot_of(code, rows, u):
    return (code == iota((rows, code.shape[1]), 0) * 4 + u).astype(F32).astype(BF16)


def rows_hot(chosen, rows):
    return (chosen[:, 0:1] == iota((chosen.shape[0], rows), 1)).astype(F32).astype(BF16)


def assemble_kernel(payload, front, own, matrix_out, pivots_out):
    (high, low), code = unpack(payload)
    rows = front.shape[0]
    pivot_hot = rows_hot(own, rows)
    for u in range(4):
        cols = slice(u * B, (u + 1) * B)
        hot = hot_of(code, rows, u)
        tile = front[:, cols] + (dot(hot, high) + dot(hot, low))
        matrix_out[:, cols] = tile
        pivots_out[:, cols] = pick(pivot_hot, tile)


def front_kernel(front, give, out):
    keep = give.shape[0]
    hot = rows_hot(give, front.shape[0])
    for u in range(4):
        out[u * keep : (u + 1) * keep, :] = pick(hot, front[:, u * B : (u + 1) * B])


def lead_kernel(payload, front_rows, give, send_first, send_rest):
    (high, low), code = unpack(payload)
    keep = give.shape[0]
    chosen = give[:, 0:1] * 4
    hot = jnp.concatenate([(chosen + u == code).astype(F32) for u in range(4)], axis=0).astype(BF16)
    sums = front_rows[...] + (dot(hot, high) + dot(hot, low))
    for i in range(send_first.shape[0] // keep):
        send_first[i * keep : (i + 1) * keep, :] = sums[:keep]
    for u in range(1, 4):
        send_rest[:, (u - 1) * B : u * B] = sums[u * keep : (u + 1) * keep]


def tiles_kernel(payload, front, first_out, rest_out):
    (high, low), code = unpack(payload)
    for u in range(4):
        hot = hot_of(code, front.shape[0], u)
        tile = front[:, u * B : (u + 1) * B] + (dot(hot, high) + dot(hot, low))
        if u == 0:
            first_out[...] = tile
        else:
            rest_out[:, (u - 1) * B : u * B] = tile


def sort_kernel(slot, gathered, out):
    out[...] = pick(rows_hot(slot, gathered.shape[0]), gathered[...])


def inverse_of(diag):
    eye = iota((B, B), 0) == iota((B, B), 1)
    only = jnp.where(eye, diag, 0.0)
    by_row = 1.0 / jnp.sum(only, axis=1, keepdims=True)
    by_col = 1.0 / jnp.sum(only, axis=0, keepdims=True)
    two = jnp.where(eye, 2.0, 0.0)
    x = by_row * (two - diag * by_col)
    xs = halves(x)
    return dot3(xs, halves(two - dot3(halves(diag), xs)))


def panel_kernel(place, w_own, w_other, r_own, r_other, active, half_out, tile_out):
    even = place[1] % 2 == 0
    w0 = jnp.where(even, w_own[...], w_other[...])
    w1 = jnp.where(even, w_other[...], w_own[...])
    r0 = jnp.where(even, r_own[...], r_other[...])
    r1 = jnp.where(even, r_other[...], r_own[...])
    act0 = active[0][:, 0:1]
    act1 = active[1][:, 0:1]
    inv0 = halves(inverse_of(w0[:B]))
    m0w = dot3(halves(w0[B:]), inv0)
    m0w_s = halves(m0w)
    p01 = halves(w1[:B])
    inv1 = halves(inverse_of(w1[B:] - dot3(m0w_s, p01)))
    m0 = dot3(halves(r0), inv0)
    m0a = jnp.where(act0 > 0, m0, 0.0)
    r1 = r1 - dot3(halves(m0a), p01)
    m1 = dot3(halves(r1), inv1)
    n1 = jnp.where(act1 > 0, m1, 0.0)
    n0 = m0a - dot3(halves(n1), m0w_s)
    half_out[...] = jnp.where(even, n0, n1)
    tile_out[...] = jnp.where(even, jnp.where(act0 > 0, m0, r0), jnp.where(act1 > 0, m1, r1))


def update_kernel(place, matrix, pivots, n_own, n_other, tile, out):
    even = place[1] % 2 == 0
    n0 = halves(jnp.where(even, n_own[...], n_other[...]))
    n1 = halves(jnp.where(even, n_other[...], n_own[...]))
    for u in range(4):
        cols = slice(u * B, (u + 1) * B)
        new = matrix[:, cols] - (
            dot3(n0, halves(pivots[:B, cols])) + dot3(n1, halves(pivots[B:, cols]))
        )
        if u == 0:
            new = jnp.where(place[1] < 2, tile[...], new)
        out[:, cols] = new


def spread_kernel(place, slot, n_early, n_late, o_early, o_late, first, w_first, tile, high_out, low_out, first_out):
    q = place[1]
    even = q % 2 == 0
    n_own = jnp.where((q < 3) | (q == 7), n_early[...], n_late[...])
    n_other = jnp.where((q < 2) | (q == 3) | (q == 6), o_early[...], o_late[...])
    hot = rows_hot(slot, high_out.shape[1])
    h0, l0 = halves(jnp.where(even, n_own, n_other))
    h1, l1 = halves(jnp.where(even, n_other, n_own))
    high_out[...] = (dot(h0, hot[:B]) + dot(h1, hot[B:])).astype(BF16)
    low_out[...] = (dot(l0, hot[:B]) + dot(l1, hot[B:])).astype(BF16)
    new = first[...] - (dot3((h0, l0), halves(w_first[:B])) + dot3((h1, l1), halves(w_first[B:])))
    first_out[...] = jnp.where(q < 2, tile[...], new)


def finish_kernel(first, rest, w_rest, high, low, out):
    n = (high[...], low[...])
    half = out.shape[1]
    for u in range(4):
        if u == 0:
            new = first[...]
        else:
            cols = slice((u - 1) * B, u * B)
            new = rest[:, cols] - dot3(n, halves(w_rest[:, cols]))
        for t in range(out.shape[0]):
            out[t, :, u, :] = new[t * half : (t + 1) * half]


def call(kernel, outs, n_in, scalars=1, outs_in_smem=0, flops=0, moved=0):
    specs = jax.tree.map(lambda _: VM, outs)
    if outs_in_smem:
        specs = specs[:-outs_in_smem] + (SM,) * outs_in_smem
    return pl.pallas_call(
        kernel,
        out_shape=outs,
        in_specs=[SM] * scalars + [VM] * (n_in - scalars),
        out_specs=specs,
        cost_estimate=pl.CostEstimate(flops=flops, bytes_accessed=moved, transcendentals=0),
        **PARAMS,
    )


def shaped(*shape, dtype=F32):
    return jax.ShapeDtypeStruct(shape, dtype)


def core_swap(x):
    return lax.ppermute(x, "pcol", [(i, i ^ 1) for i in range(lax.axis_size("pcol"))])


def spread_z(x, z):
    one = lax.ppermute(x, "pcol", [(0, 2), (1, 3)])
    three = lax.ppermute(x, "pcol", [(0, 6), (1, 7)])
    two = lax.ppermute(x, "pcol", [(0, 4), (1, 5)])
    return jnp.where(z == 0, x, jnp.where(z == 1, one, jnp.where(z == 2, two, three)))


def body(front, partials, targets, counts, local_picks, level_picks, order):
    rows = front.shape[0] * front.shape[1]
    cols = front.shape[2] * front.shape[3]
    p = lax.axis_index("prow")
    q = lax.axis_index("pcol")
    me = p * lax.axis_size("pcol") + q
    place = jnp.stack([p, q, me]).astype(jnp.int32)
    sources = partials.shape[1]
    slots = partials.shape[2]

    payload = call(pack_kernel, shaped(sources * 17, 128), 4, flops=10**6, moved=2 * 10**6)(
        place, partials[0], targets[0].T, counts
    ).reshape(sources * 17, 1, 128)
    payload = lax.all_to_all(payload, ("prow", "pcol"), 0, 0, tiled=True).reshape(sources * 17, 128)

    own, active, give, slot, fits = call(
        index_kernel,
        (
            shaped(2 * B, 128, dtype=jnp.int32),
            shaped(2, rows, 128),
            shaped(KEEP, 128, dtype=jnp.int32),
            shaped(2 * B, 128, dtype=jnp.int32),
            shaped(1, dtype=jnp.int32),
        ),
        4,
        outs_in_smem=1,
        flops=10**9,
        moved=10**6,
    )(place, local_picks, level_picks, order)
    front, own = lax.optimization_barrier((front, own))
    flat = front.reshape(rows, cols)
    copies = lax.axis_size("prow") * KEEP

    front_rows = call(front_kernel, shaped(4 * KEEP, B), 2, scalars=0, flops=10**8, moved=3 * 10**6)(flat, give)

    def gather(payload, flat, own, active, give, slot, place, front_rows):
        send_first, send_rest = call(
            lead_kernel, (shaped(copies, B), shaped(KEEP, cols - B)), 3, scalars=0, flops=10**8, moved=2 * 10**6
        )(payload, front_rows, give)
        w_first = lax.all_to_all(send_first, "prow", 0, 0, tiled=True)
        w_rest = lax.all_gather(send_rest, "prow", axis=0, tiled=True)
        first, rest = call(
            tiles_kernel, (shaped(rows, B), shaped(rows, cols - B)), 2, scalars=0, flops=4 * 10**9, moved=6 * 10**6
        )(payload, flat)
        r_other = core_swap(first)
        w_first = call(sort_kernel, shaped(2 * B, B), 2, scalars=0, flops=10**8, moved=10**6)(slot, w_first)
        w_other = core_swap(w_first)
        half, tile = call(
            panel_kernel, (shaped(rows, B), shaped(rows, B)), 6, flops=2 * 10**9, moved=4 * 10**6
        )(place, w_first, w_other, first, r_other, active)
        q = place[1]
        step = lax.ppermute(half, "pcol", [(0, 2), (1, 7)])
        n_early = jnp.where((q == 2) | (q == 7), step, half)
        n_late = lax.ppermute(n_early, "pcol", [(1, 3), (0, 6), (2, 4), (7, 5)])
        o_early = lax.ppermute(n_early, "pcol", [(0, 1), (1, 0), (2, 3), (7, 6)])
        o_late = lax.ppermute(n_late, "pcol", [(3, 2), (6, 7), (4, 5), (5, 4)])
        high, low, first = call(
            spread_kernel,
            (shaped(rows, copies, dtype=BF16), shaped(rows, copies, dtype=BF16), shaped(rows, B)),
            9,
            flops=10**9,
            moved=4 * 10**6,
        )(place, slot, n_early, n_late, o_early, o_late, first, w_first, tile)
        return call(finish_kernel, shaped(*front.shape), 5, scalars=0, flops=4 * 10**9, moved=8 * 10**6)(
            first, rest, w_rest, high, low
        )

    def add_up(payload, flat, own, active, give, slot, place, front_rows):
        matrix, pivots = call(
            assemble_kernel, (shaped(rows, cols), shaped(2 * B, cols)), 3, scalars=0, flops=4 * 10**9, moved=8 * 10**6
        )(payload, flat, own)
        r_own = matrix[:, :B]
        r_other = core_swap(r_own)
        pivots = lax.psum(pivots, "prow")
        w_own = pivots[:, :B]
        w_other = core_swap(w_own)
        half, tile = call(
            panel_kernel, (shaped(rows, B), shaped(rows, B)), 6, flops=2 * 10**9, moved=4 * 10**6
        )(place, w_own, w_other, r_own, r_other, active)
        n_own = spread_z(half, place[1] // 2)
        n_other = core_swap(n_own)
        out = call(update_kernel, shaped(rows, cols), 6, flops=2 * 10**9, moved=8 * 10**6)(
            place, matrix, pivots, n_own, n_other, tile
        )
        return out.reshape(front.shape)

    return lax.cond(fits[0] == 1, gather, add_up, payload, flat, own, active, give, slot, place, front_rows)


def solution(mesh):
    placed = (
        P(None, "prow", None, "pcol"),
        P(("prow", "pcol"), None, None, None),
        P(("prow", "pcol"), None, None),
        P(("prow", "pcol"), None),
        P(),
        P(),
        P(),
    )
    return jax.shard_map(
        body, mesh=mesh, in_specs=placed, out_specs=P(None, "prow", None, "pcol"), check_vma=False
    )
```

```python
import functools

import jax
import jax.numpy as jnp
from jax import lax
from jax.experimental import pallas as pl
from jax.experimental.pallas import tpu as pltpu
from jax.sharding import PartitionSpec as P

F32 = jnp.float32
BF16 = jnp.bfloat16
VM = pl.BlockSpec(memory_space=pltpu.VMEM)
HBM = pl.BlockSpec(memory_space=pltpu.HBM)
SM = pl.BlockSpec(memory_space=pltpu.SMEM)
B = 256
KEEP = 48
PARAMS = dict(compiler_params=pltpu.CompilerParams(vmem_limit_bytes=14 * 1024 * 1024))

ALONE = dict(compiler_params=pltpu.CompilerParams(vmem_limit_bytes=63 * 1024 * 1024))


def iota(shape, dim):
    return lax.broadcasted_iota(jnp.int32, shape, dim)


def dot(a, b):
    return jnp.dot(a, b, preferred_element_type=F32)


def halves(x):
    high = x.astype(BF16)
    return high, (x - high.astype(F32)).astype(BF16)


def dot3(a, b):
    ah, al = a
    bh, bl = b
    return dot(ah, bh) + (dot(ah, bl) + dot(al, bh))


def pick(onehot, x):
    high, low = halves(x)
    return dot(onehot, high) + dot(onehot, low)


def lookup(table, d, pos):
    n = pos.shape[1]
    hot = (iota((B, n), 0) == pos).astype(F32).astype(BF16)
    high = table // 256
    low = table - high * 256
    both = jnp.concatenate([high, low], axis=0).astype(F32).astype(BF16)
    got = dot(both, hot).astype(jnp.int32)
    rows = table.shape[0]
    values = got[:rows] * 256 + got[rows:]
    return jnp.sum(jnp.where(iota((rows, n), 0) == d, values, 0), axis=0, keepdims=True)


def index_kernel(place, local_picks, level_picks, order, own_out, active_out, give_out, slot_out, fits_out):
    rows = active_out.shape[1]
    keep = give_out.shape[0]
    p = place[0]
    retired = jnp.zeros((rows, 1), F32)
    owners, locals_ = [], []
    for k in range(order.shape[0]):
        pos = order[k : k + 1, :]
        d = jnp.zeros_like(pos)
        for level in range(level_picks.shape[1] - 1, -1, -1):
            j = lookup(level_picks[k, level], d, pos)
            bit = 1 << level
            d = (d & ~bit) | jnp.where(j >= B, bit, 0)
            pos = j & (B - 1)
        r = lookup(local_picks[k], d, pos)
        own = jnp.where(d == p, r, -1)
        own_out[k * B : (k + 1) * B, :] = jnp.broadcast_to(own, (128, B)).T
        hit = (iota((rows, B), 0) == own).astype(F32)
        retired = jnp.maximum(retired, jnp.max(hit, axis=1, keepdims=True))
        active_out[k] = jnp.broadcast_to(1.0 - retired, (rows, 128))
        owners.append(d)
        locals_.append(r)
    d = jnp.concatenate(owners, axis=1)
    r = jnp.concatenate(locals_, axis=1)
    n = d.shape[1]
    d_col = jnp.broadcast_to(d, (128, n)).T[:, 0:1]
    before = (d_col == d) & (iota((n, n), 0) < iota((n, n), 1))
    rank = jnp.sum(before.astype(jnp.int32), axis=0, keepdims=True)
    fits_out[0] = (jnp.max(rank) < keep).astype(jnp.int32)
    slot_out[...] = jnp.broadcast_to(d * keep + rank, (128, n)).T
    mine = (iota((keep, n), 0) == rank) & (d == p)
    give = jnp.sum(jnp.where(mine, r + 2, 0), axis=1, keepdims=True) - 2
    give_out[...] = jnp.broadcast_to(give, (keep, 128))


def pack_kernel(place, partials_hbm, targets_hbm, counts_hbm, out, partials, targets, counts, sems):
    slots, sources = targets.shape
    parts = sems.shape[0] - 2
    step = sources // parts
    small = [
        pltpu.make_async_copy(targets_hbm, targets, sems.at[parts]),
        pltpu.make_async_copy(counts_hbm, counts, sems.at[parts + 1]),
    ]
    large = [
        pltpu.make_async_copy(
            partials_hbm.at[i * step : (i + 1) * step], partials.at[i * step : (i + 1) * step], sems.at[i]
        )
        for i in range(parts)
    ]
    for copy in small + large:
        copy.start()
    for copy in small:
        copy.wait()
    codes = jnp.where(iota((slots, sources), 0) < counts[...], targets[...], -1)
    codes = jnp.concatenate([codes] * (128 // slots), axis=0)
    codes = jnp.where(iota(codes.shape, 0) // slots == place[2] % (128 // slots), codes, 0)
    row = codes.astype(F32).T
    for i in range(parts):
        large[i].wait()
        for s in range(i * step, (i + 1) * step):
            out[17 * s : 17 * s + 8, :] = partials[s, :, :128]
            out[17 * s + 8 : 17 * s + 16, :] = partials[s, :, 128:]
            out[17 * s + 16 : 17 * s + 17, :] = row[s : s + 1, :]


def unpack(payload):
    sources = payload.shape[0] // 17
    left, right, codes = [], [], []
    for g in range(sources // 16):
        row = jnp.zeros((1, 128), F32)
        for s in range(16 * g, 16 * g + 16):
            left.append(payload[17 * s : 17 * s + 8, :])
            right.append(payload[17 * s + 8 : 17 * s + 16, :])
            row = row + payload[17 * s + 16 : 17 * s + 17, :]
        codes.append(row)
    values = jnp.concatenate([jnp.concatenate(left, axis=0), jnp.concatenate(right, axis=0)], axis=1)
    return halves(values), jnp.concatenate(codes, axis=1).astype(jnp.int32)


def hot_of(code, rows, u):
    return (code == iota((rows, code.shape[1]), 0) * 4 + u).astype(F32).astype(BF16)


def rows_hot(chosen, rows):
    return (chosen[:, 0:1] == iota((chosen.shape[0], rows), 1)).astype(F32).astype(BF16)


def assemble_kernel(payload, front, own, matrix_out, pivots_out):
    (high, low), code = unpack(payload)
    rows = front.shape[0]
    pivot_hot = rows_hot(own, rows)
    for u in range(4):
        cols = slice(u * B, (u + 1) * B)
        hot = hot_of(code, rows, u)
        tile = front[:, cols] + (dot(hot, high) + dot(hot, low))
        matrix_out[:, cols] = tile
        pivots_out[:, cols] = pick(pivot_hot, tile)


def front_kernel(front, give, out):
    keep = give.shape[0]
    hot = rows_hot(give, front.shape[0])
    for u in range(4):
        out[u * keep : (u + 1) * keep, :] = pick(hot, front[:, u * B : (u + 1) * B])


def lead_kernel(payload, front_rows, give, send_first, send_rest):
    (high, low), code = unpack(payload)
    keep = give.shape[0]
    chosen = give[:, 0:1] * 4
    hot = jnp.concatenate([(chosen + u == code).astype(F32) for u in range(4)], axis=0).astype(BF16)
    sums = front_rows[...] + (dot(hot, high) + dot(hot, low))
    for i in range(send_first.shape[0] // keep):
        send_first[i * keep : (i + 1) * keep, :] = sums[:keep]
    for i in range(send_rest.shape[0] // keep):
        for u in range(1, 4):
            send_rest[i * keep : (i + 1) * keep, (u - 1) * B : u * B] = sums[u * keep : (u + 1) * keep]


def tiles_kernel(payload, front, first_out, rest_out):
    (high, low), code = unpack(payload)
    for u in range(4):
        hot = hot_of(code, front.shape[0], u)
        tile = front[:, u * B : (u + 1) * B] + (dot(hot, high) + dot(hot, low))
        if u == 0:
            first_out[...] = tile
        else:
            rest_out[:, (u - 1) * B : u * B] = tile


def sort_kernel(slot, gathered, out):
    out[...] = pick(rows_hot(slot, gathered.shape[0]), gathered[...])


def inverse_of(diag):
    eye = iota((B, B), 0) == iota((B, B), 1)
    only = jnp.where(eye, diag, 0.0)
    by_row = 1.0 / jnp.sum(only, axis=1, keepdims=True)
    by_col = 1.0 / jnp.sum(only, axis=0, keepdims=True)
    two = jnp.where(eye, 2.0, 0.0)
    x = by_row * (two - diag * by_col)
    xs = halves(x)
    return dot3(xs, halves(two - dot3(halves(diag), xs)))


def panel_kernel(place, w_own, w_other, r_own, r_other, active, half_out, tile_out):
    even = place[1] % 2 == 0
    w0 = jnp.where(even, w_own[...], w_other[...])
    w1 = jnp.where(even, w_other[...], w_own[...])
    r0 = jnp.where(even, r_own[...], r_other[...])
    r1 = jnp.where(even, r_other[...], r_own[...])
    act0 = active[0][:, 0:1]
    act1 = active[1][:, 0:1]
    inv0 = halves(inverse_of(w0[:B]))
    m0w = dot3(halves(w0[B:]), inv0)
    m0w_s = halves(m0w)
    p01 = halves(w1[:B])
    inv1 = halves(inverse_of(w1[B:] - dot3(m0w_s, p01)))
    m0 = dot3(halves(r0), inv0)
    m0a = jnp.where(act0 > 0, m0, 0.0)
    r1 = r1 - dot3(halves(m0a), p01)
    m1 = dot3(halves(r1), inv1)
    n1 = jnp.where(act1 > 0, m1, 0.0)
    n0 = m0a - dot3(halves(n1), m0w_s)
    half_out[...] = jnp.where(even, n0, n1)
    tile_out[...] = jnp.where(even, jnp.where(act0 > 0, m0, r0), jnp.where(act1 > 0, m1, r1))


def update_kernel(place, matrix, pivots, n_own, n_other, tile, out):
    even = place[1] % 2 == 0
    n0 = halves(jnp.where(even, n_own[...], n_other[...]))
    n1 = halves(jnp.where(even, n_other[...], n_own[...]))
    for u in range(4):
        cols = slice(u * B, (u + 1) * B)
        new = matrix[:, cols] - (
            dot3(n0, halves(pivots[:B, cols])) + dot3(n1, halves(pivots[B:, cols]))
        )
        if u == 0:
            new = jnp.where(place[1] < 2, tile[...], new)
        out[:, cols] = new


def finish_kernel(
    place, slot_hbm, n_early, n_late, o_early, o_late, first_hbm, w_first_hbm, tile_hbm, rest_hbm, w_rest_hbm, out_hbm,
    slot, n_own, n_other, first, w_first, tile, rest, w_rest, out, sems
):
    q = place[1]
    even = q % 2 == 0
    own_early = (q < 3) | (q == 7)
    other_early = (q < 2) | (q == 3) | (q == 6)
    copy = pltpu.make_async_copy

    @pl.when(own_early)
    def _():
        copy(n_early, n_own, sems.at[0]).start()

    @pl.when(jnp.logical_not(own_early))
    def _():
        copy(n_late, n_own, sems.at[0]).start()

    @pl.when(other_early)
    def _():
        copy(o_early, n_other, sems.at[1]).start()

    @pl.when(jnp.logical_not(other_early))
    def _():
        copy(o_late, n_other, sems.at[1]).start()

    moves = [
        copy(slot_hbm, slot, sems.at[2]),
        copy(first_hbm, first, sems.at[3]),
        copy(w_first_hbm, w_first, sems.at[4]),
        copy(tile_hbm, tile, sems.at[5]),
        copy(rest_hbm, rest, sems.at[6]),
        copy(w_rest_hbm, w_rest, sems.at[7]),
    ]
    for move in moves:
        move.start()
    copy(n_early, n_own, sems.at[0]).wait()
    copy(o_early, n_other, sems.at[1]).wait()
    h0, l0 = halves(jnp.where(even, n_own[...], n_other[...]))
    h1, l1 = halves(jnp.where(even, n_other[...], n_own[...]))
    for move in moves[1:4]:
        move.wait()
    rows = first.shape[0]
    half = out.shape[1]
    new = first[...] - (dot3((h0, l0), halves(w_first[:B])) + dot3((h1, l1), halves(w_first[B:])))
    new = jnp.where(q < 2, tile[...], new)
    for t in range(rows // half):
        out[t, :, 0, :] = new[t * half : (t + 1) * half]
    moves[0].wait()
    hot = rows_hot(slot, w_rest.shape[0])
    high = (dot(h0, hot[:B]) + dot(h1, hot[B:])).astype(BF16)
    low = (dot(l0, hot[:B]) + dot(l1, hot[B:])).astype(BF16)
    for move in moves[4:]:
        move.wait()
    w = [halves(w_rest[:, u * B : (u + 1) * B]) for u in range(3)]
    block = half // 2
    sent = []
    for i in range(rows // block):
        t, at = i * block // half, i * block % half
        span = slice(i * block, (i + 1) * block)
        n = (high[span], low[span])
        for u in range(1, 4):
            out[t, at : at + block, u, :] = rest[span, (u - 1) * B : u * B] - dot3(n, w[u - 1])
        done = copy(out.at[t, at : at + block], out_hbm.at[t, at : at + block], sems.at[8 + i])
        done.start()
        sent.append(done)
    for done in sent:
        done.wait()


def call(kernel, outs, n_in, scalars=1, outs_in_smem=0, flops=0, moved=0):
    specs = jax.tree.map(lambda _: VM, outs)
    if outs_in_smem:
        specs = specs[:-outs_in_smem] + (SM,) * outs_in_smem
    return pl.pallas_call(
        kernel,
        out_shape=outs,
        in_specs=[SM] * scalars + [VM] * (n_in - scalars),
        out_specs=specs,
        cost_estimate=pl.CostEstimate(flops=flops, bytes_accessed=moved, transcendentals=0),
        **PARAMS,
    )


def shaped(*shape, dtype=F32):
    return jax.ShapeDtypeStruct(shape, dtype)


def core_swap(x):
    return lax.ppermute(x, "pcol", [(i, i ^ 1) for i in range(lax.axis_size("pcol"))])


def spread_z(x, z):
    one = lax.ppermute(x, "pcol", [(0, 2), (1, 3)])
    three = lax.ppermute(x, "pcol", [(0, 6), (1, 7)])
    two = lax.ppermute(x, "pcol", [(0, 4), (1, 5)])
    return jnp.where(z == 0, x, jnp.where(z == 1, one, jnp.where(z == 2, two, three)))


def body(front, partials, targets, counts, local_picks, level_picks, order):
    rows = front.shape[0] * front.shape[1]
    cols = front.shape[2] * front.shape[3]
    p = lax.axis_index("prow")
    q = lax.axis_index("pcol")
    me = p * lax.axis_size("pcol") + q
    place = jnp.stack([p, q, me]).astype(jnp.int32)
    sources = partials.shape[1]
    slots = partials.shape[2]

    payload = pl.pallas_call(
        pack_kernel,
        out_shape=shaped(sources * 17, 128),
        in_specs=[SM, HBM, HBM, HBM],
        out_specs=VM,
        scratch_shapes=[
            pltpu.VMEM((sources, slots, B), F32),
            pltpu.VMEM((slots, sources), jnp.int32),
            pltpu.VMEM((1, sources), jnp.int32),
            pltpu.SemaphoreType.DMA((6,)),
        ],
        cost_estimate=pl.CostEstimate(flops=10**6, bytes_accessed=2 * 10**6, transcendentals=0),
        **ALONE,
    )(place, partials[0], targets[0].T, counts).reshape(sources * 17, 1, 128)
    payload = lax.all_to_all(payload, ("prow", "pcol"), 0, 0, tiled=True).reshape(sources * 17, 128)

    own, active, give, slot, fits = call(
        index_kernel,
        (
            shaped(2 * B, 128, dtype=jnp.int32),
            shaped(2, rows, 128),
            shaped(KEEP, 128, dtype=jnp.int32),
            shaped(2 * B, 128, dtype=jnp.int32),
            shaped(1, dtype=jnp.int32),
        ),
        4,
        outs_in_smem=1,
        flops=10**9,
        moved=10**6,
    )(place, local_picks, level_picks, order)
    front, own = lax.optimization_barrier((front, own))
    flat = front.reshape(rows, cols)
    copies = lax.axis_size("prow") * KEEP
    share_rows = 2 * B // lax.axis_size("prow")

    front_rows = call(front_kernel, shaped(4 * KEEP, B), 2, scalars=0, flops=10**8, moved=3 * 10**6)(flat, give)

    def gather(payload, flat, own, active, give, slot, place, front_rows):
        send_first, send_rest = call(
            lead_kernel, (shaped(copies, B), shaped(copies, cols - B)), 3, scalars=0, flops=10**8, moved=2 * 10**6
        )(payload, front_rows, give)
        w_first = lax.all_to_all(send_first, "prow", 0, 0, tiled=True)
        w_rest = lax.all_to_all(send_rest, "prow", 0, 0, tiled=True)
        first, rest = call(
            tiles_kernel, (shaped(rows, B), shaped(rows, cols - B)), 2, scalars=0, flops=4 * 10**9, moved=6 * 10**6
        )(payload, flat)
        r_other = core_swap(first)
        w_first = call(sort_kernel, shaped(2 * B, B), 2, scalars=0, flops=10**8, moved=10**6)(slot, w_first)
        w_other = core_swap(w_first)
        half, tile = call(
            panel_kernel, (shaped(rows, B), shaped(rows, B)), 6, flops=2 * 10**9, moved=4 * 10**6
        )(place, w_first, w_other, first, r_other, active)
        q = place[1]
        step = lax.ppermute(half, "pcol", [(0, 2), (1, 7)])
        n_early = jnp.where((q == 2) | (q == 7), step, half)
        n_late = lax.ppermute(n_early, "pcol", [(1, 3), (0, 6), (2, 4), (7, 5)])
        o_early = lax.ppermute(n_early, "pcol", [(0, 1), (1, 0), (2, 3), (7, 6)])
        o_late = lax.ppermute(n_late, "pcol", [(3, 2), (6, 7), (4, 5), (5, 4)])
        return pl.pallas_call(
            finish_kernel,
            out_shape=shaped(*front.shape),
            in_specs=[SM] + [HBM] * 10,
            out_specs=HBM,
            scratch_shapes=[
                pltpu.VMEM((2 * B, 128), jnp.int32),
                pltpu.VMEM((rows, B), F32),
                pltpu.VMEM((rows, B), F32),
                pltpu.VMEM((rows, B), F32),
                pltpu.VMEM((2 * B, B), F32),
                pltpu.VMEM((rows, B), F32),
                pltpu.VMEM((rows, cols - B), F32),
                pltpu.VMEM((copies, cols - B), F32),
                pltpu.VMEM(front.shape, F32),
                pltpu.SemaphoreType.DMA((12,)),
            ],
            cost_estimate=pl.CostEstimate(flops=4 * 10**9, bytes_accessed=8 * 10**6, transcendentals=0),
            **ALONE,
        )(place, slot, n_early, n_late, o_early, o_late, first, w_first, tile, rest, w_rest)

    def add_up(payload, flat, own, active, give, slot, place, front_rows):
        matrix, pivots = call(
            assemble_kernel, (shaped(rows, cols), shaped(2 * B, cols)), 3, scalars=0, flops=4 * 10**9, moved=8 * 10**6
        )(payload, flat, own)
        r_own = matrix[:, :B]
        r_other = core_swap(r_own)
        share = lax.all_to_all(pivots, "prow", 0, 0, tiled=True).reshape(-1, share_rows, cols).sum(axis=0)
        pivots = lax.all_to_all(jnp.tile(share, (lax.axis_size("prow"), 1)), "prow", 0, 0, tiled=True)
        w_own = pivots[:, :B]
        w_other = core_swap(w_own)
        half, tile = call(
            panel_kernel, (shaped(rows, B), shaped(rows, B)), 6, flops=2 * 10**9, moved=4 * 10**6
        )(place, w_own, w_other, r_own, r_other, active)
        n_own = spread_z(half, place[1] // 2)
        n_other = core_swap(n_own)
        out = call(update_kernel, shaped(rows, cols), 6, flops=2 * 10**9, moved=8 * 10**6)(
            place, matrix, pivots, n_own, n_other, tile
        )
        return out.reshape(front.shape)

    return lax.cond(fits[0] == 1, gather, add_up, payload, flat, own, active, give, slot, place, front_rows)


def solution(mesh):
    placed = (
        P(None, "prow", None, "pcol"),
        P(("prow", "pcol"), None, None, None),
        P(("prow", "pcol"), None, None),
        P(("prow", "pcol"), None),
        P(),
        P(),
        P(),
    )
    return jax.shard_map(
        body, mesh=mesh, in_specs=placed, out_specs=P(None, "prow", None, "pcol"), check_vma=False
    )
```

```python
import functools

import jax
import jax.numpy as jnp
from jax import lax
from jax.experimental import pallas as pl
from jax.experimental.pallas import tpu as pltpu
from jax.sharding import PartitionSpec as P

F32 = jnp.float32
BF16 = jnp.bfloat16
VM = pl.BlockSpec(memory_space=pltpu.VMEM)
HBM = pl.BlockSpec(memory_space=pltpu.HBM)
SM = pl.BlockSpec(memory_space=pltpu.SMEM)
B = 256
KEEP = 48
PARAMS = dict(compiler_params=pltpu.CompilerParams(vmem_limit_bytes=14 * 1024 * 1024))

ALONE = dict(compiler_params=pltpu.CompilerParams(vmem_limit_bytes=63 * 1024 * 1024))


def iota(shape, dim):
    return lax.broadcasted_iota(jnp.int32, shape, dim)


def dot(a, b):
    return jnp.dot(a, b, preferred_element_type=F32)


def halves(x):
    high = x.astype(BF16)
    return high, (x - high.astype(F32)).astype(BF16)


def dot3(a, b):
    ah, al = a
    bh, bl = b
    return dot(ah, bh) + (dot(ah, bl) + dot(al, bh))


def pick(onehot, x):
    high, low = halves(x)
    return dot(onehot, high) + dot(onehot, low)


def lookup(table, d, pos):
    n = pos.shape[1]
    hot = (iota((B, n), 0) == pos).astype(F32).astype(BF16)
    high = table // 256
    low = table - high * 256
    both = jnp.concatenate([high, low], axis=0).astype(F32).astype(BF16)
    got = dot(both, hot).astype(jnp.int32)
    rows = table.shape[0]
    values = got[:rows] * 256 + got[rows:]
    return jnp.sum(jnp.where(iota((rows, n), 0) == d, values, 0), axis=0, keepdims=True)


def turn(apart):
    apart = apart & 3
    return jnp.where(apart == 0, 0, jnp.where(apart == 1, 2, jnp.where(apart == 2, 3, 1)))


def index_kernel(place, local_picks, level_picks, order, own_out, active_out, give_out, slot_out, xy_out, yx_out, fits_out):
    rows = active_out.shape[1]
    keep = give_out.shape[0]
    p = place[0]
    retired = jnp.zeros((rows, 1), F32)
    owners, locals_ = [], []
    for k in range(order.shape[0]):
        pos = order[k : k + 1, :]
        d = jnp.zeros_like(pos)
        for level in range(level_picks.shape[1] - 1, -1, -1):
            j = lookup(level_picks[k, level], d, pos)
            bit = 1 << level
            d = (d & ~bit) | jnp.where(j >= B, bit, 0)
            pos = j & (B - 1)
        r = lookup(local_picks[k], d, pos)
        own = jnp.where(d == p, r, -1)
        own_out[k * B : (k + 1) * B, :] = jnp.broadcast_to(own, (128, B)).T
        hit = (iota((rows, B), 0) == own).astype(F32)
        retired = jnp.maximum(retired, jnp.max(hit, axis=1, keepdims=True))
        active_out[k] = jnp.broadcast_to(1.0 - retired, (rows, 128))
        owners.append(d)
        locals_.append(r)
    d = jnp.concatenate(owners, axis=1)
    r = jnp.concatenate(locals_, axis=1)
    n = d.shape[1]
    d_col = jnp.broadcast_to(d, (128, n)).T[:, 0:1]
    before = (d_col == d) & (iota((n, n), 0) < iota((n, n), 1))
    rank = jnp.sum(before.astype(jnp.int32), axis=0, keepdims=True)
    fits_out[0] = (jnp.max(rank) < keep).astype(jnp.int32)
    slot_out[...] = jnp.broadcast_to(d * keep + rank, (128, n)).T
    across = turn(d - p)
    down = turn((d >> 2) - (p >> 2))
    xy_out[...] = jnp.broadcast_to((down * 4 + across) * keep + rank, (128, n)).T
    yx_out[...] = jnp.broadcast_to((across * 4 + down) * keep + rank, (128, n)).T
    mine = (iota((keep, n), 0) == rank) & (d == p)
    give = jnp.sum(jnp.where(mine, r + 2, 0), axis=1, keepdims=True) - 2
    give_out[...] = jnp.broadcast_to(give, (keep, 128))


def pack_kernel(place, partials_hbm, targets_hbm, counts_hbm, out, partials, targets, counts, sems):
    slots, sources = targets.shape
    parts = sems.shape[0] - 2
    step = sources // parts
    small = [
        pltpu.make_async_copy(targets_hbm, targets, sems.at[parts]),
        pltpu.make_async_copy(counts_hbm, counts, sems.at[parts + 1]),
    ]
    large = [
        pltpu.make_async_copy(
            partials_hbm.at[i * step : (i + 1) * step], partials.at[i * step : (i + 1) * step], sems.at[i]
        )
        for i in range(parts)
    ]
    for copy in small + large:
        copy.start()
    for copy in small:
        copy.wait()
    codes = jnp.where(iota((slots, sources), 0) < counts[...], targets[...], -1)
    codes = jnp.concatenate([codes] * (128 // slots), axis=0)
    codes = jnp.where(iota(codes.shape, 0) // slots == place[2] % (128 // slots), codes, 0)
    row = codes.astype(F32).T
    for i in range(parts):
        large[i].wait()
        for s in range(i * step, (i + 1) * step):
            out[17 * s : 17 * s + 8, :] = partials[s, :, :128]
            out[17 * s + 8 : 17 * s + 16, :] = partials[s, :, 128:]
            out[17 * s + 16 : 17 * s + 17, :] = row[s : s + 1, :]


def unpack(payload):
    sources = payload.shape[0] // 17
    left, right, codes = [], [], []
    for g in range(sources // 16):
        row = jnp.zeros((1, 128), F32)
        for s in range(16 * g, 16 * g + 16):
            left.append(payload[17 * s : 17 * s + 8, :])
            right.append(payload[17 * s + 8 : 17 * s + 16, :])
            row = row + payload[17 * s + 16 : 17 * s + 17, :]
        codes.append(row)
    values = jnp.concatenate([jnp.concatenate(left, axis=0), jnp.concatenate(right, axis=0)], axis=1)
    return halves(values), jnp.concatenate(codes, axis=1).astype(jnp.int32)


def hot_of(code, rows, u):
    return (code == iota((rows, code.shape[1]), 0) * 4 + u).astype(F32).astype(BF16)


def rows_hot(chosen, rows):
    return (chosen[:, 0:1] == iota((chosen.shape[0], rows), 1)).astype(F32).astype(BF16)


def assemble_kernel(payload, front, own, matrix_out, pivots_out):
    (high, low), code = unpack(payload)
    rows = front.shape[0]
    pivot_hot = rows_hot(own, rows)
    for u in range(4):
        cols = slice(u * B, (u + 1) * B)
        hot = hot_of(code, rows, u)
        tile = front[:, cols] + (dot(hot, high) + dot(hot, low))
        matrix_out[:, cols] = tile
        pivots_out[:, cols] = pick(pivot_hot, tile)


def front_kernel(front, give, out):
    keep = give.shape[0]
    hot = rows_hot(give, front.shape[0])
    for u in range(4):
        out[u * keep : (u + 1) * keep, :] = pick(hot, front[:, u * B : (u + 1) * B])


def lead_kernel(payload, front_rows, give, send_first, send_xy, send_yx):
    (high, low), code = unpack(payload)
    keep = give.shape[0]
    chosen = give[:, 0:1] * 4
    hot = jnp.concatenate([(chosen + u == code).astype(F32) for u in range(4)], axis=0).astype(BF16)
    sums = front_rows[...] + (dot(hot, high) + dot(hot, low))
    for i in range(send_first.shape[0] // keep):
        send_first[i * keep : (i + 1) * keep, :] = sums[:keep]
    send_xy[:, :B] = sums[keep : 2 * keep]
    send_xy[:, B:] = sums[2 * keep : 3 * keep, : B // 2]
    send_yx[:, : B // 2] = sums[2 * keep : 3 * keep, B // 2 :]
    send_yx[:, B // 2 :] = sums[3 * keep :]


def tiles_kernel(payload, front, first_out, rest_out):
    (high, low), code = unpack(payload)
    for u in range(4):
        hot = hot_of(code, front.shape[0], u)
        tile = front[:, u * B : (u + 1) * B] + (dot(hot, high) + dot(hot, low))
        if u == 0:
            first_out[...] = tile
        else:
            rest_out[:, (u - 1) * B : u * B] = tile


def join_kernel(a0, a1, a2, a3, b0, b1, b2, b3, a_out, b_out, joined_out):
    size = a0.shape[0]
    for i, (a, b) in enumerate(((a0, b0), (a1, b1), (a2, b2), (a3, b3))):
        a_out[i * size : (i + 1) * size, :] = a[...]
        b_out[i * size : (i + 1) * size, :] = b[...]
    joined_out[...] = jnp.zeros_like(joined_out)


def sort_kernel(slot, gathered, joined, out):
    out[...] = pick(rows_hot(slot, gathered.shape[0]), gathered[...])


def inverse_of(diag):
    eye = iota((B, B), 0) == iota((B, B), 1)
    only = jnp.where(eye, diag, 0.0)
    by_row = 1.0 / jnp.sum(only, axis=1, keepdims=True)
    by_col = 1.0 / jnp.sum(only, axis=0, keepdims=True)
    two = jnp.where(eye, 2.0, 0.0)
    x = by_row * (two - diag * by_col)
    xs = halves(x)
    return dot3(xs, halves(two - dot3(halves(diag), xs)))


def sort_rest_kernel(xy, yx, a0, a1, a2, a3, b0, b1, b2, b3, high_out, low_out):
    width = a0.shape[1]
    for slot, parts, at in ((xy, (a0, a1, a2, a3), 0), (yx, (b0, b1, b2, b3), width)):
        size = a0.shape[0]
        hot = rows_hot(slot, 4 * size)
        high, low = halves(jnp.concatenate([part[...] for part in parts], axis=0))
        high_out[:, at : at + width] = dot(hot, high).astype(BF16)
        low_out[:, at : at + width] = dot(hot, low).astype(BF16)


def panel_kernel(place, w_own, w_other, r_own, r_other, active, half_out, tile_out):
    even = place[1] % 2 == 0
    w0 = jnp.where(even, w_own[...], w_other[...])
    w1 = jnp.where(even, w_other[...], w_own[...])
    r0 = jnp.where(even, r_own[...], r_other[...])
    r1 = jnp.where(even, r_other[...], r_own[...])
    act0 = active[0][:, 0:1]
    act1 = active[1][:, 0:1]
    inv0 = halves(inverse_of(w0[:B]))
    m0w = dot3(halves(w0[B:]), inv0)
    m0w_s = halves(m0w)
    p01 = halves(w1[:B])
    inv1 = halves(inverse_of(w1[B:] - dot3(m0w_s, p01)))
    m0 = dot3(halves(r0), inv0)
    m0a = jnp.where(act0 > 0, m0, 0.0)
    r1 = r1 - dot3(halves(m0a), p01)
    m1 = dot3(halves(r1), inv1)
    n1 = jnp.where(act1 > 0, m1, 0.0)
    n0 = m0a - dot3(halves(n1), m0w_s)
    half_out[...] = jnp.where(even, n0, n1)
    tile_out[...] = jnp.where(even, jnp.where(act0 > 0, m0, r0), jnp.where(act1 > 0, m1, r1))


def update_kernel(place, matrix, pivots, n_own, n_other, tile, out):
    even = place[1] % 2 == 0
    n0 = halves(jnp.where(even, n_own[...], n_other[...]))
    n1 = halves(jnp.where(even, n_other[...], n_own[...]))
    for u in range(4):
        cols = slice(u * B, (u + 1) * B)
        new = matrix[:, cols] - (
            dot3(n0, halves(pivots[:B, cols])) + dot3(n1, halves(pivots[B:, cols]))
        )
        if u == 0:
            new = jnp.where(place[1] < 2, tile[...], new)
        out[:, cols] = new


def finish_kernel(
    place, n_early, n_late, o_early, o_late, first_hbm, w_first_hbm, tile_hbm, rest_hbm, high_hbm, low_hbm, out_hbm,
    n_own, n_other, first, w_first, tile, rest, high, low, out, sems
):
    q = place[1]
    even = q % 2 == 0
    own_early = (q < 3) | (q == 7)
    other_early = (q < 2) | (q == 3) | (q == 6)
    copy = pltpu.make_async_copy

    @pl.when(own_early)
    def _():
        copy(n_early, n_own, sems.at[0]).start()

    @pl.when(jnp.logical_not(own_early))
    def _():
        copy(n_late, n_own, sems.at[0]).start()

    @pl.when(other_early)
    def _():
        copy(o_early, n_other, sems.at[1]).start()

    @pl.when(jnp.logical_not(other_early))
    def _():
        copy(o_late, n_other, sems.at[1]).start()

    moves = [
        copy(w_first_hbm, w_first, sems.at[2]),
        copy(first_hbm, first, sems.at[3]),
        copy(tile_hbm, tile, sems.at[4]),
        copy(high_hbm, high, sems.at[5]),
        copy(low_hbm, low, sems.at[6]),
        copy(rest_hbm, rest, sems.at[7]),
    ]
    for move in moves:
        move.start()
    copy(n_early, n_own, sems.at[0]).wait()
    copy(o_early, n_other, sems.at[1]).wait()
    h0, l0 = halves(jnp.where(even, n_own[...], n_other[...]))
    h1, l1 = halves(jnp.where(even, n_other[...], n_own[...]))
    rows = first.shape[0]
    half = out.shape[1]
    block = half // 2
    for move in moves[:3]:
        move.wait()
    n_high = jnp.concatenate([h0, h1], axis=1)
    n_low = jnp.concatenate([l0, l1], axis=1)
    new = first[...] - dot3((n_high, n_low), halves(w_first[...]))
    new = jnp.where(q < 2, tile[...], new)
    for t in range(rows // half):
        out[t, :, 0, :] = new[t * half : (t + 1) * half]
    for move in moves[3:]:
        move.wait()
    sent = []
    for i in range(rows // block):
        t, at = i * block // half, i * block % half
        span = slice(i * block, (i + 1) * block)
        for u in range(1, 4):
            cols = slice((u - 1) * B, u * B)
            out[t, at : at + block, u, :] = rest[span, cols] - dot3((n_high[span], n_low[span]), (high[:, cols], low[:, cols]))
        done = copy(out.at[t, at : at + block], out_hbm.at[t, at : at + block], sems.at[8 + i])
        done.start()
        sent.append(done)
    for done in sent:
        done.wait()


def call(kernel, outs, n_in, scalars=1, outs_in_smem=0, flops=0, moved=0):
    specs = jax.tree.map(lambda _: VM, outs)
    if outs_in_smem:
        specs = specs[:-outs_in_smem] + (SM,) * outs_in_smem
    return pl.pallas_call(
        kernel,
        out_shape=outs,
        in_specs=[SM] * scalars + [VM] * (n_in - scalars),
        out_specs=specs,
        cost_estimate=pl.CostEstimate(flops=flops, bytes_accessed=moved, transcendentals=0),
        **PARAMS,
    )


def shaped(*shape, dtype=F32):
    return jax.ShapeDtypeStruct(shape, dtype)


def core_swap(x):
    return lax.ppermute(x, "pcol", [(i, i ^ 1) for i in range(lax.axis_size("pcol"))])


def shift_x(step):
    return [(p, p // 4 * 4 + (p + step) % 4) for p in range(16)]


def shift_y(step):
    return [(p, (p + 4 * step) % 16) for p in range(16)]


def ring(x, shift):
    return [x] + [lax.ppermute(x, "prow", shift(step)) for step in (1, -1, 2)]


def spread_z(x, z):
    one = lax.ppermute(x, "pcol", [(0, 2), (1, 3)])
    three = lax.ppermute(x, "pcol", [(0, 6), (1, 7)])
    two = lax.ppermute(x, "pcol", [(0, 4), (1, 5)])
    return jnp.where(z == 0, x, jnp.where(z == 1, one, jnp.where(z == 2, two, three)))


def body(front, partials, targets, counts, local_picks, level_picks, order):
    rows = front.shape[0] * front.shape[1]
    cols = front.shape[2] * front.shape[3]
    p = lax.axis_index("prow")
    q = lax.axis_index("pcol")
    me = p * lax.axis_size("pcol") + q
    place = jnp.stack([p, q, me]).astype(jnp.int32)
    sources = partials.shape[1]
    slots = partials.shape[2]

    payload = pl.pallas_call(
        pack_kernel,
        out_shape=shaped(sources * 17, 128),
        in_specs=[SM, HBM, HBM, HBM],
        out_specs=VM,
        scratch_shapes=[
            pltpu.VMEM((sources, slots, B), F32),
            pltpu.VMEM((slots, sources), jnp.int32),
            pltpu.VMEM((1, sources), jnp.int32),
            pltpu.SemaphoreType.DMA((6,)),
        ],
        cost_estimate=pl.CostEstimate(flops=10**6, bytes_accessed=2 * 10**6, transcendentals=0),
        **ALONE,
    )(place, partials[0], targets[0].T, counts).reshape(sources * 17, 1, 128)
    payload = lax.all_to_all(payload, ("prow", "pcol"), 0, 0, tiled=True).reshape(sources * 17, 128)

    lists = shaped(2 * B, 128, dtype=jnp.int32)
    own, active, give, slot, xy, yx, fits = call(
        index_kernel,
        (
            lists,
            shaped(2, rows, 128),
            shaped(KEEP, 128, dtype=jnp.int32),
            lists,
            lists,
            lists,
            shaped(1, dtype=jnp.int32),
        ),
        4,
        outs_in_smem=1,
        flops=10**9,
        moved=10**6,
    )(place, local_picks, level_picks, order)
    front, own = lax.optimization_barrier((front, own))
    flat = front.reshape(rows, cols)
    copies = lax.axis_size("prow") * KEEP
    share_rows = 2 * B // lax.axis_size("prow")

    front_rows = call(front_kernel, shaped(4 * KEEP, B), 2, scalars=0, flops=10**8, moved=3 * 10**6)(flat, give)

    def gather(payload, flat, own, active, give, slot, xy, yx, place, front_rows):
        wide = (cols - B) // 2
        send_first, send_xy, send_yx = call(
            lead_kernel,
            (shaped(copies, B), shaped(KEEP, wide), shaped(KEEP, wide)),
            3,
            scalars=0,
            flops=10**8,
            moved=2 * 10**6,
        )(payload, front_rows, give)
        w_first = lax.all_to_all(send_first, "prow", 0, 0, tiled=True)
        send_xy, send_yx, joined = call(
            join_kernel, (shaped(4 * KEEP, wide), shaped(4 * KEEP, wide), shaped(8, 128)), 8, scalars=0, moved=2 * 10**6
        )(*ring(send_xy, shift_x), *ring(send_yx, shift_y))
        all_xy = ring(send_xy, shift_y)
        all_yx = ring(send_yx, shift_x)
        first, rest = call(
            tiles_kernel, (shaped(rows, B), shaped(rows, cols - B)), 2, scalars=0, flops=4 * 10**9, moved=6 * 10**6
        )(payload, flat)
        r_other = core_swap(first)
        w_first = call(sort_kernel, shaped(2 * B, B), 3, scalars=0, flops=10**8, moved=10**6)(slot, w_first, joined)
        w_high, w_low = call(
            sort_rest_kernel,
            (shaped(2 * B, cols - B, dtype=BF16), shaped(2 * B, cols - B, dtype=BF16)),
            10,
            scalars=0,
            flops=10**9,
            moved=4 * 10**6,
        )(xy, yx, *all_xy, *all_yx)
        w_other = core_swap(w_first)
        half, tile = call(
            panel_kernel, (shaped(rows, B), shaped(rows, B)), 6, flops=2 * 10**9, moved=4 * 10**6
        )(place, w_first, w_other, first, r_other, active)
        q = place[1]
        step = lax.ppermute(half, "pcol", [(0, 2), (1, 7)])
        n_early = jnp.where((q == 2) | (q == 7), step, half)
        n_late = lax.ppermute(n_early, "pcol", [(1, 3), (0, 6), (2, 4), (7, 5)])
        o_early = lax.ppermute(n_early, "pcol", [(0, 1), (1, 0), (2, 3), (7, 6)])
        o_late = lax.ppermute(n_late, "pcol", [(3, 2), (6, 7), (4, 5), (5, 4)])
        return pl.pallas_call(
            finish_kernel,
            out_shape=shaped(*front.shape),
            in_specs=[SM] + [HBM] * 10,
            out_specs=HBM,
            scratch_shapes=[
                pltpu.VMEM((rows, B), F32),
                pltpu.VMEM((rows, B), F32),
                pltpu.VMEM((rows, B), F32),
                pltpu.VMEM((2 * B, B), F32),
                pltpu.VMEM((rows, B), F32),
                pltpu.VMEM((rows, cols - B), F32),
                pltpu.VMEM((2 * B, cols - B), BF16),
                pltpu.VMEM((2 * B, cols - B), BF16),
                pltpu.VMEM(front.shape, F32),
                pltpu.SemaphoreType.DMA((12,)),
            ],
            cost_estimate=pl.CostEstimate(flops=4 * 10**9, bytes_accessed=8 * 10**6, transcendentals=0),
            **ALONE,
        )(place, n_early, n_late, o_early, o_late, first, w_first, tile, rest, w_high, w_low)

    def add_up(payload, flat, own, active, give, slot, xy, yx, place, front_rows):
        matrix, pivots = call(
            assemble_kernel, (shaped(rows, cols), shaped(2 * B, cols)), 3, scalars=0, flops=4 * 10**9, moved=8 * 10**6
        )(payload, flat, own)
        r_own = matrix[:, :B]
        r_other = core_swap(r_own)
        share = lax.all_to_all(pivots, "prow", 0, 0, tiled=True).reshape(-1, share_rows, cols).sum(axis=0)
        pivots = lax.all_to_all(jnp.tile(share, (lax.axis_size("prow"), 1)), "prow", 0, 0, tiled=True)
        w_own = pivots[:, :B]
        w_other = core_swap(w_own)
        half, tile = call(
            panel_kernel, (shaped(rows, B), shaped(rows, B)), 6, flops=2 * 10**9, moved=4 * 10**6
        )(place, w_own, w_other, r_own, r_other, active)
        n_own = spread_z(half, place[1] // 2)
        n_other = core_swap(n_own)
        out = call(update_kernel, shaped(rows, cols), 6, flops=2 * 10**9, moved=8 * 10**6)(
            place, matrix, pivots, n_own, n_other, tile
        )
        return out.reshape(front.shape)

    return lax.cond(fits[0] == 1, gather, add_up, payload, flat, own, active, give, slot, xy, yx, place, front_rows)


def solution(mesh):
    placed = (
        P(None, "prow", None, "pcol"),
        P(("prow", "pcol"), None, None, None),
        P(("prow", "pcol"), None, None),
        P(("prow", "pcol"), None),
        P(),
        P(),
        P(),
    )
    return jax.shard_map(
        body, mesh=mesh, in_specs=placed, out_specs=P(None, "prow", None, "pcol"), check_vma=False
    )
```

```python
import functools

import jax
import jax.numpy as jnp
from jax import lax
from jax.experimental import pallas as pl
from jax.experimental.pallas import tpu as pltpu
from jax.sharding import PartitionSpec as P

F32 = jnp.float32
BF16 = jnp.bfloat16
VM = pl.BlockSpec(memory_space=pltpu.VMEM)
HBM = pl.BlockSpec(memory_space=pltpu.HBM)
SM = pl.BlockSpec(memory_space=pltpu.SMEM)
B = 256
KEEP = 48
PARAMS = dict(compiler_params=pltpu.CompilerParams(vmem_limit_bytes=14 * 1024 * 1024))

ALONE = dict(compiler_params=pltpu.CompilerParams(vmem_limit_bytes=63 * 1024 * 1024))


def iota(shape, dim):
    return lax.broadcasted_iota(jnp.int32, shape, dim)


def dot(a, b):
    return jnp.dot(a, b, preferred_element_type=F32)


def halves(x):
    high = x.astype(BF16)
    return high, (x - high.astype(F32)).astype(BF16)


def dot3(a, b):
    ah, al = a
    bh, bl = b
    return dot(ah, bh) + (dot(ah, bl) + dot(al, bh))


def pick(onehot, x):
    high, low = halves(x)
    return dot(onehot, high) + dot(onehot, low)


def lookup(table, d, pos):
    n = pos.shape[1]
    hot = (iota((B, n), 0) == pos).astype(F32).astype(BF16)
    high = table // 256
    low = table - high * 256
    both = jnp.concatenate([high, low], axis=0).astype(F32).astype(BF16)
    got = dot(both, hot).astype(jnp.int32)
    rows = table.shape[0]
    values = got[:rows] * 256 + got[rows:]
    return jnp.sum(jnp.where(iota((rows, n), 0) == d, values, 0), axis=0, keepdims=True)


def turn(apart):
    apart = apart & 3
    return jnp.where(apart == 0, 0, jnp.where(apart == 1, 2, jnp.where(apart == 2, 3, 1)))


def index_kernel(place, local_picks, level_picks, order, own_out, active_out, give_out, slot_out, xy_out, yx_out, fits_out):
    rows = active_out.shape[1]
    keep = give_out.shape[0]
    p = place[0]
    retired = jnp.zeros((rows, 1), F32)
    owners, locals_ = [], []
    for k in range(order.shape[0]):
        pos = order[k : k + 1, :]
        d = jnp.zeros_like(pos)
        for level in range(level_picks.shape[1] - 1, -1, -1):
            j = lookup(level_picks[k, level], d, pos)
            bit = 1 << level
            d = (d & ~bit) | jnp.where(j >= B, bit, 0)
            pos = j & (B - 1)
        r = lookup(local_picks[k], d, pos)
        own = jnp.where(d == p, r, -1)
        own_out[k * B : (k + 1) * B, :] = jnp.broadcast_to(own, (128, B)).T
        hit = (iota((rows, B), 0) == own).astype(F32)
        retired = jnp.maximum(retired, jnp.max(hit, axis=1, keepdims=True))
        active_out[k] = jnp.broadcast_to(1.0 - retired, (rows, 128))
        owners.append(d)
        locals_.append(r)
    d = jnp.concatenate(owners, axis=1)
    r = jnp.concatenate(locals_, axis=1)
    n = d.shape[1]
    d_col = jnp.broadcast_to(d, (128, n)).T[:, 0:1]
    before = (d_col == d) & (iota((n, n), 0) < iota((n, n), 1))
    rank = jnp.sum(before.astype(jnp.int32), axis=0, keepdims=True)
    fits_out[0] = (jnp.max(rank) < keep).astype(jnp.int32)
    slot_out[...] = jnp.broadcast_to(d * keep + rank, (128, n)).T
    across = turn(d - p)
    down = turn((d >> 2) - (p >> 2))
    xy_out[...] = jnp.broadcast_to((down * 4 + across) * keep + rank, (128, n)).T
    yx_out[...] = jnp.broadcast_to((across * 4 + down) * keep + rank, (128, n)).T
    mine = (iota((keep, n), 0) == rank) & (d == p)
    give = jnp.sum(jnp.where(mine, r + 2, 0), axis=1, keepdims=True) - 2
    give_out[...] = jnp.broadcast_to(give, (keep, 128))


def pack_kernel(place, partials_hbm, targets_hbm, counts_hbm, out, partials, targets, counts, sems):
    slots, sources = targets.shape
    parts = sems.shape[0] - 2
    step = sources // parts
    small = [
        pltpu.make_async_copy(targets_hbm, targets, sems.at[parts]),
        pltpu.make_async_copy(counts_hbm, counts, sems.at[parts + 1]),
    ]
    large = [
        pltpu.make_async_copy(
            partials_hbm.at[i * step : (i + 1) * step], partials.at[i * step : (i + 1) * step], sems.at[i]
        )
        for i in range(parts)
    ]
    for copy in small + large:
        copy.start()
    for copy in small:
        copy.wait()
    codes = jnp.where(iota((slots, sources), 0) < counts[...], targets[...], -1)
    codes = jnp.concatenate([codes] * (128 // slots), axis=0)
    codes = jnp.where(iota(codes.shape, 0) // slots == place[2] % (128 // slots), codes, 0)
    row = codes.astype(F32).T
    for i in range(parts):
        large[i].wait()
        for s in range(i * step, (i + 1) * step):
            out[17 * s : 17 * s + 8, :] = partials[s, :, :128]
            out[17 * s + 8 : 17 * s + 16, :] = partials[s, :, 128:]
            out[17 * s + 16 : 17 * s + 17, :] = row[s : s + 1, :]


def unpack(payload):
    sources = payload.shape[0] // 17
    left, right, codes = [], [], []
    for g in range(sources // 16):
        row = jnp.zeros((1, 128), F32)
        for s in range(16 * g, 16 * g + 16):
            left.append(payload[17 * s : 17 * s + 8, :])
            right.append(payload[17 * s + 8 : 17 * s + 16, :])
            row = row + payload[17 * s + 16 : 17 * s + 17, :]
        codes.append(row)
    values = jnp.concatenate([jnp.concatenate(left, axis=0), jnp.concatenate(right, axis=0)], axis=1)
    return halves(values), jnp.concatenate(codes, axis=1).astype(jnp.int32)


def hot_of(code, rows, u):
    return (code == iota((rows, code.shape[1]), 0) * 4 + u).astype(F32).astype(BF16)


def rows_hot(chosen, rows):
    return (chosen[:, 0:1] == iota((chosen.shape[0], rows), 1)).astype(F32).astype(BF16)


def assemble_kernel(payload, front, own, matrix_out, pivots_out):
    (high, low), code = unpack(payload)
    rows = front.shape[0]
    pivot_hot = rows_hot(own, rows)
    for u in range(4):
        cols = slice(u * B, (u + 1) * B)
        hot = hot_of(code, rows, u)
        tile = front[:, cols] + (dot(hot, high) + dot(hot, low))
        matrix_out[:, cols] = tile
        pivots_out[:, cols] = pick(pivot_hot, tile)


def front_kernel(front, give, out):
    keep = give.shape[0]
    hot = rows_hot(give, front.shape[0])
    for u in range(4):
        out[u * keep : (u + 1) * keep, :] = pick(hot, front[:, u * B : (u + 1) * B])


def lead_kernel(payload, front_rows, give, send_first, send_rest):
    (high, low), code = unpack(payload)
    keep = give.shape[0]
    chosen = give[:, 0:1] * 4
    hot = jnp.concatenate([(chosen + u == code).astype(F32) for u in range(4)], axis=0).astype(BF16)
    sums = front_rows[...] + (dot(hot, high) + dot(hot, low))
    send_first[...] = sums[:keep]
    for i in range(send_rest.shape[0] // keep):
        for u in range(1, 4):
            send_rest[i * keep : (i + 1) * keep, (u - 1) * B : u * B] = sums[u * keep : (u + 1) * keep]


def tiles_kernel(payload, front, first_out, rest_out):
    (high, low), code = unpack(payload)
    for u in range(4):
        hot = hot_of(code, front.shape[0], u)
        tile = front[:, u * B : (u + 1) * B] + (dot(hot, high) + dot(hot, low))
        if u == 0:
            first_out[...] = tile
        else:
            rest_out[:, (u - 1) * B : u * B] = tile


def join_kernel(a0, a1, a2, a3, out):
    size = a0.shape[0]
    for i, a in enumerate((a0, a1, a2, a3)):
        out[i * size : (i + 1) * size, :] = a[...]


def sort_first_kernel(slot, a0, a1, a2, a3, out):
    hot = rows_hot(slot, 4 * a0.shape[0])
    out[...] = pick(hot, jnp.concatenate([part[...] for part in (a0, a1, a2, a3)], axis=0))


def sort_rest_kernel(slot, gathered, high_out, low_out):
    hot = rows_hot(slot, gathered.shape[0])
    high, low = halves(gathered[...])
    high_out[...] = dot(hot, high).astype(BF16)
    low_out[...] = dot(hot, low).astype(BF16)


def inverse_of(diag):
    eye = iota((B, B), 0) == iota((B, B), 1)
    only = jnp.where(eye, diag, 0.0)
    by_row = 1.0 / jnp.sum(only, axis=1, keepdims=True)
    by_col = 1.0 / jnp.sum(only, axis=0, keepdims=True)
    two = jnp.where(eye, 2.0, 0.0)
    x = by_row * (two - diag * by_col)
    xs = halves(x)
    return dot3(xs, halves(two - dot3(halves(diag), xs)))


def panel_kernel(place, w_own, w_other, r_own, r_other, active, half_out, tile_out):
    even = place[1] % 2 == 0
    w0 = jnp.where(even, w_own[...], w_other[...])
    w1 = jnp.where(even, w_other[...], w_own[...])
    r0 = jnp.where(even, r_own[...], r_other[...])
    r1 = jnp.where(even, r_other[...], r_own[...])
    act0 = active[0][:, 0:1]
    act1 = active[1][:, 0:1]
    inv0 = halves(inverse_of(w0[:B]))
    m0w = dot3(halves(w0[B:]), inv0)
    m0w_s = halves(m0w)
    p01 = halves(w1[:B])
    inv1 = halves(inverse_of(w1[B:] - dot3(m0w_s, p01)))
    m0 = dot3(halves(r0), inv0)
    m0a = jnp.where(act0 > 0, m0, 0.0)
    r1 = r1 - dot3(halves(m0a), p01)
    m1 = dot3(halves(r1), inv1)
    n1 = jnp.where(act1 > 0, m1, 0.0)
    n0 = m0a - dot3(halves(n1), m0w_s)
    half_out[...] = jnp.where(even, n0, n1)
    tile_out[...] = jnp.where(even, jnp.where(act0 > 0, m0, r0), jnp.where(act1 > 0, m1, r1))


def update_kernel(place, matrix, pivots, n_own, n_other, tile, out):
    even = place[1] % 2 == 0
    n0 = halves(jnp.where(even, n_own[...], n_other[...]))
    n1 = halves(jnp.where(even, n_other[...], n_own[...]))
    for u in range(4):
        cols = slice(u * B, (u + 1) * B)
        new = matrix[:, cols] - (
            dot3(n0, halves(pivots[:B, cols])) + dot3(n1, halves(pivots[B:, cols]))
        )
        if u == 0:
            new = jnp.where(place[1] < 2, tile[...], new)
        out[:, cols] = new


def finish_kernel(
    place, n_early, n_late, o_early, o_late, first_hbm, w_first_hbm, tile_hbm, rest_hbm, high_hbm, low_hbm, out_hbm,
    n_own, n_other, first, w_first, tile, rest, high, low, out, sems
):
    q = place[1]
    even = q % 2 == 0
    own_early = (q < 3) | (q == 7)
    other_early = (q < 2) | (q == 3) | (q == 6)
    copy = pltpu.make_async_copy

    @pl.when(own_early)
    def _():
        copy(n_early, n_own, sems.at[0]).start()

    @pl.when(jnp.logical_not(own_early))
    def _():
        copy(n_late, n_own, sems.at[0]).start()

    @pl.when(other_early)
    def _():
        copy(o_early, n_other, sems.at[1]).start()

    @pl.when(jnp.logical_not(other_early))
    def _():
        copy(o_late, n_other, sems.at[1]).start()

    moves = [
        copy(w_first_hbm, w_first, sems.at[2]),
        copy(first_hbm, first, sems.at[3]),
        copy(tile_hbm, tile, sems.at[4]),
        copy(high_hbm, high, sems.at[5]),
        copy(low_hbm, low, sems.at[6]),
        copy(rest_hbm, rest, sems.at[7]),
    ]
    for move in moves:
        move.start()
    copy(n_early, n_own, sems.at[0]).wait()
    copy(o_early, n_other, sems.at[1]).wait()
    h0, l0 = halves(jnp.where(even, n_own[...], n_other[...]))
    h1, l1 = halves(jnp.where(even, n_other[...], n_own[...]))
    rows = first.shape[0]
    half = out.shape[1]
    block = half // 2
    for move in moves[:3]:
        move.wait()
    n_high = jnp.concatenate([h0, h1], axis=1)
    n_low = jnp.concatenate([l0, l1], axis=1)
    new = first[...] - dot3((n_high, n_low), halves(w_first[...]))
    new = jnp.where(q < 2, tile[...], new)
    for t in range(rows // half):
        out[t, :, 0, :] = new[t * half : (t + 1) * half]
    for move in moves[3:]:
        move.wait()
    sent = []
    for i in range(rows // block):
        t, at = i * block // half, i * block % half
        span = slice(i * block, (i + 1) * block)
        for u in range(1, 4):
            cols = slice((u - 1) * B, u * B)
            out[t, at : at + block, u, :] = rest[span, cols] - dot3((n_high[span], n_low[span]), (high[:, cols], low[:, cols]))
        done = copy(out.at[t, at : at + block], out_hbm.at[t, at : at + block], sems.at[8 + i])
        done.start()
        sent.append(done)
    for done in sent:
        done.wait()


def call(kernel, outs, n_in, scalars=1, outs_in_smem=0, flops=0, moved=0):
    specs = jax.tree.map(lambda _: VM, outs)
    if outs_in_smem:
        specs = specs[:-outs_in_smem] + (SM,) * outs_in_smem
    return pl.pallas_call(
        kernel,
        out_shape=outs,
        in_specs=[SM] * scalars + [VM] * (n_in - scalars),
        out_specs=specs,
        cost_estimate=pl.CostEstimate(flops=flops, bytes_accessed=moved, transcendentals=0),
        **PARAMS,
    )


def shaped(*shape, dtype=F32):
    return jax.ShapeDtypeStruct(shape, dtype)


def core_swap(x):
    return lax.ppermute(x, "pcol", [(i, i ^ 1) for i in range(lax.axis_size("pcol"))])


def shift_x(step):
    return [(p, p // 4 * 4 + (p + step) % 4) for p in range(16)]


def shift_y(step):
    return [(p, (p + 4 * step) % 16) for p in range(16)]


def ring(x, shift):
    return [x] + [lax.ppermute(x, "prow", shift(step)) for step in (1, -1, 2)]


def spread_z(x, z):
    one = lax.ppermute(x, "pcol", [(0, 2), (1, 3)])
    three = lax.ppermute(x, "pcol", [(0, 6), (1, 7)])
    two = lax.ppermute(x, "pcol", [(0, 4), (1, 5)])
    return jnp.where(z == 0, x, jnp.where(z == 1, one, jnp.where(z == 2, two, three)))


def body(front, partials, targets, counts, local_picks, level_picks, order):
    rows = front.shape[0] * front.shape[1]
    cols = front.shape[2] * front.shape[3]
    p = lax.axis_index("prow")
    q = lax.axis_index("pcol")
    me = p * lax.axis_size("pcol") + q
    place = jnp.stack([p, q, me]).astype(jnp.int32)
    sources = partials.shape[1]
    slots = partials.shape[2]

    payload = pl.pallas_call(
        pack_kernel,
        out_shape=shaped(sources * 17, 128),
        in_specs=[SM, HBM, HBM, HBM],
        out_specs=VM,
        scratch_shapes=[
            pltpu.VMEM((sources, slots, B), F32),
            pltpu.VMEM((slots, sources), jnp.int32),
            pltpu.VMEM((1, sources), jnp.int32),
            pltpu.SemaphoreType.DMA((6,)),
        ],
        cost_estimate=pl.CostEstimate(flops=10**6, bytes_accessed=2 * 10**6, transcendentals=0),
        **ALONE,
    )(place, partials[0], targets[0].T, counts).reshape(sources * 17, 1, 128)
    payload = lax.all_to_all(payload, ("prow", "pcol"), 0, 0, tiled=True).reshape(sources * 17, 128)

    lists = shaped(2 * B, 128, dtype=jnp.int32)
    own, active, give, slot, xy, yx, fits = call(
        index_kernel,
        (
            lists,
            shaped(2, rows, 128),
            shaped(KEEP, 128, dtype=jnp.int32),
            lists,
            lists,
            lists,
            shaped(1, dtype=jnp.int32),
        ),
        4,
        outs_in_smem=1,
        flops=10**9,
        moved=10**6,
    )(place, local_picks, level_picks, order)
    front, own = lax.optimization_barrier((front, own))
    flat = front.reshape(rows, cols)
    copies = lax.axis_size("prow") * KEEP
    share_rows = 2 * B // lax.axis_size("prow")

    front_rows = call(front_kernel, shaped(4 * KEEP, B), 2, scalars=0, flops=10**8, moved=3 * 10**6)(flat, give)

    send_first, send_rest = call(
        lead_kernel, (shaped(KEEP, B), shaped(copies, cols - B)), 3, scalars=0, flops=10**8, moved=2 * 10**6
    )(payload, front_rows, give)
    w_rest = lax.all_to_all(send_rest, "prow", 0, 0, tiled=True)

    def panels(payload, flat, send_first, xy, active, place):
        joined = call(join_kernel, shaped(4 * KEEP, B), 4, scalars=0, moved=10**6)(*ring(send_first, shift_x))
        w_parts = ring(joined, shift_y)
        first, rest = call(
            tiles_kernel, (shaped(rows, B), shaped(rows, cols - B)), 2, scalars=0, flops=4 * 10**9, moved=6 * 10**6
        )(payload, flat)
        r_other = core_swap(first)
        w_first = call(sort_first_kernel, shaped(2 * B, B), 5, scalars=0, flops=10**8, moved=10**6)(xy, *w_parts)
        w_other = core_swap(w_first)
        half, tile = call(
            panel_kernel, (shaped(rows, B), shaped(rows, B)), 6, flops=2 * 10**9, moved=4 * 10**6
        )(place, w_first, w_other, first, r_other, active)
        q = place[1]
        step = lax.ppermute(half, "pcol", [(0, 2), (1, 7)])
        n_early = jnp.where((q == 2) | (q == 7), step, half)
        return n_early, first, w_first, tile, rest

    def nothing(payload, flat, send_first, xy, active, place):
        square = jnp.zeros((rows, B), F32)
        return square, square, jnp.zeros((2 * B, B), F32), square, jnp.zeros((rows, cols - B), F32)

    n_early, first, w_first, tile, rest = lax.cond(
        fits[0] == 1, panels, nothing, payload, flat, send_first, xy, active, place
    )
    n_late = lax.ppermute(n_early, "pcol", [(1, 3), (0, 6), (2, 4), (7, 5)])
    o_early = lax.ppermute(n_early, "pcol", [(0, 1), (1, 0), (2, 3), (7, 6)])
    o_late = lax.ppermute(n_late, "pcol", [(3, 2), (6, 7), (4, 5), (5, 4)])
    w_high, w_low = call(
        sort_rest_kernel,
        (shaped(2 * B, cols - B, dtype=BF16), shaped(2 * B, cols - B, dtype=BF16)),
        2,
        scalars=0,
        flops=10**9,
        moved=4 * 10**6,
    )(slot, w_rest)

    def finish(payload, flat, own, active, place, *arrays):
        return pl.pallas_call(
            finish_kernel,
            out_shape=shaped(*front.shape),
            in_specs=[SM] + [HBM] * 10,
            out_specs=HBM,
            scratch_shapes=[
                pltpu.VMEM((rows, B), F32),
                pltpu.VMEM((rows, B), F32),
                pltpu.VMEM((rows, B), F32),
                pltpu.VMEM((2 * B, B), F32),
                pltpu.VMEM((rows, B), F32),
                pltpu.VMEM((rows, cols - B), F32),
                pltpu.VMEM((2 * B, cols - B), BF16),
                pltpu.VMEM((2 * B, cols - B), BF16),
                pltpu.VMEM(front.shape, F32),
                pltpu.SemaphoreType.DMA((12,)),
            ],
            cost_estimate=pl.CostEstimate(flops=4 * 10**9, bytes_accessed=8 * 10**6, transcendentals=0),
            **ALONE,
        )(place, *arrays)

    def add_up(payload, flat, own, active, place, *arrays):
        matrix, pivots = call(
            assemble_kernel, (shaped(rows, cols), shaped(2 * B, cols)), 3, scalars=0, flops=4 * 10**9, moved=8 * 10**6
        )(payload, flat, own)
        r_own = matrix[:, :B]
        r_other = core_swap(r_own)
        share = lax.all_to_all(pivots, "prow", 0, 0, tiled=True).reshape(-1, share_rows, cols).sum(axis=0)
        pivots = lax.all_to_all(jnp.tile(share, (lax.axis_size("prow"), 1)), "prow", 0, 0, tiled=True)
        w_own = pivots[:, :B]
        w_other = core_swap(w_own)
        half, tile = call(
            panel_kernel, (shaped(rows, B), shaped(rows, B)), 6, flops=2 * 10**9, moved=4 * 10**6
        )(place, w_own, w_other, r_own, r_other, active)
        n_own = spread_z(half, place[1] // 2)
        n_other = core_swap(n_own)
        out = call(update_kernel, shaped(rows, cols), 6, flops=2 * 10**9, moved=8 * 10**6)(
            place, matrix, pivots, n_own, n_other, tile
        )
        return out.reshape(front.shape)

    return lax.cond(
        fits[0] == 1,
        finish,
        add_up,
        payload,
        flat,
        own,
        active,
        place,
        n_early,
        n_late,
        o_early,
        o_late,
        first,
        w_first,
        tile,
        rest,
        w_high,
        w_low,
    )


def solution(mesh):
    placed = (
        P(None, "prow", None, "pcol"),
        P(("prow", "pcol"), None, None, None),
        P(("prow", "pcol"), None, None),
        P(("prow", "pcol"), None),
        P(),
        P(),
        P(),
    )
    return jax.shard_map(
        body, mesh=mesh, in_specs=placed, out_specs=P(None, "prow", None, "pcol"), check_vma=False
    )
```

```python
import functools

import jax
import jax.numpy as jnp
from jax import lax
from jax.experimental import pallas as pl
from jax.experimental.pallas import tpu as pltpu
from jax.sharding import PartitionSpec as P

F32 = jnp.float32
BF16 = jnp.bfloat16
VM = pl.BlockSpec(memory_space=pltpu.VMEM)
HBM = pl.BlockSpec(memory_space=pltpu.HBM)
SM = pl.BlockSpec(memory_space=pltpu.SMEM)
B = 256
KEEP = 48
PARAMS = dict(compiler_params=pltpu.CompilerParams(vmem_limit_bytes=14 * 1024 * 1024))

ALONE = dict(compiler_params=pltpu.CompilerParams(vmem_limit_bytes=63 * 1024 * 1024))


def iota(shape, dim):
    return lax.broadcasted_iota(jnp.int32, shape, dim)


def dot(a, b):
    return jnp.dot(a, b, preferred_element_type=F32)


def halves(x):
    high = x.astype(BF16)
    return high, (x - high.astype(F32)).astype(BF16)


def dot3(a, b):
    ah, al = a
    bh, bl = b
    return dot(ah, bh) + (dot(ah, bl) + dot(al, bh))


def pick(onehot, x):
    high, low = halves(x)
    return dot(onehot, high) + dot(onehot, low)


def lookup(table, d, pos):
    n = pos.shape[1]
    hot = (iota((B, n), 0) == pos).astype(F32).astype(BF16)
    high = table // 256
    low = table - high * 256
    both = jnp.concatenate([high, low], axis=0).astype(F32).astype(BF16)
    got = dot(both, hot).astype(jnp.int32)
    rows = table.shape[0]
    values = got[:rows] * 256 + got[rows:]
    return jnp.sum(jnp.where(iota((rows, n), 0) == d, values, 0), axis=0, keepdims=True)


def turn(apart):
    apart = apart & 3
    return jnp.where(apart == 0, 0, jnp.where(apart == 1, 2, jnp.where(apart == 2, 3, 1)))


def index_kernel(place, local_picks, level_picks, order, own_out, active_out, give_out, slot_out, xy_out, fits_out):
    rows = active_out.shape[1]
    keep = give_out.shape[0]
    p = place[0]
    retired = jnp.zeros((rows, 1), F32)
    owners, locals_ = [], []
    for k in range(order.shape[0]):
        pos = order[k : k + 1, :]
        d = jnp.zeros_like(pos)
        for level in range(level_picks.shape[1] - 1, -1, -1):
            j = lookup(level_picks[k, level], d, pos)
            bit = 1 << level
            d = (d & ~bit) | jnp.where(j >= B, bit, 0)
            pos = j & (B - 1)
        r = lookup(local_picks[k], d, pos)
        own = jnp.where(d == p, r, -1)
        own_out[k * B : (k + 1) * B, :] = jnp.broadcast_to(own, (128, B)).T
        hit = (iota((rows, B), 0) == own).astype(F32)
        retired = jnp.maximum(retired, jnp.max(hit, axis=1, keepdims=True))
        active_out[k] = jnp.broadcast_to(1.0 - retired, (rows, 128))
        owners.append(d)
        locals_.append(r)
    d = jnp.concatenate(owners, axis=1)
    r = jnp.concatenate(locals_, axis=1)
    n = d.shape[1]
    d_col = jnp.broadcast_to(d, (128, n)).T[:, 0:1]
    before = (d_col == d) & (iota((n, n), 0) < iota((n, n), 1))
    rank = jnp.sum(before.astype(jnp.int32), axis=0, keepdims=True)
    fits_out[0] = (jnp.max(rank) < keep).astype(jnp.int32)
    slot_out[...] = jnp.broadcast_to(d * keep + rank, (128, n)).T
    across = turn(d - p)
    down = turn((d >> 2) - (p >> 2))
    xy_out[...] = jnp.broadcast_to((down * 4 + across) * keep + rank, (128, n)).T
    mine = (iota((keep, n), 0) == rank) & (d == p)
    give = jnp.sum(jnp.where(mine, r + 2, 0), axis=1, keepdims=True) - 2
    give_out[...] = jnp.broadcast_to(give, (keep, 128))


def pack_kernel(place, partials_hbm, targets_hbm, counts_hbm, out, partials, targets, counts, sems):
    slots, sources = targets.shape
    parts = sems.shape[0] - 2
    step = sources // parts
    small = [
        pltpu.make_async_copy(targets_hbm, targets, sems.at[parts]),
        pltpu.make_async_copy(counts_hbm, counts, sems.at[parts + 1]),
    ]
    large = [
        pltpu.make_async_copy(
            partials_hbm.at[i * step : (i + 1) * step], partials.at[i * step : (i + 1) * step], sems.at[i]
        )
        for i in range(parts)
    ]
    for copy in small + large:
        copy.start()
    for copy in small:
        copy.wait()
    codes = jnp.where(iota((slots, sources), 0) < counts[...], targets[...], -1)
    codes = jnp.concatenate([codes] * (128 // slots), axis=0)
    codes = jnp.where(iota(codes.shape, 0) // slots == place[2] % (128 // slots), codes, 0)
    row = codes.astype(F32).T
    for i in range(parts):
        large[i].wait()
        for s in range(i * step, (i + 1) * step):
            out[17 * s : 17 * s + 8, :] = partials[s, :, :128]
            out[17 * s + 8 : 17 * s + 16, :] = partials[s, :, 128:]
            out[17 * s + 16 : 17 * s + 17, :] = row[s : s + 1, :]


def unpack(payload):
    sources = payload.shape[0] // 17
    left, right, codes = [], [], []
    for g in range(sources // 16):
        row = jnp.zeros((1, 128), F32)
        for s in range(16 * g, 16 * g + 16):
            left.append(payload[17 * s : 17 * s + 8, :])
            right.append(payload[17 * s + 8 : 17 * s + 16, :])
            row = row + payload[17 * s + 16 : 17 * s + 17, :]
        codes.append(row)
    values = jnp.concatenate([jnp.concatenate(left, axis=0), jnp.concatenate(right, axis=0)], axis=1)
    return halves(values), jnp.concatenate(codes, axis=1).astype(jnp.int32)


def hot_of(code, rows, u):
    return (code == iota((rows, code.shape[1]), 0) * 4 + u).astype(F32).astype(BF16)


def rows_hot(chosen, rows):
    return (chosen[:, 0:1] == iota((chosen.shape[0], rows), 1)).astype(F32).astype(BF16)


def assemble_kernel(payload, front, own, matrix_out, pivots_out):
    (high, low), code = unpack(payload)
    rows = front.shape[0]
    pivot_hot = rows_hot(own, rows)
    for u in range(4):
        cols = slice(u * B, (u + 1) * B)
        hot = hot_of(code, rows, u)
        tile = front[:, cols] + (dot(hot, high) + dot(hot, low))
        matrix_out[:, cols] = tile
        pivots_out[:, cols] = pick(pivot_hot, tile)


def front_kernel(front, give, out):
    keep = give.shape[0]
    hot = rows_hot(give, front.shape[0])
    for u in range(4):
        out[u * keep : (u + 1) * keep, :] = pick(hot, front[:, u * B : (u + 1) * B])


def lead_kernel(payload, front_rows, give, send_first, send_rest):
    (high, low), code = unpack(payload)
    keep = give.shape[0]
    chosen = give[:, 0:1] * 4
    hot = jnp.concatenate([(chosen + u == code).astype(F32) for u in range(4)], axis=0).astype(BF16)
    sums = front_rows[...] + (dot(hot, high) + dot(hot, low))
    for i in range(send_first.shape[0] // keep):
        send_first[i * keep : (i + 1) * keep, :] = sums[:keep]
    for u in range(1, 4):
        send_rest[:, (u - 1) * B : u * B] = sums[u * keep : (u + 1) * keep]


def tiles_kernel(payload, front, first_out, rest_out):
    (high, low), code = unpack(payload)
    for u in range(4):
        hot = hot_of(code, front.shape[0], u)
        tile = front[:, u * B : (u + 1) * B] + (dot(hot, high) + dot(hot, low))
        if u == 0:
            first_out[...] = tile
        else:
            rest_out[:, (u - 1) * B : u * B] = tile


def join_kernel(a0, a1, a2, a3, out):
    size = a0.shape[0]
    for i, a in enumerate((a0, a1, a2, a3)):
        out[i * size : (i + 1) * size, :] = a[...]


def sort_first_kernel(slot, gathered, out):
    out[...] = pick(rows_hot(slot, gathered.shape[0]), gathered[...])


def inverse_of(diag):
    eye = iota((B, B), 0) == iota((B, B), 1)
    only = jnp.where(eye, diag, 0.0)
    by_row = 1.0 / jnp.sum(only, axis=1, keepdims=True)
    by_col = 1.0 / jnp.sum(only, axis=0, keepdims=True)
    two = jnp.where(eye, 2.0, 0.0)
    x = by_row * (two - diag * by_col)
    xs = halves(x)
    return dot3(xs, halves(two - dot3(halves(diag), xs)))


def panel_kernel(place, w_own, w_other, r_own, r_other, active, half_out, tile_out):
    even = place[1] % 2 == 0
    w0 = jnp.where(even, w_own[...], w_other[...])
    w1 = jnp.where(even, w_other[...], w_own[...])
    r0 = jnp.where(even, r_own[...], r_other[...])
    r1 = jnp.where(even, r_other[...], r_own[...])
    act0 = active[0][:, 0:1]
    act1 = active[1][:, 0:1]
    inv0 = halves(inverse_of(w0[:B]))
    m0w = dot3(halves(w0[B:]), inv0)
    m0w_s = halves(m0w)
    p01 = halves(w1[:B])
    inv1 = halves(inverse_of(w1[B:] - dot3(m0w_s, p01)))
    m0 = dot3(halves(r0), inv0)
    m0a = jnp.where(act0 > 0, m0, 0.0)
    r1 = r1 - dot3(halves(m0a), p01)
    m1 = dot3(halves(r1), inv1)
    n1 = jnp.where(act1 > 0, m1, 0.0)
    n0 = m0a - dot3(halves(n1), m0w_s)
    half_out[...] = jnp.where(even, n0, n1)
    tile_out[...] = jnp.where(even, jnp.where(act0 > 0, m0, r0), jnp.where(act1 > 0, m1, r1))


def update_kernel(place, matrix, pivots, n_own, n_other, tile, out):
    even = place[1] % 2 == 0
    n0 = halves(jnp.where(even, n_own[...], n_other[...]))
    n1 = halves(jnp.where(even, n_other[...], n_own[...]))
    for u in range(4):
        cols = slice(u * B, (u + 1) * B)
        new = matrix[:, cols] - (
            dot3(n0, halves(pivots[:B, cols])) + dot3(n1, halves(pivots[B:, cols]))
        )
        if u == 0:
            new = jnp.where(place[1] < 2, tile[...], new)
        out[:, cols] = new


def finish_kernel(
    place, n_early, n_late, o_early, o_late, first_hbm, w_first_hbm, tile_hbm, rest_hbm, xy_hbm, a0, a1, a2, a3, out_hbm,
    n_own, n_other, first, w_first, tile, rest, xy, w_rest, out, sems
):
    q = place[1]
    even = q % 2 == 0
    own_early = (q < 3) | (q == 7)
    other_early = (q < 2) | (q == 3) | (q == 6)
    copy = pltpu.make_async_copy

    @pl.when(own_early)
    def _():
        copy(n_early, n_own, sems.at[0]).start()

    @pl.when(jnp.logical_not(own_early))
    def _():
        copy(n_late, n_own, sems.at[0]).start()

    @pl.when(other_early)
    def _():
        copy(o_early, n_other, sems.at[1]).start()

    @pl.when(jnp.logical_not(other_early))
    def _():
        copy(o_late, n_other, sems.at[1]).start()

    size = a0.shape[0]
    moves = [
        copy(xy_hbm, xy, sems.at[2]),
        copy(w_first_hbm, w_first, sems.at[3]),
        copy(first_hbm, first, sems.at[4]),
        copy(tile_hbm, tile, sems.at[5]),
        copy(a0, w_rest.at[:size], sems.at[6]),
        copy(a1, w_rest.at[size : 2 * size], sems.at[7]),
        copy(a2, w_rest.at[2 * size : 3 * size], sems.at[8]),
        copy(a3, w_rest.at[3 * size :], sems.at[9]),
        copy(rest_hbm, rest, sems.at[10]),
    ]
    for move in moves:
        move.start()
    copy(n_early, n_own, sems.at[0]).wait()
    copy(o_early, n_other, sems.at[1]).wait()
    h0, l0 = halves(jnp.where(even, n_own[...], n_other[...]))
    h1, l1 = halves(jnp.where(even, n_other[...], n_own[...]))
    rows = first.shape[0]
    half = out.shape[1]
    block = half // 2
    moves[0].wait()
    n_high = jnp.concatenate([h0, h1], axis=1)
    n_low = jnp.concatenate([l0, l1], axis=1)
    hot = rows_hot(xy, w_rest.shape[0])
    high = dot(n_high, hot).astype(BF16)
    low = dot(n_low, hot).astype(BF16)
    for move in moves[1:4]:
        move.wait()
    new = first[...] - dot3((n_high, n_low), halves(w_first[...]))
    new = jnp.where(q < 2, tile[...], new)
    for t in range(rows // half):
        out[t, :, 0, :] = new[t * half : (t + 1) * half]
    for move in moves[4:]:
        move.wait()
    w = [halves(w_rest[:, u * B : (u + 1) * B]) for u in range(3)]
    sent = []
    for i in range(rows // block):
        t, at = i * block // half, i * block % half
        span = slice(i * block, (i + 1) * block)
        for u in range(1, 4):
            cols = slice((u - 1) * B, u * B)
            out[t, at : at + block, u, :] = rest[span, cols] - dot3((high[span], low[span]), w[u - 1])
        done = copy(out.at[t, at : at + block], out_hbm.at[t, at : at + block], sems.at[11 + i])
        done.start()
        sent.append(done)
    for done in sent:
        done.wait()


def call(kernel, outs, n_in, scalars=1, outs_in_smem=0, flops=0, moved=0):
    specs = jax.tree.map(lambda _: VM, outs)
    if outs_in_smem:
        specs = specs[:-outs_in_smem] + (SM,) * outs_in_smem
    return pl.pallas_call(
        kernel,
        out_shape=outs,
        in_specs=[SM] * scalars + [VM] * (n_in - scalars),
        out_specs=specs,
        cost_estimate=pl.CostEstimate(flops=flops, bytes_accessed=moved, transcendentals=0),
        **PARAMS,
    )


def shaped(*shape, dtype=F32):
    return jax.ShapeDtypeStruct(shape, dtype)


def core_swap(x):
    return lax.ppermute(x, "pcol", [(i, i ^ 1) for i in range(lax.axis_size("pcol"))])


def shift_x(step):
    return [(p, p // 4 * 4 + (p + step) % 4) for p in range(16)]


def shift_y(step):
    return [(p, (p + 4 * step) % 16) for p in range(16)]


def ring(x, shift):
    return [x] + [lax.ppermute(x, "prow", shift(step)) for step in (1, -1, 2)]


def spread_z(x, z):
    one = lax.ppermute(x, "pcol", [(0, 2), (1, 3)])
    three = lax.ppermute(x, "pcol", [(0, 6), (1, 7)])
    two = lax.ppermute(x, "pcol", [(0, 4), (1, 5)])
    return jnp.where(z == 0, x, jnp.where(z == 1, one, jnp.where(z == 2, two, three)))


def body(front, partials, targets, counts, local_picks, level_picks, order):
    rows = front.shape[0] * front.shape[1]
    cols = front.shape[2] * front.shape[3]
    p = lax.axis_index("prow")
    q = lax.axis_index("pcol")
    me = p * lax.axis_size("pcol") + q
    place = jnp.stack([p, q, me]).astype(jnp.int32)
    sources = partials.shape[1]
    slots = partials.shape[2]

    payload = pl.pallas_call(
        pack_kernel,
        out_shape=shaped(sources * 17, 128),
        in_specs=[SM, HBM, HBM, HBM],
        out_specs=VM,
        scratch_shapes=[
            pltpu.VMEM((sources, slots, B), F32),
            pltpu.VMEM((slots, sources), jnp.int32),
            pltpu.VMEM((1, sources), jnp.int32),
            pltpu.SemaphoreType.DMA((6,)),
        ],
        cost_estimate=pl.CostEstimate(flops=10**6, bytes_accessed=2 * 10**6, transcendentals=0),
        **ALONE,
    )(place, partials[0], targets[0].T, counts).reshape(sources * 17, 1, 128)
    payload = lax.all_to_all(payload, ("prow", "pcol"), 0, 0, tiled=True).reshape(sources * 17, 128)

    lists = shaped(2 * B, 128, dtype=jnp.int32)
    own, active, give, slot, xy, fits = call(
        index_kernel,
        (
            lists,
            shaped(2, rows, 128),
            shaped(KEEP, 128, dtype=jnp.int32),
            lists,
            lists,
            shaped(1, dtype=jnp.int32),
        ),
        4,
        outs_in_smem=1,
        flops=10**9,
        moved=10**6,
    )(place, local_picks, level_picks, order)
    front, own = lax.optimization_barrier((front, own))
    flat = front.reshape(rows, cols)
    copies = lax.axis_size("prow") * KEEP
    share_rows = 2 * B // lax.axis_size("prow")

    front_rows = call(front_kernel, shaped(4 * KEEP, B), 2, scalars=0, flops=10**8, moved=3 * 10**6)(flat, give)

    send_first, send_rest = call(
        lead_kernel, (shaped(copies, B), shaped(KEEP, cols - B)), 3, scalars=0, flops=10**8, moved=2 * 10**6
    )(payload, front_rows, give)
    w_first = lax.all_to_all(send_first, "prow", 0, 0, tiled=True)
    joined = call(join_kernel, shaped(4 * KEEP, cols - B), 4, scalars=0, moved=10**6)(*ring(send_rest, shift_x))
    w_parts = ring(joined, shift_y)
    first, rest = call(
        tiles_kernel, (shaped(rows, B), shaped(rows, cols - B)), 2, scalars=0, flops=4 * 10**9, moved=6 * 10**6
    )(payload, flat)

    def panels(w_first, first, slot, active, place, joined):
        r_other = core_swap(first)
        w_first = call(sort_first_kernel, shaped(2 * B, B), 2, scalars=0, flops=10**8, moved=10**6)(slot, w_first)
        w_other = core_swap(w_first)
        half, tile = call(
            panel_kernel, (shaped(rows, B), shaped(rows, B)), 6, flops=2 * 10**9, moved=4 * 10**6
        )(place, w_first, w_other, first, r_other, active)
        q = place[1]
        step = lax.ppermute(half, "pcol", [(0, 2), (1, 7)])
        n_early = jnp.where((q == 2) | (q == 7), step, half)
        n_late = lax.ppermute(n_early, "pcol", [(1, 3), (0, 6), (2, 4), (7, 5)])
        o_early = lax.ppermute(n_early, "pcol", [(0, 1), (1, 0), (2, 3), (7, 6)])
        o_late = lax.ppermute(n_late, "pcol", [(3, 2), (6, 7), (4, 5), (5, 4)])
        return n_early, n_late, o_early, o_late, w_first, tile

    def nothing(w_first, first, slot, active, place, joined):
        square = jnp.zeros((rows, B), F32)
        return square, square, square, square, jnp.zeros((2 * B, B), F32), square

    n_early, n_late, o_early, o_late, w_first, tile = lax.cond(
        fits[0] == 1, panels, nothing, w_first, first, slot, active, place, joined
    )

    def finish(payload, flat, own, active, place, *arrays):
        return pl.pallas_call(
            finish_kernel,
            out_shape=shaped(*front.shape),
            in_specs=[SM] + [HBM] * 13,
            out_specs=HBM,
            scratch_shapes=[
                pltpu.VMEM((rows, B), F32),
                pltpu.VMEM((rows, B), F32),
                pltpu.VMEM((rows, B), F32),
                pltpu.VMEM((2 * B, B), F32),
                pltpu.VMEM((rows, B), F32),
                pltpu.VMEM((rows, cols - B), F32),
                pltpu.VMEM((2 * B, 128), jnp.int32),
                pltpu.VMEM((copies, cols - B), F32),
                pltpu.VMEM(front.shape, F32),
                pltpu.SemaphoreType.DMA((15,)),
            ],
            cost_estimate=pl.CostEstimate(flops=4 * 10**9, bytes_accessed=8 * 10**6, transcendentals=0),
            **ALONE,
        )(place, *arrays)

    def add_up(payload, flat, own, active, place, *arrays):
        matrix, pivots = call(
            assemble_kernel, (shaped(rows, cols), shaped(2 * B, cols)), 3, scalars=0, flops=4 * 10**9, moved=8 * 10**6
        )(payload, flat, own)
        r_own = matrix[:, :B]
        r_other = core_swap(r_own)
        share = lax.all_to_all(pivots, "prow", 0, 0, tiled=True).reshape(-1, share_rows, cols).sum(axis=0)
        pivots = lax.all_to_all(jnp.tile(share, (lax.axis_size("prow"), 1)), "prow", 0, 0, tiled=True)
        w_own = pivots[:, :B]
        w_other = core_swap(w_own)
        half, tile = call(
            panel_kernel, (shaped(rows, B), shaped(rows, B)), 6, flops=2 * 10**9, moved=4 * 10**6
        )(place, w_own, w_other, r_own, r_other, active)
        n_own = spread_z(half, place[1] // 2)
        n_other = core_swap(n_own)
        out = call(update_kernel, shaped(rows, cols), 6, flops=2 * 10**9, moved=8 * 10**6)(
            place, matrix, pivots, n_own, n_other, tile
        )
        return out.reshape(front.shape)

    return lax.cond(
        fits[0] == 1,
        finish,
        add_up,
        payload,
        flat,
        own,
        active,
        place,
        n_early,
        n_late,
        o_early,
        o_late,
        first,
        w_first,
        tile,
        rest,
        xy,
        *w_parts,
    )


def solution(mesh):
    placed = (
        P(None, "prow", None, "pcol"),
        P(("prow", "pcol"), None, None, None),
        P(("prow", "pcol"), None, None),
        P(("prow", "pcol"), None),
        P(),
        P(),
        P(),
    )
    return jax.shard_map(
        body, mesh=mesh, in_specs=placed, out_specs=P(None, "prow", None, "pcol"), check_vma=False
    )
```

```python
import functools

import jax
import jax.numpy as jnp
from jax import lax
from jax.experimental import pallas as pl
from jax.experimental.pallas import tpu as pltpu
from jax.sharding import PartitionSpec as P

F32 = jnp.float32
BF16 = jnp.bfloat16
VM = pl.BlockSpec(memory_space=pltpu.VMEM)
HBM = pl.BlockSpec(memory_space=pltpu.HBM)
SM = pl.BlockSpec(memory_space=pltpu.SMEM)
B = 256
KEEP = 48
PARAMS = dict(compiler_params=pltpu.CompilerParams(vmem_limit_bytes=14 * 1024 * 1024))

ALONE = dict(compiler_params=pltpu.CompilerParams(vmem_limit_bytes=63 * 1024 * 1024))


def iota(shape, dim):
    return lax.broadcasted_iota(jnp.int32, shape, dim)


def dot(a, b):
    return jnp.dot(a, b, preferred_element_type=F32)


def halves(x):
    high = x.astype(BF16)
    return high, (x - high.astype(F32)).astype(BF16)


def dot3(a, b):
    ah, al = a
    bh, bl = b
    return dot(ah, bh) + (dot(ah, bl) + dot(al, bh))


def pick(onehot, x):
    high, low = halves(x)
    return dot(onehot, high) + dot(onehot, low)


def lookup(table, d, pos):
    n = pos.shape[1]
    hot = (iota((B, n), 0) == pos).astype(F32).astype(BF16)
    high = table // 256
    low = table - high * 256
    both = jnp.concatenate([high, low], axis=0).astype(F32).astype(BF16)
    got = dot(both, hot).astype(jnp.int32)
    rows = table.shape[0]
    values = got[:rows] * 256 + got[rows:]
    return jnp.sum(jnp.where(iota((rows, n), 0) == d, values, 0), axis=0, keepdims=True)


def turn(apart):
    apart = apart & 3
    return jnp.where(apart == 0, 0, jnp.where(apart == 1, 2, jnp.where(apart == 2, 3, 1)))


def index_kernel(place, local_picks, level_picks, order, own_out, active_out, give_out, slot_out, xy_out, fits_out):
    rows = active_out.shape[1]
    keep = give_out.shape[0]
    p = place[0]
    retired = jnp.zeros((rows, 1), F32)
    owners, locals_ = [], []
    for k in range(order.shape[0]):
        pos = order[k : k + 1, :]
        d = jnp.zeros_like(pos)
        for level in range(level_picks.shape[1] - 1, -1, -1):
            j = lookup(level_picks[k, level], d, pos)
            bit = 1 << level
            d = (d & ~bit) | jnp.where(j >= B, bit, 0)
            pos = j & (B - 1)
        r = lookup(local_picks[k], d, pos)
        own = jnp.where(d == p, r, -1)
        own_out[k * B : (k + 1) * B, :] = jnp.broadcast_to(own, (128, B)).T
        hit = (iota((rows, B), 0) == own).astype(F32)
        retired = jnp.maximum(retired, jnp.max(hit, axis=1, keepdims=True))
        active_out[k] = jnp.broadcast_to(1.0 - retired, (rows, 128))
        owners.append(d)
        locals_.append(r)
    d = jnp.concatenate(owners, axis=1)
    r = jnp.concatenate(locals_, axis=1)
    n = d.shape[1]
    d_col = jnp.broadcast_to(d, (128, n)).T[:, 0:1]
    before = (d_col == d) & (iota((n, n), 0) < iota((n, n), 1))
    rank = jnp.sum(before.astype(jnp.int32), axis=0, keepdims=True)
    fits_out[0] = (jnp.max(rank) < keep).astype(jnp.int32)
    slot_out[...] = rows_hot(jnp.broadcast_to(d * keep + rank, (128, n)).T, slot_out.shape[1])
    across = turn(d - p)
    down = turn((d >> 2) - (p >> 2))
    xy_out[...] = rows_hot(jnp.broadcast_to((down * 4 + across) * keep + rank, (128, n)).T, xy_out.shape[1])
    mine = (iota((keep, n), 0) == rank) & (d == p)
    give = jnp.sum(jnp.where(mine, r + 2, 0), axis=1, keepdims=True) - 2
    give_out[...] = jnp.broadcast_to(give, (keep, 128))


def pack_kernel(place, partials_hbm, targets_hbm, counts_hbm, out, partials, targets, counts, sems):
    slots, sources = targets.shape
    parts = sems.shape[0] - 2
    step = sources // parts
    small = [
        pltpu.make_async_copy(targets_hbm, targets, sems.at[parts]),
        pltpu.make_async_copy(counts_hbm, counts, sems.at[parts + 1]),
    ]
    large = [
        pltpu.make_async_copy(
            partials_hbm.at[i * step : (i + 1) * step], partials.at[i * step : (i + 1) * step], sems.at[i]
        )
        for i in range(parts)
    ]
    for copy in small + large:
        copy.start()
    for copy in small:
        copy.wait()
    codes = jnp.where(iota((slots, sources), 0) < counts[...], targets[...], -1)
    codes = jnp.concatenate([codes] * (128 // slots), axis=0)
    codes = jnp.where(iota(codes.shape, 0) // slots == place[2] % (128 // slots), codes, 0)
    row = codes.astype(F32).T
    for i in range(parts):
        large[i].wait()
        for s in range(i * step, (i + 1) * step):
            out[17 * s : 17 * s + 8, :] = partials[s, :, :128]
            out[17 * s + 8 : 17 * s + 16, :] = partials[s, :, 128:]
            out[17 * s + 16 : 17 * s + 17, :] = row[s : s + 1, :]


def unpack(payload):
    sources = payload.shape[0] // 17
    left, right, codes = [], [], []
    for g in range(sources // 16):
        row = jnp.zeros((1, 128), F32)
        for s in range(16 * g, 16 * g + 16):
            left.append(payload[17 * s : 17 * s + 8, :])
            right.append(payload[17 * s + 8 : 17 * s + 16, :])
            row = row + payload[17 * s + 16 : 17 * s + 17, :]
        codes.append(row)
    values = jnp.concatenate([jnp.concatenate(left, axis=0), jnp.concatenate(right, axis=0)], axis=1)
    return halves(values), jnp.concatenate(codes, axis=1).astype(jnp.int32)


def hot_of(code, rows, u):
    return (code == iota((rows, code.shape[1]), 0) * 4 + u).astype(F32).astype(BF16)


def rows_hot(chosen, rows):
    return (chosen[:, 0:1] == iota((chosen.shape[0], rows), 1)).astype(F32).astype(BF16)


def assemble_kernel(payload, front, own, matrix_out, pivots_out):
    (high, low), code = unpack(payload)
    rows = front.shape[0]
    pivot_hot = rows_hot(own, rows)
    for u in range(4):
        cols = slice(u * B, (u + 1) * B)
        hot = hot_of(code, rows, u)
        tile = front[:, cols] + (dot(hot, high) + dot(hot, low))
        matrix_out[:, cols] = tile
        pivots_out[:, cols] = pick(pivot_hot, tile)


def front_kernel(front, give, out):
    keep = give.shape[0]
    hot = rows_hot(give, front.shape[0])
    for u in range(4):
        out[u * keep : (u + 1) * keep, :] = pick(hot, front[:, u * B : (u + 1) * B])


def lead_kernel(payload, front_rows, give, send_first, send_rest):
    (high, low), code = unpack(payload)
    keep = give.shape[0]
    chosen = give[:, 0:1] * 4
    hot = jnp.concatenate([(chosen + u == code).astype(F32) for u in range(4)], axis=0).astype(BF16)
    sums = front_rows[...] + (dot(hot, high) + dot(hot, low))
    for i in range(send_first.shape[0] // keep):
        send_first[i * keep : (i + 1) * keep, :] = sums[:keep]
    for u in range(1, 4):
        send_rest[:, (u - 1) * B : u * B] = sums[u * keep : (u + 1) * keep]


def tiles_kernel(payload, front, first_out, rest_out, done_out):
    done_out[...] = jnp.zeros_like(done_out)
    (high, low), code = unpack(payload)
    for u in range(4):
        hot = hot_of(code, front.shape[0], u)
        tile = front[:, u * B : (u + 1) * B] + (dot(hot, high) + dot(hot, low))
        if u == 0:
            first_out[...] = tile
        else:
            rest_out[:, (u - 1) * B : u * B] = tile


def join_kernel(done, a0, a1, a2, a3, out):
    size = a0.shape[0]
    for i, a in enumerate((a0, a1, a2, a3)):
        out[i * size : (i + 1) * size, :] = a[...]


def sort_first_kernel(slot, gathered, out):
    out[...] = pick(slot[...], gathered[...])


def inverse_of(diag):
    eye = iota((B, B), 0) == iota((B, B), 1)
    only = jnp.where(eye, diag, 0.0)
    by_row = 1.0 / jnp.sum(only, axis=1, keepdims=True)
    by_col = 1.0 / jnp.sum(only, axis=0, keepdims=True)
    two = jnp.where(eye, 2.0, 0.0)
    x = by_row * (two - diag * by_col)
    xs = halves(x)
    return dot3(xs, halves(two - dot3(halves(diag), xs)))


def panel_kernel(place, w_own, w_other, r_own, r_other, active, half_out, tile_out):
    even = place[1] % 2 == 0
    w0 = jnp.where(even, w_own[...], w_other[...])
    w1 = jnp.where(even, w_other[...], w_own[...])
    r0 = jnp.where(even, r_own[...], r_other[...])
    r1 = jnp.where(even, r_other[...], r_own[...])
    act0 = active[0][:, 0:1]
    act1 = active[1][:, 0:1]
    inv0 = halves(inverse_of(w0[:B]))
    m0w = dot3(halves(w0[B:]), inv0)
    m0w_s = halves(m0w)
    p01 = halves(w1[:B])
    inv1 = halves(inverse_of(w1[B:] - dot3(m0w_s, p01)))
    m0 = dot3(halves(r0), inv0)
    m0a = jnp.where(act0 > 0, m0, 0.0)
    r1 = r1 - dot3(halves(m0a), p01)
    m1 = dot3(halves(r1), inv1)
    n1 = jnp.where(act1 > 0, m1, 0.0)
    n0 = m0a - dot3(halves(n1), m0w_s)
    half_out[...] = jnp.where(even, n0, n1)
    tile_out[...] = jnp.where(even, jnp.where(act0 > 0, m0, r0), jnp.where(act1 > 0, m1, r1))


def update_kernel(place, matrix, pivots, n_own, n_other, tile, out):
    even = place[1] % 2 == 0
    n0 = halves(jnp.where(even, n_own[...], n_other[...]))
    n1 = halves(jnp.where(even, n_other[...], n_own[...]))
    for u in range(4):
        cols = slice(u * B, (u + 1) * B)
        new = matrix[:, cols] - (
            dot3(n0, halves(pivots[:B, cols])) + dot3(n1, halves(pivots[B:, cols]))
        )
        if u == 0:
            new = jnp.where(place[1] < 2, tile[...], new)
        out[:, cols] = new


def finish_kernel(
    place, n_early, n_last, o_early, o_last, tile_hbm, first_hbm, w_first_hbm, rest_hbm, xy_hbm,
    a0, a1, a2, a3, out_hbm, n_own, n_other, first, w_first, tile, rest, xy, w_rest, out, sems
):
    q = place[1]
    even = q % 2 == 0
    far = (q == 4) | (q == 5)
    copy = pltpu.make_async_copy

    @pl.when(far)
    def _():
        copy(n_last, n_own, sems.at[0]).start()
        copy(o_last, n_other, sems.at[1]).start()

    @pl.when(jnp.logical_not(far))
    def _():
        copy(n_early, n_own, sems.at[0]).start()
        copy(o_early, n_other, sems.at[1]).start()

    size = a0.shape[0]
    moves = [
        copy(xy_hbm, xy, sems.at[2]),
        copy(w_first_hbm, w_first, sems.at[3]),
        copy(first_hbm, first, sems.at[4]),
        copy(tile_hbm, tile, sems.at[5]),
        copy(a0, w_rest.at[:size], sems.at[6]),
        copy(a1, w_rest.at[size : 2 * size], sems.at[7]),
        copy(a2, w_rest.at[2 * size : 3 * size], sems.at[8]),
        copy(a3, w_rest.at[3 * size :], sems.at[9]),
        copy(rest_hbm, rest, sems.at[10]),
    ]
    for move in moves:
        move.start()
    copy(n_early, n_own, sems.at[0]).wait()
    copy(o_early, n_other, sems.at[1]).wait()
    h0, l0 = halves(jnp.where(even, n_own[...], n_other[...]))
    h1, l1 = halves(jnp.where(even, n_other[...], n_own[...]))
    rows = first.shape[0]
    half = out.shape[1]
    block = half // 2
    moves[0].wait()
    n_high = jnp.concatenate([h0, h1], axis=1)
    n_low = jnp.concatenate([l0, l1], axis=1)
    hot = xy[...]
    high = dot(n_high, hot).astype(BF16)
    low = dot(n_low, hot).astype(BF16)
    for move in moves[1:4]:
        move.wait()
    new = first[...] - dot3((n_high, n_low), halves(w_first[...]))
    new = jnp.where(q < 2, tile[...], new)
    for t in range(rows // half):
        out[t, :, 0, :] = new[t * half : (t + 1) * half]
    for move in moves[4:]:
        move.wait()
    w = [halves(w_rest[:, u * B : (u + 1) * B]) for u in range(3)]
    sent = []
    for i in range(rows // block):
        t, at = i * block // half, i * block % half
        span = slice(i * block, (i + 1) * block)
        for u in range(1, 4):
            cols = slice((u - 1) * B, u * B)
            out[t, at : at + block, u, :] = rest[span, cols] - dot3((high[span], low[span]), w[u - 1])
        done = copy(out.at[t, at : at + block], out_hbm.at[t, at : at + block], sems.at[11 + i])
        done.start()
        sent.append(done)
    for done in sent:
        done.wait()


def call(kernel, outs, n_in, scalars=1, outs_in_smem=0, flops=0, moved=0):
    specs = jax.tree.map(lambda _: VM, outs)
    if outs_in_smem:
        specs = specs[:-outs_in_smem] + (SM,) * outs_in_smem
    return pl.pallas_call(
        kernel,
        out_shape=outs,
        in_specs=[SM] * scalars + [VM] * (n_in - scalars),
        out_specs=specs,
        cost_estimate=pl.CostEstimate(flops=flops, bytes_accessed=moved, transcendentals=0),
        **PARAMS,
    )


def shaped(*shape, dtype=F32):
    return jax.ShapeDtypeStruct(shape, dtype)


def core_swap(x):
    return lax.ppermute(x, "pcol", [(i, i ^ 1) for i in range(lax.axis_size("pcol"))])


def shift_x(step):
    return [(p, p // 4 * 4 + (p + step) % 4) for p in range(16)]


def shift_y(step):
    return [(p, (p + 4 * step) % 16) for p in range(16)]


def ring(x, shift):
    return [x] + [lax.ppermute(x, "prow", shift(step)) for step in (1, -1, 2)]


def spread_z(x, z):
    one = lax.ppermute(x, "pcol", [(0, 2), (1, 3)])
    three = lax.ppermute(x, "pcol", [(0, 6), (1, 7)])
    two = lax.ppermute(x, "pcol", [(0, 4), (1, 5)])
    return jnp.where(z == 0, x, jnp.where(z == 1, one, jnp.where(z == 2, two, three)))


def body(front, partials, targets, counts, local_picks, level_picks, order):
    rows = front.shape[0] * front.shape[1]
    cols = front.shape[2] * front.shape[3]
    p = lax.axis_index("prow")
    q = lax.axis_index("pcol")
    me = p * lax.axis_size("pcol") + q
    place = jnp.stack([p, q, me]).astype(jnp.int32)
    sources = partials.shape[1]
    slots = partials.shape[2]

    payload = pl.pallas_call(
        pack_kernel,
        out_shape=shaped(sources * 17, 128),
        in_specs=[SM, HBM, HBM, HBM],
        out_specs=VM,
        scratch_shapes=[
            pltpu.VMEM((sources, slots, B), F32),
            pltpu.VMEM((slots, sources), jnp.int32),
            pltpu.VMEM((1, sources), jnp.int32),
            pltpu.SemaphoreType.DMA((6,)),
        ],
        cost_estimate=pl.CostEstimate(flops=10**6, bytes_accessed=2 * 10**6, transcendentals=0),
        **ALONE,
    )(place, partials[0], targets[0].T, counts).reshape(sources * 17, 1, 128)
    payload = lax.all_to_all(payload, ("prow", "pcol"), 0, 0, tiled=True).reshape(sources * 17, 128)

    copies = lax.axis_size("prow") * KEEP
    hots = shaped(2 * B, copies, dtype=BF16)
    own, active, give, slot, xy, fits = call(
        index_kernel,
        (
            shaped(2 * B, 128, dtype=jnp.int32),
            shaped(2, rows, 128),
            shaped(KEEP, 128, dtype=jnp.int32),
            hots,
            hots,
            shaped(1, dtype=jnp.int32),
        ),
        4,
        outs_in_smem=1,
        flops=10**9,
        moved=10**6,
    )(place, local_picks, level_picks, order)
    front, own = lax.optimization_barrier((front, own))
    flat = front.reshape(rows, cols)
    share_rows = 2 * B // lax.axis_size("prow")

    front_rows = call(front_kernel, shaped(4 * KEEP, B), 2, scalars=0, flops=10**8, moved=3 * 10**6)(flat, give)

    send_first, send_rest = call(
        lead_kernel, (shaped(copies, B), shaped(KEEP, cols - B)), 3, scalars=0, flops=10**8, moved=2 * 10**6
    )(payload, front_rows, give)
    w_first = lax.all_to_all(send_first, "prow", 0, 0, tiled=True)
    first, rest, done = call(
        tiles_kernel,
        (shaped(rows, B), shaped(rows, cols - B), shaped(8, 128)),
        2,
        scalars=0,
        flops=4 * 10**9,
        moved=6 * 10**6,
    )(payload, flat)
    joined = call(join_kernel, shaped(4 * KEEP, cols - B), 5, scalars=0, moved=10**6)(done, *ring(send_rest, shift_x))
    w_parts = ring(joined, shift_y)
    w_first = call(sort_first_kernel, shaped(2 * B, B), 2, scalars=0, flops=10**8, moved=10**6)(slot, w_first)

    def panels(w_first, first, active, place, joined):
        r_other = core_swap(first)
        w_other = core_swap(w_first)
        half, tile = call(
            panel_kernel, (shaped(rows, B), shaped(rows, B)), 6, flops=2 * 10**9, moved=4 * 10**6
        )(place, w_first, w_other, first, r_other, active)
        q = place[1]
        near = (q == 2) | (q == 7)
        side = (q == 3) | (q == 6)
        step = lax.ppermute(half, "pcol", [(0, 2), (1, 7)])
        late = lax.ppermute(half, "pcol", [(1, 3), (0, 6)])
        last = lax.ppermute(step, "pcol", [(2, 4), (7, 5)])
        early = jnp.where(side, late, jnp.where(near, step, half))
        o_early = lax.ppermute(early, "pcol", [(0, 1), (1, 0), (2, 3), (3, 2), (6, 7), (7, 6)])
        o_last = lax.ppermute(last, "pcol", [(4, 5), (5, 4)])
        return early, last, o_early, o_last, tile

    def nothing(w_first, first, active, place, joined):
        return (jnp.zeros((rows, B), F32),) * 5

    parts = lax.cond(fits[0] == 1, panels, nothing, w_first, first, active, place, joined)

    def finish(payload, flat, own, active, place, *arrays):
        return pl.pallas_call(
            finish_kernel,
            out_shape=shaped(*front.shape),
            in_specs=[SM] + [HBM] * 13,
            out_specs=HBM,
            scratch_shapes=[
                pltpu.VMEM((rows, B), F32),
                pltpu.VMEM((rows, B), F32),
                pltpu.VMEM((rows, B), F32),
                pltpu.VMEM((2 * B, B), F32),
                pltpu.VMEM((rows, B), F32),
                pltpu.VMEM((rows, cols - B), F32),
                pltpu.VMEM((2 * B, copies), BF16),
                pltpu.VMEM((copies, cols - B), F32),
                pltpu.VMEM(front.shape, F32),
                pltpu.SemaphoreType.DMA((15,)),
            ],
            cost_estimate=pl.CostEstimate(flops=4 * 10**9, bytes_accessed=8 * 10**6, transcendentals=0),
            **ALONE,
        )(place, *arrays)

    def add_up(payload, flat, own, active, place, *arrays):
        matrix, pivots = call(
            assemble_kernel, (shaped(rows, cols), shaped(2 * B, cols)), 3, scalars=0, flops=4 * 10**9, moved=8 * 10**6
        )(payload, flat, own)
        r_own = matrix[:, :B]
        r_other = core_swap(r_own)
        share = lax.all_to_all(pivots, "prow", 0, 0, tiled=True).reshape(-1, share_rows, cols).sum(axis=0)
        pivots = lax.all_to_all(jnp.tile(share, (lax.axis_size("prow"), 1)), "prow", 0, 0, tiled=True)
        w_own = pivots[:, :B]
        w_other = core_swap(w_own)
        half, tile = call(
            panel_kernel, (shaped(rows, B), shaped(rows, B)), 6, flops=2 * 10**9, moved=4 * 10**6
        )(place, w_own, w_other, r_own, r_other, active)
        n_own = spread_z(half, place[1] // 2)
        n_other = core_swap(n_own)
        out = call(update_kernel, shaped(rows, cols), 6, flops=2 * 10**9, moved=8 * 10**6)(
            place, matrix, pivots, n_own, n_other, tile
        )
        return out.reshape(front.shape)

    return lax.cond(
        fits[0] == 1,
        finish,
        add_up,
        payload,
        flat,
        own,
        active,
        place,
        *parts,
        first,
        w_first,
        rest,
        xy,
        *w_parts,
    )


def solution(mesh):
    placed = (
        P(None, "prow", None, "pcol"),
        P(("prow", "pcol"), None, None, None),
        P(("prow", "pcol"), None, None),
        P(("prow", "pcol"), None),
        P(),
        P(),
        P(),
    )
    return jax.shard_map(
        body, mesh=mesh, in_specs=placed, out_specs=P(None, "prow", None, "pcol"), check_vma=False
    )
```

```python
import functools

import jax
import jax.numpy as jnp
from jax import lax
from jax.experimental import pallas as pl
from jax.experimental.pallas import tpu as pltpu
from jax.sharding import PartitionSpec as P

F32 = jnp.float32
BF16 = jnp.bfloat16
VM = pl.BlockSpec(memory_space=pltpu.VMEM)
HBM = pl.BlockSpec(memory_space=pltpu.HBM)
SM = pl.BlockSpec(memory_space=pltpu.SMEM)
B = 256
KEEP = 48
PARAMS = dict(compiler_params=pltpu.CompilerParams(vmem_limit_bytes=14 * 1024 * 1024))

ALONE = dict(compiler_params=pltpu.CompilerParams(vmem_limit_bytes=63 * 1024 * 1024))


def iota(shape, dim):
    return lax.broadcasted_iota(jnp.int32, shape, dim)


def dot(a, b):
    return jnp.dot(a, b, preferred_element_type=F32)


def halves(x):
    high = x.astype(BF16)
    return high, (x - high.astype(F32)).astype(BF16)


def dot3(a, b):
    ah, al = a
    bh, bl = b
    return dot(ah, bh) + (dot(ah, bl) + dot(al, bh))


def pick(onehot, x):
    high, low = halves(x)
    return dot(onehot, high) + dot(onehot, low)


def lookup(table, d, pos):
    n = pos.shape[1]
    hot = (iota((B, n), 0) == pos).astype(F32).astype(BF16)
    high = table // 256
    low = table - high * 256
    both = jnp.concatenate([high, low], axis=0).astype(F32).astype(BF16)
    got = dot(both, hot).astype(jnp.int32)
    rows = table.shape[0]
    values = got[:rows] * 256 + got[rows:]
    return jnp.sum(jnp.where(iota((rows, n), 0) == d, values, 0), axis=0, keepdims=True)


def turn(apart):
    apart = apart & 3
    return jnp.where(apart == 0, 0, jnp.where(apart == 1, 2, jnp.where(apart == 2, 3, 1)))


def index_kernel(place, local_picks, level_picks, order, own_out, active_out, give_out, slot_out, xy_out, fits_out):
    rows = active_out.shape[1]
    keep = give_out.shape[0]
    p = place[0]
    retired = jnp.zeros((rows, 1), F32)
    owners, locals_ = [], []
    for k in range(order.shape[0]):
        pos = order[k : k + 1, :]
        d = jnp.zeros_like(pos)
        for level in range(level_picks.shape[1] - 1, -1, -1):
            j = lookup(level_picks[k, level], d, pos)
            bit = 1 << level
            d = (d & ~bit) | jnp.where(j >= B, bit, 0)
            pos = j & (B - 1)
        r = lookup(local_picks[k], d, pos)
        own = jnp.where(d == p, r, -1)
        own_out[k * B : (k + 1) * B, :] = jnp.broadcast_to(own, (128, B)).T
        hit = (iota((rows, B), 0) == own).astype(F32)
        retired = jnp.maximum(retired, jnp.max(hit, axis=1, keepdims=True))
        active_out[k] = jnp.broadcast_to(1.0 - retired, (rows, 128))
        owners.append(d)
        locals_.append(r)
    d = jnp.concatenate(owners, axis=1)
    r = jnp.concatenate(locals_, axis=1)
    n = d.shape[1]
    d_col = jnp.broadcast_to(d, (128, n)).T[:, 0:1]
    before = (d_col == d) & (iota((n, n), 0) < iota((n, n), 1))
    rank = jnp.sum(before.astype(jnp.int32), axis=0, keepdims=True)
    fits_out[0] = (jnp.max(rank) < keep).astype(jnp.int32)
    slot_out[...] = rows_hot(jnp.broadcast_to(d * keep + rank, (128, n)).T, slot_out.shape[1])
    across = turn(d - p)
    down = turn((d >> 2) - (p >> 2))
    xy_out[...] = rows_hot(jnp.broadcast_to((down * 4 + across) * keep + rank, (128, n)).T, xy_out.shape[1])
    mine = (iota((keep, n), 0) == rank) & (d == p)
    give = jnp.sum(jnp.where(mine, r + 2, 0), axis=1, keepdims=True) - 2
    give_out[...] = jnp.broadcast_to(give, (keep, 128))


def pack_kernel(place, partials_hbm, targets_hbm, counts_hbm, out, partials, targets, counts, sems):
    slots, sources = targets.shape
    parts = sems.shape[0] - 2
    step = sources // parts
    small = [
        pltpu.make_async_copy(targets_hbm, targets, sems.at[parts]),
        pltpu.make_async_copy(counts_hbm, counts, sems.at[parts + 1]),
    ]
    large = [
        pltpu.make_async_copy(
            partials_hbm.at[i * step : (i + 1) * step], partials.at[i * step : (i + 1) * step], sems.at[i]
        )
        for i in range(parts)
    ]
    for copy in small + large:
        copy.start()
    for copy in small:
        copy.wait()
    codes = jnp.where(iota((slots, sources), 0) < counts[...], targets[...], -1)
    codes = jnp.concatenate([codes] * (128 // slots), axis=0)
    codes = jnp.where(iota(codes.shape, 0) // slots == place[2] % (128 // slots), codes, 0)
    row = codes.astype(F32).T
    for i in range(parts):
        large[i].wait()
        for s in range(i * step, (i + 1) * step):
            out[17 * s : 17 * s + 8, :] = partials[s, :, :128]
            out[17 * s + 8 : 17 * s + 16, :] = partials[s, :, 128:]
            out[17 * s + 16 : 17 * s + 17, :] = row[s : s + 1, :]


def unpack(payload):
    sources = payload.shape[0] // 17
    left, right, codes = [], [], []
    for g in range(sources // 16):
        row = jnp.zeros((1, 128), F32)
        for s in range(16 * g, 16 * g + 16):
            left.append(payload[17 * s : 17 * s + 8, :])
            right.append(payload[17 * s + 8 : 17 * s + 16, :])
            row = row + payload[17 * s + 16 : 17 * s + 17, :]
        codes.append(row)
    values = jnp.concatenate([jnp.concatenate(left, axis=0), jnp.concatenate(right, axis=0)], axis=1)
    return halves(values), jnp.concatenate(codes, axis=1).astype(jnp.int32)


def hot_of(code, rows, u):
    return (code == iota((rows, code.shape[1]), 0) * 4 + u).astype(F32).astype(BF16)


def rows_hot(chosen, rows):
    return (chosen[:, 0:1] == iota((chosen.shape[0], rows), 1)).astype(F32).astype(BF16)


def assemble_kernel(payload, front, own, matrix_out, pivots_out):
    (high, low), code = unpack(payload)
    rows = front.shape[0]
    pivot_hot = rows_hot(own, rows)
    for u in range(4):
        cols = slice(u * B, (u + 1) * B)
        hot = hot_of(code, rows, u)
        tile = front[:, cols] + (dot(hot, high) + dot(hot, low))
        matrix_out[:, cols] = tile
        pivots_out[:, cols] = pick(pivot_hot, tile)


def front_kernel(front, give, out):
    keep = give.shape[0]
    hot = rows_hot(give, front.shape[0])
    for u in range(4):
        out[u * keep : (u + 1) * keep, :] = pick(hot, front[:, u * B : (u + 1) * B])


def lead_kernel(payload, front_rows, give, send_first, send_rest):
    (high, low), code = unpack(payload)
    keep = give.shape[0]
    chosen = give[:, 0:1] * 4
    hot = jnp.concatenate([(chosen + u == code).astype(F32) for u in range(4)], axis=0).astype(BF16)
    sums = front_rows[...] + (dot(hot, high) + dot(hot, low))
    for i in range(send_first.shape[0] // keep):
        send_first[i * keep : (i + 1) * keep, :] = sums[:keep]
    for u in range(1, 4):
        send_rest[:, (u - 1) * B : u * B] = sums[u * keep : (u + 1) * keep]


def tiles_kernel(payload, front, first_out, rest_out, done_out):
    done_out[...] = jnp.zeros_like(done_out)
    (high, low), code = unpack(payload)
    for u in range(4):
        hot = hot_of(code, front.shape[0], u)
        tile = front[:, u * B : (u + 1) * B] + (dot(hot, high) + dot(hot, low))
        if u == 0:
            first_out[...] = tile
        else:
            rest_out[:, (u - 1) * B : u * B] = tile


def join_kernel(tiles_done, sort_done, a0, a1, a2, a3, out):
    size = a0.shape[0]
    for i, a in enumerate((a0, a1, a2, a3)):
        out[i * size : (i + 1) * size, :] = a[...]


def sort_first_kernel(slot, gathered, out, done_out):
    done_out[...] = jnp.zeros_like(done_out)
    out[...] = pick(slot[...], gathered[...])


def inverse_of(diag):
    eye = iota((B, B), 0) == iota((B, B), 1)
    only = jnp.where(eye, diag, 0.0)
    by_row = 1.0 / jnp.sum(only, axis=1, keepdims=True)
    by_col = 1.0 / jnp.sum(only, axis=0, keepdims=True)
    two = jnp.where(eye, 2.0, 0.0)
    x = by_row * (two - diag * by_col)
    xs = halves(x)
    return dot3(xs, halves(two - dot3(halves(diag), xs)))


def panel_kernel(place, w_own, w_other, r_own, r_other, active, half_out, tile_out):
    even = place[1] % 2 == 0
    w0 = jnp.where(even, w_own[...], w_other[...])
    w1 = jnp.where(even, w_other[...], w_own[...])
    r0 = jnp.where(even, r_own[...], r_other[...])
    r1 = jnp.where(even, r_other[...], r_own[...])
    act0 = active[0][:, 0:1]
    act1 = active[1][:, 0:1]
    inv0 = halves(inverse_of(w0[:B]))
    m0w = dot3(halves(w0[B:]), inv0)
    m0w_s = halves(m0w)
    p01 = halves(w1[:B])
    inv1 = halves(inverse_of(w1[B:] - dot3(m0w_s, p01)))
    m0 = dot3(halves(r0), inv0)
    m0a = jnp.where(act0 > 0, m0, 0.0)
    r1 = r1 - dot3(halves(m0a), p01)
    m1 = dot3(halves(r1), inv1)
    n1 = jnp.where(act1 > 0, m1, 0.0)
    n0 = m0a - dot3(halves(n1), m0w_s)
    half_out[...] = jnp.where(even, n0, n1)
    tile_out[...] = jnp.where(even, jnp.where(act0 > 0, m0, r0), jnp.where(act1 > 0, m1, r1))


def update_kernel(place, matrix, pivots, n_own, n_other, tile, out):
    even = place[1] % 2 == 0
    n0 = halves(jnp.where(even, n_own[...], n_other[...]))
    n1 = halves(jnp.where(even, n_other[...], n_own[...]))
    for u in range(4):
        cols = slice(u * B, (u + 1) * B)
        new = matrix[:, cols] - (
            dot3(n0, halves(pivots[:B, cols])) + dot3(n1, halves(pivots[B:, cols]))
        )
        if u == 0:
            new = jnp.where(place[1] < 2, tile[...], new)
        out[:, cols] = new


def finish_kernel(
    place, n_early, n_last, o_early, o_last, tile_hbm, first_hbm, w_first_hbm, rest_hbm, xy_hbm,
    a0, a1, a2, a3, out_hbm, n_own, n_other, first, w_first, tile, rest, xy, w_rest, out, sems
):
    q = place[1]
    even = q % 2 == 0
    far = (q == 4) | (q == 5)
    copy = pltpu.make_async_copy

    @pl.when(far)
    def _():
        copy(n_last, n_own, sems.at[0]).start()
        copy(o_last, n_other, sems.at[1]).start()

    @pl.when(jnp.logical_not(far))
    def _():
        copy(n_early, n_own, sems.at[0]).start()
        copy(o_early, n_other, sems.at[1]).start()

    size = a0.shape[0]
    moves = [
        copy(xy_hbm, xy, sems.at[2]),
        copy(w_first_hbm, w_first, sems.at[3]),
        copy(first_hbm, first, sems.at[4]),
        copy(tile_hbm, tile, sems.at[5]),
        copy(a0, w_rest.at[:size], sems.at[6]),
        copy(a1, w_rest.at[size : 2 * size], sems.at[7]),
        copy(a2, w_rest.at[2 * size : 3 * size], sems.at[8]),
        copy(a3, w_rest.at[3 * size :], sems.at[9]),
        copy(rest_hbm, rest, sems.at[10]),
    ]
    for move in moves:
        move.start()
    copy(n_early, n_own, sems.at[0]).wait()
    copy(o_early, n_other, sems.at[1]).wait()
    h0, l0 = halves(jnp.where(even, n_own[...], n_other[...]))
    h1, l1 = halves(jnp.where(even, n_other[...], n_own[...]))
    rows = first.shape[0]
    half = out.shape[1]
    block = half // 2
    moves[0].wait()
    n_high = jnp.concatenate([h0, h1], axis=1)
    n_low = jnp.concatenate([l0, l1], axis=1)
    hot = xy[...]
    high = dot(n_high, hot).astype(BF16)
    low = dot(n_low, hot).astype(BF16)
    for move in moves[1:4]:
        move.wait()
    new = first[...] - dot3((n_high, n_low), halves(w_first[...]))
    new = jnp.where(q < 2, tile[...], new)
    for t in range(rows // half):
        out[t, :, 0, :] = new[t * half : (t + 1) * half]
    for move in moves[4:]:
        move.wait()
    w = [halves(w_rest[:, u * B : (u + 1) * B]) for u in range(3)]
    sent = []
    for i in range(rows // block):
        t, at = i * block // half, i * block % half
        span = slice(i * block, (i + 1) * block)
        for u in range(1, 4):
            cols = slice((u - 1) * B, u * B)
            out[t, at : at + block, u, :] = rest[span, cols] - dot3((high[span], low[span]), w[u - 1])
        done = copy(out.at[t, at : at + block], out_hbm.at[t, at : at + block], sems.at[11 + i])
        done.start()
        sent.append(done)
    for done in sent:
        done.wait()


def call(kernel, outs, n_in, scalars=1, outs_in_smem=0, flops=0, moved=0):
    specs = jax.tree.map(lambda _: VM, outs)
    if outs_in_smem:
        specs = specs[:-outs_in_smem] + (SM,) * outs_in_smem
    return pl.pallas_call(
        kernel,
        out_shape=outs,
        in_specs=[SM] * scalars + [VM] * (n_in - scalars),
        out_specs=specs,
        cost_estimate=pl.CostEstimate(flops=flops, bytes_accessed=moved, transcendentals=0),
        **PARAMS,
    )


def shaped(*shape, dtype=F32):
    return jax.ShapeDtypeStruct(shape, dtype)


def core_swap(x):
    return lax.ppermute(x, "pcol", [(i, i ^ 1) for i in range(lax.axis_size("pcol"))])


def shift_x(step):
    return [(p, p // 4 * 4 + (p + step) % 4) for p in range(16)]


def shift_y(step):
    return [(p, (p + 4 * step) % 16) for p in range(16)]


def ring(x, shift):
    return [x] + [lax.ppermute(x, "prow", shift(step)) for step in (1, -1, 2)]


def spread_z(x, z):
    one = lax.ppermute(x, "pcol", [(0, 2), (1, 3)])
    three = lax.ppermute(x, "pcol", [(0, 6), (1, 7)])
    two = lax.ppermute(x, "pcol", [(0, 4), (1, 5)])
    return jnp.where(z == 0, x, jnp.where(z == 1, one, jnp.where(z == 2, two, three)))


def body(front, partials, targets, counts, local_picks, level_picks, order):
    rows = front.shape[0] * front.shape[1]
    cols = front.shape[2] * front.shape[3]
    p = lax.axis_index("prow")
    q = lax.axis_index("pcol")
    me = p * lax.axis_size("pcol") + q
    place = jnp.stack([p, q, me]).astype(jnp.int32)
    sources = partials.shape[1]
    slots = partials.shape[2]

    payload = pl.pallas_call(
        pack_kernel,
        out_shape=shaped(sources * 17, 128),
        in_specs=[SM, HBM, HBM, HBM],
        out_specs=VM,
        scratch_shapes=[
            pltpu.VMEM((sources, slots, B), F32),
            pltpu.VMEM((slots, sources), jnp.int32),
            pltpu.VMEM((1, sources), jnp.int32),
            pltpu.SemaphoreType.DMA((6,)),
        ],
        cost_estimate=pl.CostEstimate(flops=10**6, bytes_accessed=2 * 10**6, transcendentals=0),
        **ALONE,
    )(place, partials[0], targets[0].T, counts).reshape(sources * 17, 1, 128)
    payload = lax.all_to_all(payload, ("prow", "pcol"), 0, 0, tiled=True).reshape(sources * 17, 128)

    copies = lax.axis_size("prow") * KEEP
    hots = shaped(2 * B, copies, dtype=BF16)
    own, active, give, slot, xy, fits = call(
        index_kernel,
        (
            shaped(2 * B, 128, dtype=jnp.int32),
            shaped(2, rows, 128),
            shaped(KEEP, 128, dtype=jnp.int32),
            hots,
            hots,
            shaped(1, dtype=jnp.int32),
        ),
        4,
        outs_in_smem=1,
        flops=10**9,
        moved=10**6,
    )(place, local_picks, level_picks, order)
    front, own = lax.optimization_barrier((front, own))
    flat = front.reshape(rows, cols)
    share_rows = 2 * B // lax.axis_size("prow")

    front_rows = call(front_kernel, shaped(4 * KEEP, B), 2, scalars=0, flops=10**8, moved=3 * 10**6)(flat, give)

    send_first, send_rest = call(
        lead_kernel, (shaped(copies, B), shaped(KEEP, cols - B)), 3, scalars=0, flops=10**8, moved=2 * 10**6
    )(payload, front_rows, give)
    w_first = lax.all_to_all(send_first, "prow", 0, 0, tiled=True)
    first, rest, done = call(
        tiles_kernel,
        (shaped(rows, B), shaped(rows, cols - B), shaped(8, 128)),
        2,
        scalars=0,
        flops=4 * 10**9,
        moved=6 * 10**6,
    )(payload, flat)
    w_first, sorted_ = call(
        sort_first_kernel, (shaped(2 * B, B), shaped(8, 128)), 2, scalars=0, flops=10**8, moved=10**6
    )(slot, w_first)
    joined = call(join_kernel, shaped(4 * KEEP, cols - B), 6, scalars=0, moved=10**6)(
        done, sorted_, *ring(send_rest, shift_x)
    )
    w_parts = ring(joined, shift_y)

    def panels(w_first, first, active, place, joined):
        r_other = core_swap(first)
        w_other = core_swap(w_first)
        half, tile = call(
            panel_kernel, (shaped(rows, B), shaped(rows, B)), 6, flops=2 * 10**9, moved=4 * 10**6
        )(place, w_first, w_other, first, r_other, active)
        q = place[1]
        near = (q == 2) | (q == 7)
        side = (q == 3) | (q == 6)
        step = lax.ppermute(half, "pcol", [(0, 2), (1, 7)])
        late = lax.ppermute(half, "pcol", [(1, 3), (0, 6)])
        last = lax.ppermute(step, "pcol", [(2, 4), (7, 5)])
        early = jnp.where(side, late, jnp.where(near, step, half))
        o_early = lax.ppermute(early, "pcol", [(0, 1), (1, 0), (2, 3), (3, 2), (6, 7), (7, 6)])
        o_last = lax.ppermute(last, "pcol", [(4, 5), (5, 4)])
        return early, last, o_early, o_last, tile

    def nothing(w_first, first, active, place, joined):
        return (jnp.zeros((rows, B), F32),) * 5

    parts = lax.cond(fits[0] == 1, panels, nothing, w_first, first, active, place, joined)

    def finish(payload, flat, own, active, place, *arrays):
        return pl.pallas_call(
            finish_kernel,
            out_shape=shaped(*front.shape),
            in_specs=[SM] + [HBM] * 13,
            out_specs=HBM,
            scratch_shapes=[
                pltpu.VMEM((rows, B), F32),
                pltpu.VMEM((rows, B), F32),
                pltpu.VMEM((rows, B), F32),
                pltpu.VMEM((2 * B, B), F32),
                pltpu.VMEM((rows, B), F32),
                pltpu.VMEM((rows, cols - B), F32),
                pltpu.VMEM((2 * B, copies), BF16),
                pltpu.VMEM((copies, cols - B), F32),
                pltpu.VMEM(front.shape, F32),
                pltpu.SemaphoreType.DMA((15,)),
            ],
            cost_estimate=pl.CostEstimate(flops=4 * 10**9, bytes_accessed=8 * 10**6, transcendentals=0),
            **ALONE,
        )(place, *arrays)

    def add_up(payload, flat, own, active, place, *arrays):
        matrix, pivots = call(
            assemble_kernel, (shaped(rows, cols), shaped(2 * B, cols)), 3, scalars=0, flops=4 * 10**9, moved=8 * 10**6
        )(payload, flat, own)
        r_own = matrix[:, :B]
        r_other = core_swap(r_own)
        share = lax.all_to_all(pivots, "prow", 0, 0, tiled=True).reshape(-1, share_rows, cols).sum(axis=0)
        pivots = lax.all_to_all(jnp.tile(share, (lax.axis_size("prow"), 1)), "prow", 0, 0, tiled=True)
        w_own = pivots[:, :B]
        w_other = core_swap(w_own)
        half, tile = call(
            panel_kernel, (shaped(rows, B), shaped(rows, B)), 6, flops=2 * 10**9, moved=4 * 10**6
        )(place, w_own, w_other, r_own, r_other, active)
        n_own = spread_z(half, place[1] // 2)
        n_other = core_swap(n_own)
        out = call(update_kernel, shaped(rows, cols), 6, flops=2 * 10**9, moved=8 * 10**6)(
            place, matrix, pivots, n_own, n_other, tile
        )
        return out.reshape(front.shape)

    return lax.cond(
        fits[0] == 1,
        finish,
        add_up,
        payload,
        flat,
        own,
        active,
        place,
        *parts,
        first,
        w_first,
        rest,
        xy,
        *w_parts,
    )


def solution(mesh):
    placed = (
        P(None, "prow", None, "pcol"),
        P(("prow", "pcol"), None, None, None),
        P(("prow", "pcol"), None, None),
        P(("prow", "pcol"), None),
        P(),
        P(),
        P(),
    )
    return jax.shard_map(
        body, mesh=mesh, in_specs=placed, out_specs=P(None, "prow", None, "pcol"), check_vma=False
    )
```

```python
import functools

import jax
import jax.numpy as jnp
from jax import lax
from jax.experimental import pallas as pl
from jax.experimental.pallas import tpu as pltpu
from jax.sharding import PartitionSpec as P

F32 = jnp.float32
BF16 = jnp.bfloat16
VM = pl.BlockSpec(memory_space=pltpu.VMEM)
HBM = pl.BlockSpec(memory_space=pltpu.HBM)
SM = pl.BlockSpec(memory_space=pltpu.SMEM)
B = 256
KEEP = 48
PARAMS = dict(compiler_params=pltpu.CompilerParams(vmem_limit_bytes=14 * 1024 * 1024))

ALONE = dict(compiler_params=pltpu.CompilerParams(vmem_limit_bytes=63 * 1024 * 1024))


def iota(shape, dim):
    return lax.broadcasted_iota(jnp.int32, shape, dim)


def dot(a, b):
    return jnp.dot(a, b, preferred_element_type=F32)


def halves(x):
    high = x.astype(BF16)
    return high, (x - high.astype(F32)).astype(BF16)


def dot3(a, b):
    ah, al = a
    bh, bl = b
    return dot(ah, bh) + (dot(ah, bl) + dot(al, bh))


def pick(onehot, x):
    high, low = halves(x)
    return dot(onehot, high) + dot(onehot, low)


def lookup(table, d, pos):
    n = pos.shape[1]
    hot = (iota((B, n), 0) == pos).astype(F32).astype(BF16)
    high = table // 256
    low = table - high * 256
    both = jnp.concatenate([high, low], axis=0).astype(F32).astype(BF16)
    got = dot(both, hot).astype(jnp.int32)
    rows = table.shape[0]
    values = got[:rows] * 256 + got[rows:]
    return jnp.sum(jnp.where(iota((rows, n), 0) == d, values, 0), axis=0, keepdims=True)


def turn(apart):
    apart = apart & 3
    return jnp.where(apart == 0, 0, jnp.where(apart == 1, 2, jnp.where(apart == 2, 3, 1)))


def index_kernel(place, local_picks, level_picks, order, own_out, active_out, give_out, slot_out, xy_out, fits_out):
    rows = active_out.shape[1]
    keep = give_out.shape[0]
    p = place[0]
    retired = jnp.zeros((rows, 1), F32)
    owners, locals_ = [], []
    for k in range(order.shape[0]):
        pos = order[k : k + 1, :]
        d = jnp.zeros_like(pos)
        for level in range(level_picks.shape[1] - 1, -1, -1):
            j = lookup(level_picks[k, level], d, pos)
            bit = 1 << level
            d = (d & ~bit) | jnp.where(j >= B, bit, 0)
            pos = j & (B - 1)
        r = lookup(local_picks[k], d, pos)
        own = jnp.where(d == p, r, -1)
        own_out[k * B : (k + 1) * B, :] = jnp.broadcast_to(own, (128, B)).T
        hit = (iota((rows, B), 0) == own).astype(F32)
        retired = jnp.maximum(retired, jnp.max(hit, axis=1, keepdims=True))
        active_out[k] = jnp.broadcast_to(1.0 - retired, (rows, 128))
        owners.append(d)
        locals_.append(r)
    d = jnp.concatenate(owners, axis=1)
    r = jnp.concatenate(locals_, axis=1)
    n = d.shape[1]
    d_col = jnp.broadcast_to(d, (128, n)).T[:, 0:1]
    before = (d_col == d) & (iota((n, n), 0) < iota((n, n), 1))
    rank = jnp.sum(before.astype(jnp.int32), axis=0, keepdims=True)
    fits_out[0] = (jnp.max(rank) < keep).astype(jnp.int32)
    slot_out[...] = rows_hot(jnp.broadcast_to(d * keep + rank, (128, n)).T, slot_out.shape[1])
    across = turn(d - p)
    down = turn((d >> 2) - (p >> 2))
    xy_out[...] = rows_hot(jnp.broadcast_to((down * 4 + across) * keep + rank, (128, n)).T, xy_out.shape[1])
    mine = (iota((keep, n), 0) == rank) & (d == p)
    give = jnp.sum(jnp.where(mine, r + 2, 0), axis=1, keepdims=True) - 2
    give_out[...] = jnp.broadcast_to(give, (keep, 128))


def pack_kernel(place, partials_hbm, targets_hbm, counts_hbm, out_hbm, partials, targets, counts, out, sems, out_sems):
    slots, sources = targets.shape
    parts = sems.shape[0] - 2
    step = sources // parts
    small = [
        pltpu.make_async_copy(targets_hbm, targets, sems.at[parts]),
        pltpu.make_async_copy(counts_hbm, counts, sems.at[parts + 1]),
    ]
    large = [
        pltpu.make_async_copy(
            partials_hbm.at[i * step : (i + 1) * step], partials.at[i * step : (i + 1) * step], sems.at[i]
        )
        for i in range(parts)
    ]
    for copy in small + large:
        copy.start()
    for copy in small:
        copy.wait()
    codes = jnp.where(iota((slots, sources), 0) < counts[...], targets[...], -1)
    codes = jnp.concatenate([codes] * (128 // slots), axis=0)
    codes = jnp.where(iota(codes.shape, 0) // slots == place[2] % (128 // slots), codes, 0)
    row = codes.astype(F32).T
    sent = []
    for i in range(parts):
        large[i].wait()
        for s in range(i * step, (i + 1) * step):
            out[17 * s : 17 * s + 8, :] = partials[s, :, :128]
            out[17 * s + 8 : 17 * s + 16, :] = partials[s, :, 128:]
            out[17 * s + 16 : 17 * s + 17, :] = row[s : s + 1, :]
        span = slice(17 * step * i, 17 * step * (i + 1))
        sent.append(pltpu.make_async_copy(out.at[span], out_hbm.at[span], out_sems.at[i]))
        sent[-1].start()
    for copy in sent:
        copy.wait()


def unpack(payload):
    sources = payload.shape[0] // 17
    left, right, codes = [], [], []
    for g in range(sources // 16):
        row = jnp.zeros((1, 128), F32)
        for s in range(16 * g, 16 * g + 16):
            left.append(payload[17 * s : 17 * s + 8, :])
            right.append(payload[17 * s + 8 : 17 * s + 16, :])
            row = row + payload[17 * s + 16 : 17 * s + 17, :]
        codes.append(row)
    values = jnp.concatenate([jnp.concatenate(left, axis=0), jnp.concatenate(right, axis=0)], axis=1)
    return halves(values), jnp.concatenate(codes, axis=1).astype(jnp.int32)


def hot_of(code, rows, u):
    return (code == iota((rows, code.shape[1]), 0) * 4 + u).astype(F32).astype(BF16)


def rows_hot(chosen, rows):
    return (chosen[:, 0:1] == iota((chosen.shape[0], rows), 1)).astype(F32).astype(BF16)


def assemble_kernel(payload, front, own, matrix_out, pivots_out):
    (high, low), code = unpack(payload)
    rows = front.shape[0]
    pivot_hot = rows_hot(own, rows)
    for u in range(4):
        cols = slice(u * B, (u + 1) * B)
        hot = hot_of(code, rows, u)
        tile = front[:, cols] + (dot(hot, high) + dot(hot, low))
        matrix_out[:, cols] = tile
        pivots_out[:, cols] = pick(pivot_hot, tile)


def front_kernel(front, give, out):
    keep = give.shape[0]
    hot = rows_hot(give, front.shape[0])
    for u in range(4):
        out[u * keep : (u + 1) * keep, :] = pick(hot, front[:, u * B : (u + 1) * B])


def lead_kernel(payload, front_rows, give, send_first, send_rest):
    (high, low), code = unpack(payload)
    keep = give.shape[0]
    chosen = give[:, 0:1] * 4
    hot = jnp.concatenate([(chosen + u == code).astype(F32) for u in range(4)], axis=0).astype(BF16)
    sums = front_rows[...] + (dot(hot, high) + dot(hot, low))
    for i in range(send_first.shape[0] // keep):
        send_first[i * keep : (i + 1) * keep, :] = sums[:keep]
    for u in range(1, 4):
        send_rest[:, (u - 1) * B : u * B] = sums[u * keep : (u + 1) * keep]


def tiles_kernel(payload, front, first_out, rest_out):
    (high, low), code = unpack(payload)
    for u in range(4):
        hot = hot_of(code, front.shape[0], u)
        tile = front[:, u * B : (u + 1) * B] + (dot(hot, high) + dot(hot, low))
        if u == 0:
            first_out[...] = tile
        else:
            rest_out[:, (u - 1) * B : u * B] = tile


def first_kernel(r_done, slot, gathered, a0, a1, a2, a3, first_out, joined_out):
    size = a0.shape[0]
    for i, part in enumerate((a0, a1, a2, a3)):
        joined_out[i * size : (i + 1) * size, :] = part[...]
    first_out[...] = pick(slot[...], gathered[...])


def inverse_of(diag):
    eye = iota((B, B), 0) == iota((B, B), 1)
    only = jnp.where(eye, diag, 0.0)
    by_row = 1.0 / jnp.sum(only, axis=1, keepdims=True)
    by_col = 1.0 / jnp.sum(only, axis=0, keepdims=True)
    two = jnp.where(eye, 2.0, 0.0)
    x = by_row * (two - diag * by_col)
    xs = halves(x)
    return dot3(xs, halves(two - dot3(halves(diag), xs)))


def panel_kernel(place, w_own, w_other, r_own, r_other, active, half_out, tile_out):
    even = place[1] % 2 == 0
    w0 = jnp.where(even, w_own[...], w_other[...])
    w1 = jnp.where(even, w_other[...], w_own[...])
    r0 = jnp.where(even, r_own[...], r_other[...])
    r1 = jnp.where(even, r_other[...], r_own[...])
    act0 = active[0][:, 0:1]
    act1 = active[1][:, 0:1]
    inv0 = halves(inverse_of(w0[:B]))
    m0w = dot3(halves(w0[B:]), inv0)
    m0w_s = halves(m0w)
    p01 = halves(w1[:B])
    inv1 = halves(inverse_of(w1[B:] - dot3(m0w_s, p01)))
    m0 = dot3(halves(r0), inv0)
    m0a = jnp.where(act0 > 0, m0, 0.0)
    r1 = r1 - dot3(halves(m0a), p01)
    m1 = dot3(halves(r1), inv1)
    n1 = jnp.where(act1 > 0, m1, 0.0)
    n0 = m0a - dot3(halves(n1), m0w_s)
    half_out[...] = jnp.where(even, n0, n1)
    tile_out[...] = jnp.where(even, jnp.where(act0 > 0, m0, r0), jnp.where(act1 > 0, m1, r1))


def update_kernel(place, matrix, pivots, n_own, n_other, tile, out):
    even = place[1] % 2 == 0
    n0 = halves(jnp.where(even, n_own[...], n_other[...]))
    n1 = halves(jnp.where(even, n_other[...], n_own[...]))
    for u in range(4):
        cols = slice(u * B, (u + 1) * B)
        new = matrix[:, cols] - (
            dot3(n0, halves(pivots[:B, cols])) + dot3(n1, halves(pivots[B:, cols]))
        )
        if u == 0:
            new = jnp.where(place[1] < 2, tile[...], new)
        out[:, cols] = new


def finish_kernel(
    place, n_early, n_last, o_early, o_last, tile_hbm, first_hbm, w_first_hbm, rest_hbm, xy_hbm,
    a0, a1, a2, a3, out_hbm, n_own, n_other, first, w_first, tile, rest, xy, w_rest, out, sems
):
    q = place[1]
    even = q % 2 == 0
    far = (q == 4) | (q == 5)
    copy = pltpu.make_async_copy

    @pl.when(far)
    def _():
        copy(n_last, n_own, sems.at[0]).start()
        copy(o_last, n_other, sems.at[1]).start()

    @pl.when(jnp.logical_not(far))
    def _():
        copy(n_early, n_own, sems.at[0]).start()
        copy(o_early, n_other, sems.at[1]).start()

    size = a0.shape[0]
    moves = [
        copy(xy_hbm, xy, sems.at[2]),
        copy(w_first_hbm, w_first, sems.at[3]),
        copy(first_hbm, first, sems.at[4]),
        copy(tile_hbm, tile, sems.at[5]),
        copy(a0, w_rest.at[:size], sems.at[6]),
        copy(a1, w_rest.at[size : 2 * size], sems.at[7]),
        copy(a2, w_rest.at[2 * size : 3 * size], sems.at[8]),
        copy(a3, w_rest.at[3 * size :], sems.at[9]),
        copy(rest_hbm, rest, sems.at[10]),
    ]
    for move in moves:
        move.start()
    copy(n_early, n_own, sems.at[0]).wait()
    copy(o_early, n_other, sems.at[1]).wait()
    h0, l0 = halves(jnp.where(even, n_own[...], n_other[...]))
    h1, l1 = halves(jnp.where(even, n_other[...], n_own[...]))
    rows = first.shape[0]
    half = out.shape[1]
    block = half // 2
    moves[0].wait()
    n_high = jnp.concatenate([h0, h1], axis=1)
    n_low = jnp.concatenate([l0, l1], axis=1)
    hot = xy[...]
    high = dot(n_high, hot).astype(BF16)
    low = dot(n_low, hot).astype(BF16)
    for move in moves[1:4]:
        move.wait()
    new = first[...] - dot3((n_high, n_low), halves(w_first[...]))
    new = jnp.where(q < 2, tile[...], new)
    for t in range(rows // half):
        out[t, :, 0, :] = new[t * half : (t + 1) * half]
    for move in moves[4:]:
        move.wait()
    w = [halves(w_rest[:, u * B : (u + 1) * B]) for u in range(3)]
    sent = []
    for i in range(rows // block):
        t, at = i * block // half, i * block % half
        span = slice(i * block, (i + 1) * block)
        for u in range(1, 4):
            cols = slice((u - 1) * B, u * B)
            out[t, at : at + block, u, :] = rest[span, cols] - dot3((high[span], low[span]), w[u - 1])
        done = copy(out.at[t, at : at + block], out_hbm.at[t, at : at + block], sems.at[11 + i])
        done.start()
        sent.append(done)
    for done in sent:
        done.wait()


def call(kernel, outs, n_in, scalars=1, outs_in_smem=0, flops=0, moved=0):
    specs = jax.tree.map(lambda _: VM, outs)
    if outs_in_smem:
        specs = specs[:-outs_in_smem] + (SM,) * outs_in_smem
    return pl.pallas_call(
        kernel,
        out_shape=outs,
        in_specs=[SM] * scalars + [VM] * (n_in - scalars),
        out_specs=specs,
        cost_estimate=pl.CostEstimate(flops=flops, bytes_accessed=moved, transcendentals=0),
        **PARAMS,
    )


def shaped(*shape, dtype=F32):
    return jax.ShapeDtypeStruct(shape, dtype)


def core_swap(x):
    return lax.ppermute(x, "pcol", [(i, i ^ 1) for i in range(lax.axis_size("pcol"))])


def shift_x(step):
    return [(p, p // 4 * 4 + (p + step) % 4) for p in range(16)]


def shift_y(step):
    return [(p, (p + 4 * step) % 16) for p in range(16)]


def ring(x, shift):
    return [x] + [lax.ppermute(x, "prow", shift(step)) for step in (1, -1, 2)]


def spread_z(x, z):
    one = lax.ppermute(x, "pcol", [(0, 2), (1, 3)])
    three = lax.ppermute(x, "pcol", [(0, 6), (1, 7)])
    two = lax.ppermute(x, "pcol", [(0, 4), (1, 5)])
    return jnp.where(z == 0, x, jnp.where(z == 1, one, jnp.where(z == 2, two, three)))


def body(front, partials, targets, counts, local_picks, level_picks, order):
    rows = front.shape[0] * front.shape[1]
    cols = front.shape[2] * front.shape[3]
    p = lax.axis_index("prow")
    q = lax.axis_index("pcol")
    me = p * lax.axis_size("pcol") + q
    place = jnp.stack([p, q, me]).astype(jnp.int32)
    sources = partials.shape[1]
    slots = partials.shape[2]

    payload = pl.pallas_call(
        pack_kernel,
        out_shape=shaped(sources * 17, 128),
        in_specs=[SM, HBM, HBM, HBM],
        out_specs=HBM,
        scratch_shapes=[
            pltpu.VMEM((sources, slots, B), F32),
            pltpu.VMEM((slots, sources), jnp.int32),
            pltpu.VMEM((1, sources), jnp.int32),
            pltpu.VMEM((sources * 17, 128), F32),
            pltpu.SemaphoreType.DMA((6,)),
            pltpu.SemaphoreType.DMA((4,)),
        ],
        cost_estimate=pl.CostEstimate(flops=10**6, bytes_accessed=2 * 10**6, transcendentals=0),
        **ALONE,
    )(place, partials[0], targets[0].T, counts).reshape(sources * 17, 1, 128)
    payload = lax.all_to_all(payload, ("prow", "pcol"), 0, 0, tiled=True).reshape(sources * 17, 128)

    copies = lax.axis_size("prow") * KEEP
    hots = shaped(2 * B, copies, dtype=BF16)
    own, active, give, slot, xy, fits = call(
        index_kernel,
        (
            shaped(2 * B, 128, dtype=jnp.int32),
            shaped(2, rows, 128),
            shaped(KEEP, 128, dtype=jnp.int32),
            hots,
            hots,
            shaped(1, dtype=jnp.int32),
        ),
        4,
        outs_in_smem=1,
        flops=10**9,
        moved=10**6,
    )(place, local_picks, level_picks, order)
    front, own = lax.optimization_barrier((front, own))
    flat = front.reshape(rows, cols)
    share_rows = 2 * B // lax.axis_size("prow")

    front_rows = call(front_kernel, shaped(4 * KEEP, B), 2, scalars=0, flops=10**8, moved=3 * 10**6)(flat, give)

    send_first, send_rest = call(
        lead_kernel, (shaped(copies, B), shaped(KEEP, cols - B)), 3, scalars=0, flops=10**8, moved=2 * 10**6
    )(payload, front_rows, give)
    w_first = lax.all_to_all(send_first, "prow", 0, 0, tiled=True)
    first, rest = call(
        tiles_kernel,
        (shaped(rows, B), shaped(rows, cols - B)),
        2,
        scalars=0,
        flops=4 * 10**9,
        moved=6 * 10**6,
    )(payload, flat)
    r_other = core_swap(first)
    whole = lambda *shape: pl.BlockSpec(shape, lambda i: (0, 0))
    w_first, joined = pl.pallas_call(
        first_kernel,
        out_shape=(shaped(2 * B, B), shaped(4 * KEEP, cols - B)),
        grid=(1,),
        in_specs=[whole(8, 128), whole(2 * B, copies), whole(copies, B)] + [whole(KEEP, cols - B)] * 4,
        out_specs=(whole(2 * B, B), whole(4 * KEEP, cols - B)),
        cost_estimate=pl.CostEstimate(flops=10**8, bytes_accessed=2 * 10**6, transcendentals=0),
        **PARAMS,
    )(r_other, slot, w_first, *ring(send_rest, shift_x))
    w_other = core_swap(w_first)
    w_parts = ring(joined, shift_y)


    def panels(w_first, w_other, first, r_other, active, place, joined):
        half, tile = call(
            panel_kernel, (shaped(rows, B), shaped(rows, B)), 6, flops=2 * 10**9, moved=4 * 10**6
        )(place, w_first, w_other, first, r_other, active)
        q = place[1]
        near = (q == 2) | (q == 7)
        side = (q == 3) | (q == 6)
        step = lax.ppermute(half, "pcol", [(0, 2), (1, 7)])
        late = lax.ppermute(half, "pcol", [(1, 3), (0, 6)])
        last = lax.ppermute(step, "pcol", [(2, 4), (7, 5)])
        early = jnp.where(side, late, jnp.where(near, step, half))
        o_early = lax.ppermute(early, "pcol", [(0, 1), (1, 0), (2, 3), (3, 2), (6, 7), (7, 6)])
        o_last = lax.ppermute(last, "pcol", [(4, 5), (5, 4)])
        return early, last, o_early, o_last, tile

    def nothing(w_first, w_other, first, r_other, active, place, joined):
        return (jnp.zeros((rows, B), F32),) * 5

    parts = lax.cond(fits[0] == 1, panels, nothing, w_first, w_other, first, r_other, active, place, joined)

    def finish(payload, flat, own, active, place, *arrays):
        return pl.pallas_call(
            finish_kernel,
            out_shape=shaped(*front.shape),
            in_specs=[SM] + [HBM] * 13,
            out_specs=HBM,
            scratch_shapes=[
                pltpu.VMEM((rows, B), F32),
                pltpu.VMEM((rows, B), F32),
                pltpu.VMEM((rows, B), F32),
                pltpu.VMEM((2 * B, B), F32),
                pltpu.VMEM((rows, B), F32),
                pltpu.VMEM((rows, cols - B), F32),
                pltpu.VMEM((2 * B, copies), BF16),
                pltpu.VMEM((copies, cols - B), F32),
                pltpu.VMEM(front.shape, F32),
                pltpu.SemaphoreType.DMA((15,)),
            ],
            cost_estimate=pl.CostEstimate(flops=4 * 10**9, bytes_accessed=8 * 10**6, transcendentals=0),
            **ALONE,
        )(place, *arrays)

    def add_up(payload, flat, own, active, place, *arrays):
        matrix, pivots = call(
            assemble_kernel, (shaped(rows, cols), shaped(2 * B, cols)), 3, scalars=0, flops=4 * 10**9, moved=8 * 10**6
        )(payload, flat, own)
        r_own = matrix[:, :B]
        r_other = core_swap(r_own)
        share = lax.all_to_all(pivots, "prow", 0, 0, tiled=True).reshape(-1, share_rows, cols).sum(axis=0)
        pivots = lax.all_to_all(jnp.tile(share, (lax.axis_size("prow"), 1)), "prow", 0, 0, tiled=True)
        w_own = pivots[:, :B]
        w_other = core_swap(w_own)
        half, tile = call(
            panel_kernel, (shaped(rows, B), shaped(rows, B)), 6, flops=2 * 10**9, moved=4 * 10**6
        )(place, w_own, w_other, r_own, r_other, active)
        n_own = spread_z(half, place[1] // 2)
        n_other = core_swap(n_own)
        out = call(update_kernel, shaped(rows, cols), 6, flops=2 * 10**9, moved=8 * 10**6)(
            place, matrix, pivots, n_own, n_other, tile
        )
        return out.reshape(front.shape)

    return lax.cond(
        fits[0] == 1,
        finish,
        add_up,
        payload,
        flat,
        own,
        active,
        place,
        *parts,
        first,
        w_first,
        rest,
        xy,
        *w_parts,
    )


def solution(mesh):
    placed = (
        P(None, "prow", None, "pcol"),
        P(("prow", "pcol"), None, None, None),
        P(("prow", "pcol"), None, None),
        P(("prow", "pcol"), None),
        P(),
        P(),
        P(),
    )
    return jax.shard_map(
        body, mesh=mesh, in_specs=placed, out_specs=P(None, "prow", None, "pcol"), check_vma=False
    )
```

```python
import functools

import jax
import jax.numpy as jnp
from jax import lax
from jax.experimental import pallas as pl
from jax.experimental.pallas import tpu as pltpu
from jax.sharding import PartitionSpec as P

F32 = jnp.float32
BF16 = jnp.bfloat16
VM = pl.BlockSpec(memory_space=pltpu.VMEM)
HBM = pl.BlockSpec(memory_space=pltpu.HBM)
SM = pl.BlockSpec(memory_space=pltpu.SMEM)
B = 256
KEEP = 48
PARAMS = dict(compiler_params=pltpu.CompilerParams(vmem_limit_bytes=14 * 1024 * 1024))

ALONE = dict(compiler_params=pltpu.CompilerParams(vmem_limit_bytes=63 * 1024 * 1024))


def iota(shape, dim):
    return lax.broadcasted_iota(jnp.int32, shape, dim)


def dot(a, b):
    return jnp.dot(a, b, preferred_element_type=F32)


def halves(x):
    high = x.astype(BF16)
    return high, (x - high.astype(F32)).astype(BF16)


def dot3(a, b):
    ah, al = a
    bh, bl = b
    return dot(ah, bh) + (dot(ah, bl) + dot(al, bh))


def pick(onehot, x):
    high, low = halves(x)
    return dot(onehot, high) + dot(onehot, low)


def lookup(table, d, pos):
    n = pos.shape[1]
    hot = (iota((B, n), 0) == pos).astype(F32).astype(BF16)
    high = table // 256
    low = table - high * 256
    both = jnp.concatenate([high, low], axis=0).astype(F32).astype(BF16)
    got = dot(both, hot).astype(jnp.int32)
    rows = table.shape[0]
    values = got[:rows] * 256 + got[rows:]
    return jnp.sum(jnp.where(iota((rows, n), 0) == d, values, 0), axis=0, keepdims=True)


def turn(apart):
    apart = apart & 3
    return jnp.where(apart == 0, 0, jnp.where(apart == 1, 2, jnp.where(apart == 2, 3, 1)))


def index_kernel(place, local_picks, level_picks, order, own_out, active_out, give_out, slot_out, xy_out, fits_out):
    rows = active_out.shape[1]
    keep = give_out.shape[0]
    p = place[0]
    retired = jnp.zeros((rows, 1), F32)
    owners, locals_ = [], []
    for k in range(order.shape[0]):
        pos = order[k : k + 1, :]
        d = jnp.zeros_like(pos)
        for level in range(level_picks.shape[1] - 1, -1, -1):
            j = lookup(level_picks[k, level], d, pos)
            bit = 1 << level
            d = (d & ~bit) | jnp.where(j >= B, bit, 0)
            pos = j & (B - 1)
        r = lookup(local_picks[k], d, pos)
        own = jnp.where(d == p, r, -1)
        own_out[k * B : (k + 1) * B, :] = jnp.broadcast_to(own, (128, B)).T
        hit = (iota((rows, B), 0) == own).astype(F32)
        retired = jnp.maximum(retired, jnp.max(hit, axis=1, keepdims=True))
        active_out[k] = jnp.broadcast_to(1.0 - retired, (rows, 128))
        owners.append(d)
        locals_.append(r)
    d = jnp.concatenate(owners, axis=1)
    r = jnp.concatenate(locals_, axis=1)
    n = d.shape[1]
    d_col = jnp.broadcast_to(d, (128, n)).T[:, 0:1]
    before = (d_col == d) & (iota((n, n), 0) < iota((n, n), 1))
    rank = jnp.sum(before.astype(jnp.int32), axis=0, keepdims=True)
    fits_out[0] = (jnp.max(rank) < keep).astype(jnp.int32)
    slot_out[...] = rows_hot(jnp.broadcast_to(d * keep + rank, (128, n)).T, slot_out.shape[1])
    across = turn(d - p)
    down = turn((d >> 2) - (p >> 2))
    xy_out[...] = rows_hot(jnp.broadcast_to((down * 4 + across) * keep + rank, (128, n)).T, xy_out.shape[1])
    mine = (iota((keep, n), 0) == rank) & (d == p)
    give = jnp.sum(jnp.where(mine, r + 2, 0), axis=1, keepdims=True) - 2
    give_out[...] = jnp.broadcast_to(give, (keep, 128))


def pack_kernel(place, partials_hbm, targets_hbm, counts_hbm, out_hbm, partials, targets, counts, out, sems, out_sems):
    slots, sources = targets.shape
    parts = sems.shape[0] - 2
    step = sources // parts
    small = [
        pltpu.make_async_copy(targets_hbm, targets, sems.at[parts]),
        pltpu.make_async_copy(counts_hbm, counts, sems.at[parts + 1]),
    ]
    large = [
        pltpu.make_async_copy(
            partials_hbm.at[i * step : (i + 1) * step], partials.at[i * step : (i + 1) * step], sems.at[i]
        )
        for i in range(parts)
    ]
    for copy in small + large:
        copy.start()
    for copy in small:
        copy.wait()
    codes = jnp.where(iota((slots, sources), 0) < counts[...], targets[...], -1)
    codes = jnp.concatenate([codes] * (128 // slots), axis=0)
    codes = jnp.where(iota(codes.shape, 0) // slots == place[2] % (128 // slots), codes, 0)
    row = codes.astype(F32).T
    sent = []
    for i in range(parts):
        large[i].wait()
        for s in range(i * step, (i + 1) * step):
            out[17 * s : 17 * s + 8, :] = partials[s, :, :128]
            out[17 * s + 8 : 17 * s + 16, :] = partials[s, :, 128:]
            out[17 * s + 16 : 17 * s + 17, :] = row[s : s + 1, :]
        span = slice(17 * step * i, 17 * step * (i + 1))
        sent.append(pltpu.make_async_copy(out.at[span], out_hbm.at[span], out_sems.at[i]))
        sent[-1].start()
    for copy in sent:
        copy.wait()


def unpack(payload):
    sources = payload.shape[0] // 17
    left, right, codes = [], [], []
    for g in range(sources // 16):
        row = jnp.zeros((1, 128), F32)
        for s in range(16 * g, 16 * g + 16):
            left.append(payload[17 * s : 17 * s + 8, :])
            right.append(payload[17 * s + 8 : 17 * s + 16, :])
            row = row + payload[17 * s + 16 : 17 * s + 17, :]
        codes.append(row)
    values = jnp.concatenate([jnp.concatenate(left, axis=0), jnp.concatenate(right, axis=0)], axis=1)
    return halves(values), jnp.concatenate(codes, axis=1).astype(jnp.int32)


def hot_of(code, rows, u):
    return (code == iota((rows, code.shape[1]), 0) * 4 + u).astype(F32).astype(BF16)


def rows_hot(chosen, rows):
    return (chosen[:, 0:1] == iota((chosen.shape[0], rows), 1)).astype(F32).astype(BF16)


def assemble_kernel(payload, front, own, matrix_out, pivots_out):
    (high, low), code = unpack(payload)
    rows = front.shape[0]
    pivot_hot = rows_hot(own, rows)
    for u in range(4):
        cols = slice(u * B, (u + 1) * B)
        hot = hot_of(code, rows, u)
        tile = front[:, cols] + (dot(hot, high) + dot(hot, low))
        matrix_out[:, cols] = tile
        pivots_out[:, cols] = pick(pivot_hot, tile)


def front_kernel(front, give, out):
    keep = give.shape[0]
    hot = rows_hot(give, front.shape[0])
    for u in range(4):
        out[u * keep : (u + 1) * keep, :] = pick(hot, front[:, u * B : (u + 1) * B])


def lead_kernel(payload, front_rows, give, send_first, send_rest):
    (high, low), code = unpack(payload)
    keep = give.shape[0]
    chosen = give[:, 0:1] * 4
    hot = jnp.concatenate([(chosen + u == code).astype(F32) for u in range(4)], axis=0).astype(BF16)
    sums = front_rows[...] + (dot(hot, high) + dot(hot, low))
    for i in range(send_first.shape[0] // keep):
        send_first[i * keep : (i + 1) * keep, :] = sums[:keep]
    for u in range(1, 4):
        send_rest[:, (u - 1) * B : u * B] = sums[u * keep : (u + 1) * keep]


def tiles_kernel(payload, front, first_out, rest_out, done_out):
    done_out[...] = jnp.zeros_like(done_out)
    (high, low), code = unpack(payload)
    for u in range(4):
        hot = hot_of(code, front.shape[0], u)
        tile = front[:, u * B : (u + 1) * B] + (dot(hot, high) + dot(hot, low))
        if u == 0:
            first_out[...] = tile
        else:
            rest_out[:, (u - 1) * B : u * B] = tile


def join_kernel(tiles_done, sort_done, a0, a1, a2, a3, out):
    size = a0.shape[0]
    for i, a in enumerate((a0, a1, a2, a3)):
        out[i * size : (i + 1) * size, :] = a[...]


def sort_first_kernel(slot, gathered, out, done_out):
    done_out[...] = jnp.zeros_like(done_out)
    out[...] = pick(slot[...], gathered[...])


def inverse_of(diag):
    eye = iota((B, B), 0) == iota((B, B), 1)
    only = jnp.where(eye, diag, 0.0)
    by_row = 1.0 / jnp.sum(only, axis=1, keepdims=True)
    by_col = 1.0 / jnp.sum(only, axis=0, keepdims=True)
    two = jnp.where(eye, 2.0, 0.0)
    x = by_row * (two - diag * by_col)
    xs = halves(x)
    return dot3(xs, halves(two - dot3(halves(diag), xs)))


def panel_kernel(place, w_own, w_other, r_own, r_other, active, half_out, tile_out):
    even = place[1] % 2 == 0
    w0 = jnp.where(even, w_own[...], w_other[...])
    w1 = jnp.where(even, w_other[...], w_own[...])
    r0 = jnp.where(even, r_own[...], r_other[...])
    r1 = jnp.where(even, r_other[...], r_own[...])
    act0 = active[0][:, 0:1]
    act1 = active[1][:, 0:1]
    inv0 = halves(inverse_of(w0[:B]))
    m0w = dot3(halves(w0[B:]), inv0)
    m0w_s = halves(m0w)
    p01 = halves(w1[:B])
    inv1 = halves(inverse_of(w1[B:] - dot3(m0w_s, p01)))
    m0 = dot3(halves(r0), inv0)
    m0a = jnp.where(act0 > 0, m0, 0.0)
    r1 = r1 - dot3(halves(m0a), p01)
    m1 = dot3(halves(r1), inv1)
    n1 = jnp.where(act1 > 0, m1, 0.0)
    n0 = m0a - dot3(halves(n1), m0w_s)
    half_out[...] = jnp.where(even, n0, n1)
    tile_out[...] = jnp.where(even, jnp.where(act0 > 0, m0, r0), jnp.where(act1 > 0, m1, r1))


def update_kernel(place, matrix, pivots, n_own, n_other, tile, out):
    even = place[1] % 2 == 0
    n0 = halves(jnp.where(even, n_own[...], n_other[...]))
    n1 = halves(jnp.where(even, n_other[...], n_own[...]))
    for u in range(4):
        cols = slice(u * B, (u + 1) * B)
        new = matrix[:, cols] - (
            dot3(n0, halves(pivots[:B, cols])) + dot3(n1, halves(pivots[B:, cols]))
        )
        if u == 0:
            new = jnp.where(place[1] < 2, tile[...], new)
        out[:, cols] = new


def finish_kernel(
    place, n_early, n_late, o_early, o_late, tile_hbm, first_hbm, w_first_hbm, rest_hbm, xy_hbm,
    a0, a1, a2, a3, out_hbm, n_own, n_other, first, w_first, tile, rest, xy, w_rest, out, sems
):
    q = place[1]
    even = q % 2 == 0
    copy = pltpu.make_async_copy
    for early, first_of, second_of, target, at in (
        ((q < 3) | (q == 7), n_early, n_late, n_own, 0),
        ((q < 2) | (q == 3) | (q == 6), o_early, o_late, n_other, 1),
    ):

        @pl.when(early)
        def _():
            copy(first_of, target, sems.at[at]).start()

        @pl.when(jnp.logical_not(early))
        def _():
            copy(second_of, target, sems.at[at]).start()

    size = a0.shape[0]
    moves = [
        copy(xy_hbm, xy, sems.at[2]),
        copy(w_first_hbm, w_first, sems.at[3]),
        copy(first_hbm, first, sems.at[4]),
        copy(tile_hbm, tile, sems.at[5]),
        copy(a0, w_rest.at[:size], sems.at[6]),
        copy(a1, w_rest.at[size : 2 * size], sems.at[7]),
        copy(a2, w_rest.at[2 * size : 3 * size], sems.at[8]),
        copy(a3, w_rest.at[3 * size :], sems.at[9]),
        copy(rest_hbm, rest, sems.at[10]),
    ]
    for move in moves:
        move.start()
    copy(n_early, n_own, sems.at[0]).wait()
    copy(o_early, n_other, sems.at[1]).wait()
    h0, l0 = halves(jnp.where(even, n_own[...], n_other[...]))
    h1, l1 = halves(jnp.where(even, n_other[...], n_own[...]))
    rows = first.shape[0]
    half = out.shape[1]
    block = half // 2
    moves[0].wait()
    n_high = jnp.concatenate([h0, h1], axis=1)
    n_low = jnp.concatenate([l0, l1], axis=1)
    hot = xy[...]
    high = dot(n_high, hot).astype(BF16)
    low = dot(n_low, hot).astype(BF16)
    for move in moves[1:4]:
        move.wait()
    new = first[...] - dot3((n_high, n_low), halves(w_first[...]))
    new = jnp.where(q < 2, tile[...], new)
    for t in range(rows // half):
        out[t, :, 0, :] = new[t * half : (t + 1) * half]
    for move in moves[4:]:
        move.wait()
    w = [halves(w_rest[:, u * B : (u + 1) * B]) for u in range(3)]
    sent = []
    for i in range(rows // block):
        t, at = i * block // half, i * block % half
        span = slice(i * block, (i + 1) * block)
        for u in range(1, 4):
            cols = slice((u - 1) * B, u * B)
            out[t, at : at + block, u, :] = rest[span, cols] - dot3((high[span], low[span]), w[u - 1])
        done = copy(out.at[t, at : at + block], out_hbm.at[t, at : at + block], sems.at[11 + i])
        done.start()
        sent.append(done)
    for done in sent:
        done.wait()


def call(kernel, outs, n_in, scalars=1, outs_in_smem=0, flops=0, moved=0):
    specs = jax.tree.map(lambda _: VM, outs)
    if outs_in_smem:
        specs = specs[:-outs_in_smem] + (SM,) * outs_in_smem
    return pl.pallas_call(
        kernel,
        out_shape=outs,
        in_specs=[SM] * scalars + [VM] * (n_in - scalars),
        out_specs=specs,
        cost_estimate=pl.CostEstimate(flops=flops, bytes_accessed=moved, transcendentals=0),
        **PARAMS,
    )


def shaped(*shape, dtype=F32):
    return jax.ShapeDtypeStruct(shape, dtype)


def core_swap(x):
    return lax.ppermute(x, "pcol", [(i, i ^ 1) for i in range(lax.axis_size("pcol"))])


def shift_x(step):
    return [(p, p // 4 * 4 + (p + step) % 4) for p in range(16)]


def shift_y(step):
    return [(p, (p + 4 * step) % 16) for p in range(16)]


def ring(x, shift):
    return [x] + [lax.ppermute(x, "prow", shift(step)) for step in (1, -1, 2)]


def spread_z(x, z):
    one = lax.ppermute(x, "pcol", [(0, 2), (1, 3)])
    three = lax.ppermute(x, "pcol", [(0, 6), (1, 7)])
    two = lax.ppermute(x, "pcol", [(0, 4), (1, 5)])
    return jnp.where(z == 0, x, jnp.where(z == 1, one, jnp.where(z == 2, two, three)))


def body(front, partials, targets, counts, local_picks, level_picks, order):
    rows = front.shape[0] * front.shape[1]
    cols = front.shape[2] * front.shape[3]
    p = lax.axis_index("prow")
    q = lax.axis_index("pcol")
    me = p * lax.axis_size("pcol") + q
    place = jnp.stack([p, q, me]).astype(jnp.int32)
    sources = partials.shape[1]
    slots = partials.shape[2]

    payload = pl.pallas_call(
        pack_kernel,
        out_shape=shaped(sources * 17, 128),
        in_specs=[SM, HBM, HBM, HBM],
        out_specs=HBM,
        scratch_shapes=[
            pltpu.VMEM((sources, slots, B), F32),
            pltpu.VMEM((slots, sources), jnp.int32),
            pltpu.VMEM((1, sources), jnp.int32),
            pltpu.VMEM((sources * 17, 128), F32),
            pltpu.SemaphoreType.DMA((6,)),
            pltpu.SemaphoreType.DMA((4,)),
        ],
        cost_estimate=pl.CostEstimate(flops=10**6, bytes_accessed=2 * 10**6, transcendentals=0),
        **ALONE,
    )(place, partials[0], targets[0].T, counts).reshape(sources * 17, 1, 128)
    payload = lax.all_to_all(payload, ("prow", "pcol"), 0, 0, tiled=True).reshape(sources * 17, 128)

    copies = lax.axis_size("prow") * KEEP
    hots = shaped(2 * B, copies, dtype=BF16)
    own, active, give, slot, xy, fits = call(
        index_kernel,
        (
            shaped(2 * B, 128, dtype=jnp.int32),
            shaped(2, rows, 128),
            shaped(KEEP, 128, dtype=jnp.int32),
            hots,
            hots,
            shaped(1, dtype=jnp.int32),
        ),
        4,
        outs_in_smem=1,
        flops=10**9,
        moved=10**6,
    )(place, local_picks, level_picks, order)
    front, own = lax.optimization_barrier((front, own))
    flat = front.reshape(rows, cols)
    share_rows = 2 * B // lax.axis_size("prow")

    front_rows = call(front_kernel, shaped(4 * KEEP, B), 2, scalars=0, flops=10**8, moved=3 * 10**6)(flat, give)

    send_first, send_rest = call(
        lead_kernel, (shaped(copies, B), shaped(KEEP, cols - B)), 3, scalars=0, flops=10**8, moved=2 * 10**6
    )(payload, front_rows, give)
    w_first = lax.all_to_all(send_first, "prow", 0, 0, tiled=True)
    first, rest, done = call(
        tiles_kernel,
        (shaped(rows, B), shaped(rows, cols - B), shaped(8, 128)),
        2,
        scalars=0,
        flops=4 * 10**9,
        moved=6 * 10**6,
    )(payload, flat)
    w_first, sorted_ = call(
        sort_first_kernel, (shaped(2 * B, B), shaped(8, 128)), 2, scalars=0, flops=10**8, moved=10**6
    )(slot, w_first)
    joined = call(join_kernel, shaped(4 * KEEP, cols - B), 6, scalars=0, moved=10**6)(
        done, sorted_, *ring(send_rest, shift_x)
    )
    w_parts = ring(joined, shift_y)

    def panels(w_first, first, active, place, joined):
        r_other = core_swap(first)
        w_other = core_swap(w_first)
        half, tile = call(
            panel_kernel, (shaped(rows, B), shaped(rows, B)), 6, flops=2 * 10**9, moved=4 * 10**6
        )(place, w_first, w_other, first, r_other, active)
        q = place[1]
        step = lax.ppermute(half, "pcol", [(0, 2), (1, 7)])
        n_early = jnp.where((q == 2) | (q == 7), step, half)
        n_late = lax.ppermute(n_early, "pcol", [(1, 3), (0, 6), (2, 4), (7, 5)])
        o_early = lax.ppermute(n_early, "pcol", [(0, 1), (1, 0), (2, 3), (7, 6)])
        o_late = lax.ppermute(n_late, "pcol", [(3, 2), (6, 7), (4, 5), (5, 4)])
        return n_early, n_late, o_early, o_late, tile

    def nothing(w_first, first, active, place, joined):
        return (jnp.zeros((rows, B), F32),) * 5

    parts = lax.cond(fits[0] == 1, panels, nothing, w_first, first, active, place, joined)

    def finish(payload, flat, own, active, place, *arrays):
        return pl.pallas_call(
            finish_kernel,
            out_shape=shaped(*front.shape),
            in_specs=[SM] + [HBM] * 13,
            out_specs=HBM,
            scratch_shapes=[
                pltpu.VMEM((rows, B), F32),
                pltpu.VMEM((rows, B), F32),
                pltpu.VMEM((rows, B), F32),
                pltpu.VMEM((2 * B, B), F32),
                pltpu.VMEM((rows, B), F32),
                pltpu.VMEM((rows, cols - B), F32),
                pltpu.VMEM((2 * B, copies), BF16),
                pltpu.VMEM((copies, cols - B), F32),
                pltpu.VMEM(front.shape, F32),
                pltpu.SemaphoreType.DMA((15,)),
            ],
            cost_estimate=pl.CostEstimate(flops=4 * 10**9, bytes_accessed=8 * 10**6, transcendentals=0),
            **ALONE,
        )(place, *arrays)

    def add_up(payload, flat, own, active, place, *arrays):
        matrix, pivots = call(
            assemble_kernel, (shaped(rows, cols), shaped(2 * B, cols)), 3, scalars=0, flops=4 * 10**9, moved=8 * 10**6
        )(payload, flat, own)
        r_own = matrix[:, :B]
        r_other = core_swap(r_own)
        share = lax.all_to_all(pivots, "prow", 0, 0, tiled=True).reshape(-1, share_rows, cols).sum(axis=0)
        pivots = lax.all_to_all(jnp.tile(share, (lax.axis_size("prow"), 1)), "prow", 0, 0, tiled=True)
        w_own = pivots[:, :B]
        w_other = core_swap(w_own)
        half, tile = call(
            panel_kernel, (shaped(rows, B), shaped(rows, B)), 6, flops=2 * 10**9, moved=4 * 10**6
        )(place, w_own, w_other, r_own, r_other, active)
        n_own = spread_z(half, place[1] // 2)
        n_other = core_swap(n_own)
        out = call(update_kernel, shaped(rows, cols), 6, flops=2 * 10**9, moved=8 * 10**6)(
            place, matrix, pivots, n_own, n_other, tile
        )
        return out.reshape(front.shape)

    return lax.cond(
        fits[0] == 1,
        finish,
        add_up,
        payload,
        flat,
        own,
        active,
        place,
        *parts,
        first,
        w_first,
        rest,
        xy,
        *w_parts,
    )


def solution(mesh):
    placed = (
        P(None, "prow", None, "pcol"),
        P(("prow", "pcol"), None, None, None),
        P(("prow", "pcol"), None, None),
        P(("prow", "pcol"), None),
        P(),
        P(),
        P(),
    )
    return jax.shard_map(
        body, mesh=mesh, in_specs=placed, out_specs=P(None, "prow", None, "pcol"), check_vma=False
    )
```

```python
import functools

import jax
import jax.numpy as jnp
from jax import lax
from jax.experimental import pallas as pl
from jax.experimental.pallas import tpu as pltpu
from jax.sharding import PartitionSpec as P

F32 = jnp.float32
BF16 = jnp.bfloat16
VM = pl.BlockSpec(memory_space=pltpu.VMEM)
HBM = pl.BlockSpec(memory_space=pltpu.HBM)
SM = pl.BlockSpec(memory_space=pltpu.SMEM)
B = 256
KEEP = 48
PARAMS = dict(compiler_params=pltpu.CompilerParams(vmem_limit_bytes=14 * 1024 * 1024))

ALONE = dict(compiler_params=pltpu.CompilerParams(vmem_limit_bytes=63 * 1024 * 1024))


def iota(shape, dim):
    return lax.broadcasted_iota(jnp.int32, shape, dim)


def dot(a, b):
    return jnp.dot(a, b, preferred_element_type=F32)


def halves(x):
    high = x.astype(BF16)
    return high, (x - high.astype(F32)).astype(BF16)


def dot3(a, b):
    ah, al = a
    bh, bl = b
    return dot(ah, bh) + (dot(ah, bl) + dot(al, bh))


def pick(onehot, x):
    high, low = halves(x)
    return dot(onehot, high) + dot(onehot, low)


def lookup(table, d, pos):
    n = pos.shape[1]
    hot = (iota((B, n), 0) == pos).astype(F32).astype(BF16)
    high = table // 256
    low = table - high * 256
    both = jnp.concatenate([high, low], axis=0).astype(F32).astype(BF16)
    got = dot(both, hot).astype(jnp.int32)
    rows = table.shape[0]
    values = got[:rows] * 256 + got[rows:]
    return jnp.sum(jnp.where(iota((rows, n), 0) == d, values, 0), axis=0, keepdims=True)


def turn(apart):
    apart = apart & 3
    return jnp.where(apart == 0, 0, jnp.where(apart == 1, 2, jnp.where(apart == 2, 3, 1)))


def index_kernel(place, local_picks, level_picks, order, own_out, active_out, give_out, slot_out, xy_out, fits_out):
    rows = active_out.shape[1]
    keep = give_out.shape[0]
    p = place[0]
    retired = jnp.zeros((rows, 1), F32)
    owners, locals_ = [], []
    for k in range(order.shape[0]):
        pos = order[k : k + 1, :]
        d = jnp.zeros_like(pos)
        for level in range(level_picks.shape[1] - 1, -1, -1):
            j = lookup(level_picks[k, level], d, pos)
            bit = 1 << level
            d = (d & ~bit) | jnp.where(j >= B, bit, 0)
            pos = j & (B - 1)
        r = lookup(local_picks[k], d, pos)
        own = jnp.where(d == p, r, -1)
        own_out[k * B : (k + 1) * B, :] = jnp.broadcast_to(own, (128, B)).T
        hit = (iota((rows, B), 0) == own).astype(F32)
        retired = jnp.maximum(retired, jnp.max(hit, axis=1, keepdims=True))
        active_out[k] = jnp.broadcast_to(1.0 - retired, (rows, 128))
        owners.append(d)
        locals_.append(r)
    d = jnp.concatenate(owners, axis=1)
    r = jnp.concatenate(locals_, axis=1)
    n = d.shape[1]
    d_col = jnp.broadcast_to(d, (128, n)).T[:, 0:1]
    before = (d_col == d) & (iota((n, n), 0) < iota((n, n), 1))
    rank = jnp.sum(before.astype(jnp.int32), axis=0, keepdims=True)
    fits_out[0] = (jnp.max(rank) < keep).astype(jnp.int32)
    slot_out[...] = rows_hot(jnp.broadcast_to(d * keep + rank, (128, n)).T, slot_out.shape[1])
    across = turn(d - p)
    down = turn((d >> 2) - (p >> 2))
    xy_out[...] = rows_hot(jnp.broadcast_to((down * 4 + across) * keep + rank, (128, n)).T, xy_out.shape[1])
    mine = (iota((keep, n), 0) == rank) & (d == p)
    give = jnp.sum(jnp.where(mine, r + 2, 0), axis=1, keepdims=True) - 2
    give_out[...] = jnp.broadcast_to(give, (keep, 128))


def pack_kernel(place, partials_hbm, targets_hbm, counts_hbm, out_hbm, partials, targets, counts, out, sems, out_sems):
    slots, sources = targets.shape
    parts = sems.shape[0] - 2
    step = sources // parts
    small = [
        pltpu.make_async_copy(targets_hbm, targets, sems.at[parts]),
        pltpu.make_async_copy(counts_hbm, counts, sems.at[parts + 1]),
    ]
    large = [
        pltpu.make_async_copy(
            partials_hbm.at[i * step : (i + 1) * step], partials.at[i * step : (i + 1) * step], sems.at[i]
        )
        for i in range(parts)
    ]
    for copy in small + large:
        copy.start()
    for copy in small:
        copy.wait()
    codes = jnp.where(iota((slots, sources), 0) < counts[...], targets[...], -1)
    codes = jnp.concatenate([codes] * (128 // slots), axis=0)
    codes = jnp.where(iota(codes.shape, 0) // slots == place[2] % (128 // slots), codes, 0)
    row = codes.astype(F32).T
    sent = []
    for i in range(parts):
        large[i].wait()
        for s in range(i * step, (i + 1) * step):
            out[17 * s : 17 * s + 8, :] = partials[s, :, :128]
            out[17 * s + 8 : 17 * s + 16, :] = partials[s, :, 128:]
            out[17 * s + 16 : 17 * s + 17, :] = row[s : s + 1, :]
        span = slice(17 * step * i, 17 * step * (i + 1))
        sent.append(pltpu.make_async_copy(out.at[span], out_hbm.at[span], out_sems.at[i]))
        sent[-1].start()
    for copy in sent:
        copy.wait()


def unpack(payload):
    sources = payload.shape[0] // 17
    left, right, codes = [], [], []
    for g in range(sources // 16):
        row = jnp.zeros((1, 128), F32)
        for s in range(16 * g, 16 * g + 16):
            left.append(payload[17 * s : 17 * s + 8, :])
            right.append(payload[17 * s + 8 : 17 * s + 16, :])
            row = row + payload[17 * s + 16 : 17 * s + 17, :]
        codes.append(row)
    values = jnp.concatenate([jnp.concatenate(left, axis=0), jnp.concatenate(right, axis=0)], axis=1)
    return halves(values), jnp.concatenate(codes, axis=1).astype(jnp.int32)


def hot_of(code, rows, u):
    return (code == iota((rows, code.shape[1]), 0) * 4 + u).astype(F32).astype(BF16)


def rows_hot(chosen, rows):
    return (chosen[:, 0:1] == iota((chosen.shape[0], rows), 1)).astype(F32).astype(BF16)


def assemble_kernel(payload, front, own, matrix_out, pivots_out):
    (high, low), code = unpack(payload)
    rows = front.shape[0]
    pivot_hot = rows_hot(own, rows)
    for u in range(4):
        cols = slice(u * B, (u + 1) * B)
        hot = hot_of(code, rows, u)
        tile = front[:, cols] + (dot(hot, high) + dot(hot, low))
        matrix_out[:, cols] = tile
        pivots_out[:, cols] = pick(pivot_hot, tile)


def front_kernel(front, give, out):
    keep = give.shape[0]
    hot = rows_hot(give, front.shape[0])
    for u in range(4):
        out[u * keep : (u + 1) * keep, :] = pick(hot, front[:, u * B : (u + 1) * B])


def lead_kernel(payload, front_rows, give, send_first, send_rest):
    (high, low), code = unpack(payload)
    keep = give.shape[0]
    chosen = give[:, 0:1] * 4
    hot = jnp.concatenate([(chosen + u == code).astype(F32) for u in range(4)], axis=0).astype(BF16)
    sums = front_rows[...] + (dot(hot, high) + dot(hot, low))
    for i in range(send_first.shape[0] // keep):
        send_first[i * keep : (i + 1) * keep, :] = sums[:keep]
    for u in range(1, 4):
        send_rest[:, (u - 1) * B : u * B] = sums[u * keep : (u + 1) * keep]


def tile_kernel(payload, front, first_out):
    (high, low), code = unpack(payload)
    hot = hot_of(code, front.shape[0], 0)
    first_out[...] = front[...] + (dot(hot, high) + dot(hot, low))


def tiles_kernel(payload, front, rest_out, done_out):
    done_out[...] = jnp.zeros_like(done_out)
    (high, low), code = unpack(payload)
    for u in range(1, 4):
        cols = slice(u * B, (u + 1) * B)
        hot = hot_of(code, front.shape[0], u)
        rest_out[:, cols.start - B : cols.stop - B] = front[:, cols] + (dot(hot, high) + dot(hot, low))


def join_kernel(r_done, tiles_done, sort_done, a0, a1, a2, a3, out):
    size = a0.shape[0]
    for i, a in enumerate((a0, a1, a2, a3)):
        out[i * size : (i + 1) * size, :] = a[...]


def sort_first_kernel(slot, gathered, out, done_out):
    done_out[...] = jnp.zeros_like(done_out)
    out[...] = pick(slot[...], gathered[...])


def inverse_of(diag):
    eye = iota((B, B), 0) == iota((B, B), 1)
    only = jnp.where(eye, diag, 0.0)
    by_row = 1.0 / jnp.sum(only, axis=1, keepdims=True)
    by_col = 1.0 / jnp.sum(only, axis=0, keepdims=True)
    two = jnp.where(eye, 2.0, 0.0)
    x = by_row * (two - diag * by_col)
    xs = halves(x)
    return dot3(xs, halves(two - dot3(halves(diag), xs)))


def panel_kernel(place, w_own, w_other, r_own, r_other, active, half_out, tile_out):
    even = place[1] % 2 == 0
    w0 = jnp.where(even, w_own[...], w_other[...])
    w1 = jnp.where(even, w_other[...], w_own[...])
    r0 = jnp.where(even, r_own[...], r_other[...])
    r1 = jnp.where(even, r_other[...], r_own[...])
    act0 = active[0][:, 0:1]
    act1 = active[1][:, 0:1]
    inv0 = halves(inverse_of(w0[:B]))
    m0w = dot3(halves(w0[B:]), inv0)
    m0w_s = halves(m0w)
    p01 = halves(w1[:B])
    inv1 = halves(inverse_of(w1[B:] - dot3(m0w_s, p01)))
    m0 = dot3(halves(r0), inv0)
    m0a = jnp.where(act0 > 0, m0, 0.0)
    r1 = r1 - dot3(halves(m0a), p01)
    m1 = dot3(halves(r1), inv1)
    n1 = jnp.where(act1 > 0, m1, 0.0)
    n0 = m0a - dot3(halves(n1), m0w_s)
    half_out[...] = jnp.where(even, n0, n1)
    tile_out[...] = jnp.where(even, jnp.where(act0 > 0, m0, r0), jnp.where(act1 > 0, m1, r1))


def update_kernel(place, matrix, pivots, n_own, n_other, tile, out):
    even = place[1] % 2 == 0
    n0 = halves(jnp.where(even, n_own[...], n_other[...]))
    n1 = halves(jnp.where(even, n_other[...], n_own[...]))
    for u in range(4):
        cols = slice(u * B, (u + 1) * B)
        new = matrix[:, cols] - (
            dot3(n0, halves(pivots[:B, cols])) + dot3(n1, halves(pivots[B:, cols]))
        )
        if u == 0:
            new = jnp.where(place[1] < 2, tile[...], new)
        out[:, cols] = new


def finish_kernel(
    place, n_early, n_late, o_early, o_late, tile_hbm, first_hbm, w_first_hbm, rest_hbm, xy_hbm,
    a0, a1, a2, a3, out_hbm, n_own, n_other, first, w_first, tile, rest, xy, w_rest, out, sems
):
    q = place[1]
    even = q % 2 == 0
    copy = pltpu.make_async_copy
    for early, first_of, second_of, target, at in (
        ((q < 3) | (q == 7), n_early, n_late, n_own, 0),
        ((q < 2) | (q == 3) | (q == 6), o_early, o_late, n_other, 1),
    ):

        @pl.when(early)
        def _():
            copy(first_of, target, sems.at[at]).start()

        @pl.when(jnp.logical_not(early))
        def _():
            copy(second_of, target, sems.at[at]).start()

    size = a0.shape[0]
    moves = [
        copy(xy_hbm, xy, sems.at[2]),
        copy(w_first_hbm, w_first, sems.at[3]),
        copy(first_hbm, first, sems.at[4]),
        copy(tile_hbm, tile, sems.at[5]),
        copy(a0, w_rest.at[:size], sems.at[6]),
        copy(a1, w_rest.at[size : 2 * size], sems.at[7]),
        copy(a2, w_rest.at[2 * size : 3 * size], sems.at[8]),
        copy(a3, w_rest.at[3 * size :], sems.at[9]),
        copy(rest_hbm, rest, sems.at[10]),
    ]
    for move in moves:
        move.start()
    copy(n_early, n_own, sems.at[0]).wait()
    copy(o_early, n_other, sems.at[1]).wait()
    h0, l0 = halves(jnp.where(even, n_own[...], n_other[...]))
    h1, l1 = halves(jnp.where(even, n_other[...], n_own[...]))
    rows = first.shape[0]
    half = out.shape[1]
    block = half // 2
    moves[0].wait()
    n_high = jnp.concatenate([h0, h1], axis=1)
    n_low = jnp.concatenate([l0, l1], axis=1)
    hot = xy[...]
    high = dot(n_high, hot).astype(BF16)
    low = dot(n_low, hot).astype(BF16)
    for move in moves[1:4]:
        move.wait()
    new = first[...] - dot3((n_high, n_low), halves(w_first[...]))
    new = jnp.where(q < 2, tile[...], new)
    for t in range(rows // half):
        out[t, :, 0, :] = new[t * half : (t + 1) * half]
    for move in moves[4:]:
        move.wait()
    w = [halves(w_rest[:, u * B : (u + 1) * B]) for u in range(3)]
    sent = []
    for i in range(rows // block):
        t, at = i * block // half, i * block % half
        span = slice(i * block, (i + 1) * block)
        for u in range(1, 4):
            cols = slice((u - 1) * B, u * B)
            out[t, at : at + block, u, :] = rest[span, cols] - dot3((high[span], low[span]), w[u - 1])
        done = copy(out.at[t, at : at + block], out_hbm.at[t, at : at + block], sems.at[11 + i])
        done.start()
        sent.append(done)
    for done in sent:
        done.wait()


def call(kernel, outs, n_in, scalars=1, outs_in_smem=0, flops=0, moved=0):
    specs = jax.tree.map(lambda _: VM, outs)
    if outs_in_smem:
        specs = specs[:-outs_in_smem] + (SM,) * outs_in_smem
    return pl.pallas_call(
        kernel,
        out_shape=outs,
        in_specs=[SM] * scalars + [VM] * (n_in - scalars),
        out_specs=specs,
        cost_estimate=pl.CostEstimate(flops=flops, bytes_accessed=moved, transcendentals=0),
        **PARAMS,
    )


def shaped(*shape, dtype=F32):
    return jax.ShapeDtypeStruct(shape, dtype)


def core_swap(x):
    return lax.ppermute(x, "pcol", [(i, i ^ 1) for i in range(lax.axis_size("pcol"))])


def shift_x(step):
    return [(p, p // 4 * 4 + (p + step) % 4) for p in range(16)]


def shift_y(step):
    return [(p, (p + 4 * step) % 16) for p in range(16)]


def ring(x, shift):
    return [x] + [lax.ppermute(x, "prow", shift(step)) for step in (1, -1, 2)]


def spread_z(x, z):
    one = lax.ppermute(x, "pcol", [(0, 2), (1, 3)])
    three = lax.ppermute(x, "pcol", [(0, 6), (1, 7)])
    two = lax.ppermute(x, "pcol", [(0, 4), (1, 5)])
    return jnp.where(z == 0, x, jnp.where(z == 1, one, jnp.where(z == 2, two, three)))


def body(front, partials, targets, counts, local_picks, level_picks, order):
    rows = front.shape[0] * front.shape[1]
    cols = front.shape[2] * front.shape[3]
    p = lax.axis_index("prow")
    q = lax.axis_index("pcol")
    me = p * lax.axis_size("pcol") + q
    place = jnp.stack([p, q, me]).astype(jnp.int32)
    sources = partials.shape[1]
    slots = partials.shape[2]

    payload = pl.pallas_call(
        pack_kernel,
        out_shape=shaped(sources * 17, 128),
        in_specs=[SM, HBM, HBM, HBM],
        out_specs=HBM,
        scratch_shapes=[
            pltpu.VMEM((sources, slots, B), F32),
            pltpu.VMEM((slots, sources), jnp.int32),
            pltpu.VMEM((1, sources), jnp.int32),
            pltpu.VMEM((sources * 17, 128), F32),
            pltpu.SemaphoreType.DMA((10,)),
            pltpu.SemaphoreType.DMA((8,)),
        ],
        cost_estimate=pl.CostEstimate(flops=10**6, bytes_accessed=2 * 10**6, transcendentals=0),
        **ALONE,
    )(place, partials[0], targets[0].T, counts).reshape(sources * 17, 1, 128)
    payload = lax.all_to_all(payload, ("prow", "pcol"), 0, 0, tiled=True).reshape(sources * 17, 128)

    copies = lax.axis_size("prow") * KEEP
    hots = shaped(2 * B, copies, dtype=BF16)
    own, active, give, slot, xy, fits = call(
        index_kernel,
        (
            shaped(2 * B, 128, dtype=jnp.int32),
            shaped(2, rows, 128),
            shaped(KEEP, 128, dtype=jnp.int32),
            hots,
            hots,
            shaped(1, dtype=jnp.int32),
        ),
        4,
        outs_in_smem=1,
        flops=10**9,
        moved=10**6,
    )(place, local_picks, level_picks, order)
    front, own = lax.optimization_barrier((front, own))
    flat = front.reshape(rows, cols)
    share_rows = 2 * B // lax.axis_size("prow")

    front_rows = call(front_kernel, shaped(4 * KEEP, B), 2, scalars=0, flops=10**8, moved=3 * 10**6)(flat, give)

    send_first, send_rest = call(
        lead_kernel, (shaped(copies, B), shaped(KEEP, cols - B)), 3, scalars=0, flops=10**8, moved=2 * 10**6
    )(payload, front_rows, give)
    w_first = lax.all_to_all(send_first, "prow", 0, 0, tiled=True)
    whole = lambda *shape: pl.BlockSpec(shape, lambda i: (0, 0))
    first = pl.pallas_call(
        tile_kernel,
        out_shape=shaped(rows, B),
        grid=(1,),
        in_specs=[whole(*payload.shape), whole(rows, B)],
        out_specs=whole(rows, B),
        cost_estimate=pl.CostEstimate(flops=10**9, bytes_accessed=2 * 10**6, transcendentals=0),
        **PARAMS,
    )(payload, flat)
    rest, done = call(
        tiles_kernel,
        (shaped(rows, cols - B), shaped(8, 128)),
        2,
        scalars=0,
        flops=4 * 10**9,
        moved=6 * 10**6,
    )(payload, flat)
    r_other = core_swap(first)
    w_first, sorted_ = call(
        sort_first_kernel, (shaped(2 * B, B), shaped(8, 128)), 2, scalars=0, flops=10**8, moved=10**6
    )(slot, w_first)
    joined = pl.pallas_call(
        join_kernel,
        out_shape=shaped(4 * KEEP, cols - B),
        grid=(1,),
        in_specs=[whole(8, 128)] * 3 + [whole(KEEP, cols - B)] * 4,
        out_specs=whole(4 * KEEP, cols - B),
        cost_estimate=pl.CostEstimate(flops=0, bytes_accessed=10**6, transcendentals=0),
        **PARAMS,
    )(r_other, done, sorted_, *ring(send_rest, shift_x))
    w_parts = ring(joined, shift_y)

    def panels(w_first, first, r_other, active, place, joined):
        w_other = core_swap(w_first)
        half, tile = call(
            panel_kernel, (shaped(rows, B), shaped(rows, B)), 6, flops=2 * 10**9, moved=4 * 10**6
        )(place, w_first, w_other, first, r_other, active)
        q = place[1]
        step = lax.ppermute(half, "pcol", [(0, 2), (1, 7)])
        n_early = jnp.where((q == 2) | (q == 7), step, half)
        n_late = lax.ppermute(n_early, "pcol", [(1, 3), (0, 6), (2, 4), (7, 5)])
        o_early = lax.ppermute(n_early, "pcol", [(0, 1), (1, 0), (2, 3), (7, 6)])
        o_late = lax.ppermute(n_late, "pcol", [(3, 2), (6, 7), (4, 5), (5, 4)])
        return n_early, n_late, o_early, o_late, tile

    def nothing(w_first, first, r_other, active, place, joined):
        return (jnp.zeros((rows, B), F32),) * 5

    parts = lax.cond(fits[0] == 1, panels, nothing, w_first, first, r_other, active, place, joined)

    def finish(payload, flat, own, active, place, *arrays):
        return pl.pallas_call(
            finish_kernel,
            out_shape=shaped(*front.shape),
            in_specs=[SM] + [HBM] * 13,
            out_specs=HBM,
            scratch_shapes=[
                pltpu.VMEM((rows, B), F32),
                pltpu.VMEM((rows, B), F32),
                pltpu.VMEM((rows, B), F32),
                pltpu.VMEM((2 * B, B), F32),
                pltpu.VMEM((rows, B), F32),
                pltpu.VMEM((rows, cols - B), F32),
                pltpu.VMEM((2 * B, copies), BF16),
                pltpu.VMEM((copies, cols - B), F32),
                pltpu.VMEM(front.shape, F32),
                pltpu.SemaphoreType.DMA((15,)),
            ],
            cost_estimate=pl.CostEstimate(flops=4 * 10**9, bytes_accessed=8 * 10**6, transcendentals=0),
            **ALONE,
        )(place, *arrays)

    def add_up(payload, flat, own, active, place, *arrays):
        matrix, pivots = call(
            assemble_kernel, (shaped(rows, cols), shaped(2 * B, cols)), 3, scalars=0, flops=4 * 10**9, moved=8 * 10**6
        )(payload, flat, own)
        r_own = matrix[:, :B]
        r_other = core_swap(r_own)
        share = lax.all_to_all(pivots, "prow", 0, 0, tiled=True).reshape(-1, share_rows, cols).sum(axis=0)
        pivots = lax.all_to_all(jnp.tile(share, (lax.axis_size("prow"), 1)), "prow", 0, 0, tiled=True)
        w_own = pivots[:, :B]
        w_other = core_swap(w_own)
        half, tile = call(
            panel_kernel, (shaped(rows, B), shaped(rows, B)), 6, flops=2 * 10**9, moved=4 * 10**6
        )(place, w_own, w_other, r_own, r_other, active)
        n_own = spread_z(half, place[1] // 2)
        n_other = core_swap(n_own)
        out = call(update_kernel, shaped(rows, cols), 6, flops=2 * 10**9, moved=8 * 10**6)(
            place, matrix, pivots, n_own, n_other, tile
        )
        return out.reshape(front.shape)

    return lax.cond(
        fits[0] == 1,
        finish,
        add_up,
        payload,
        flat,
        own,
        active,
        place,
        *parts,
        first,
        w_first,
        rest,
        xy,
        *w_parts,
    )


def solution(mesh):
    placed = (
        P(None, "prow", None, "pcol"),
        P(("prow", "pcol"), None, None, None),
        P(("prow", "pcol"), None, None),
        P(("prow", "pcol"), None),
        P(),
        P(),
        P(),
    )
    return jax.shard_map(
        body, mesh=mesh, in_specs=placed, out_specs=P(None, "prow", None, "pcol"), check_vma=False
    )
```

```python
import functools

import jax
import jax.numpy as jnp
from jax import lax
from jax.experimental import pallas as pl
from jax.experimental.pallas import tpu as pltpu
from jax.sharding import PartitionSpec as P

F32 = jnp.float32
BF16 = jnp.bfloat16
VM = pl.BlockSpec(memory_space=pltpu.VMEM)
HBM = pl.BlockSpec(memory_space=pltpu.HBM)
SM = pl.BlockSpec(memory_space=pltpu.SMEM)
B = 256
KEEP = 48
PARAMS = dict(compiler_params=pltpu.CompilerParams(vmem_limit_bytes=14 * 1024 * 1024))

ALONE = dict(compiler_params=pltpu.CompilerParams(vmem_limit_bytes=63 * 1024 * 1024))


def iota(shape, dim):
    return lax.broadcasted_iota(jnp.int32, shape, dim)


def dot(a, b):
    return jnp.dot(a, b, preferred_element_type=F32)


def halves(x):
    high = x.astype(BF16)
    return high, (x - high.astype(F32)).astype(BF16)


def dot3(a, b):
    ah, al = a
    bh, bl = b
    return dot(ah, bh) + (dot(ah, bl) + dot(al, bh))


def pick(onehot, x):
    high, low = halves(x)
    return dot(onehot, high) + dot(onehot, low)


def lookup(table, d, pos):
    n = pos.shape[1]
    hot = (iota((B, n), 0) == pos).astype(F32).astype(BF16)
    high = table // 256
    low = table - high * 256
    both = jnp.concatenate([high, low], axis=0).astype(F32).astype(BF16)
    got = dot(both, hot).astype(jnp.int32)
    rows = table.shape[0]
    values = got[:rows] * 256 + got[rows:]
    return jnp.sum(jnp.where(iota((rows, n), 0) == d, values, 0), axis=0, keepdims=True)


def turn(apart):
    apart = apart & 3
    return jnp.where(apart == 0, 0, jnp.where(apart == 1, 2, jnp.where(apart == 2, 3, 1)))


def index_kernel(place, local_picks, level_picks, order, own_out, active_out, give_out, slot_out, xy_out, fits_out):
    rows = active_out.shape[1]
    keep = give_out.shape[0]
    p = place[0]
    retired = jnp.zeros((rows, 1), F32)
    owners, locals_ = [], []
    for k in range(order.shape[0]):
        pos = order[k : k + 1, :]
        d = jnp.zeros_like(pos)
        for level in range(level_picks.shape[1] - 1, -1, -1):
            j = lookup(level_picks[k, level], d, pos)
            bit = 1 << level
            d = (d & ~bit) | jnp.where(j >= B, bit, 0)
            pos = j & (B - 1)
        r = lookup(local_picks[k], d, pos)
        own = jnp.where(d == p, r, -1)
        own_out[k * B : (k + 1) * B, :] = jnp.broadcast_to(own, (128, B)).T
        hit = (iota((rows, B), 0) == own).astype(F32)
        retired = jnp.maximum(retired, jnp.max(hit, axis=1, keepdims=True))
        active_out[k] = jnp.broadcast_to(1.0 - retired, (rows, 128))
        owners.append(d)
        locals_.append(r)
    d = jnp.concatenate(owners, axis=1)
    r = jnp.concatenate(locals_, axis=1)
    n = d.shape[1]
    d_col = jnp.broadcast_to(d, (128, n)).T[:, 0:1]
    before = (d_col == d) & (iota((n, n), 0) < iota((n, n), 1))
    rank = jnp.sum(before.astype(jnp.int32), axis=0, keepdims=True)
    fits_out[0] = (jnp.max(rank) < keep).astype(jnp.int32)
    slot_out[...] = rows_hot(jnp.broadcast_to(d * keep + rank, (128, n)).T, slot_out.shape[1])
    across = turn(d - p)
    down = turn((d >> 2) - (p >> 2))
    xy_out[...] = rows_hot(jnp.broadcast_to((down * 4 + across) * keep + rank, (128, n)).T, xy_out.shape[1])
    mine = (iota((keep, n), 0) == rank) & (d == p)
    give = jnp.sum(jnp.where(mine, r + 2, 0), axis=1, keepdims=True) - 2
    give_out[...] = jnp.broadcast_to(give, (keep, 128))


def pack_kernel(place, partials_hbm, targets_hbm, counts_hbm, out_hbm, partials, targets, counts, out, sems, out_sems):
    slots, sources = targets.shape
    parts = sems.shape[0] - 2
    step = sources // parts
    small = [
        pltpu.make_async_copy(targets_hbm, targets, sems.at[parts]),
        pltpu.make_async_copy(counts_hbm, counts, sems.at[parts + 1]),
    ]
    large = [
        pltpu.make_async_copy(
            partials_hbm.at[i * step : (i + 1) * step], partials.at[i * step : (i + 1) * step], sems.at[i]
        )
        for i in range(parts)
    ]
    for copy in small + large:
        copy.start()
    for copy in small:
        copy.wait()
    codes = jnp.where(iota((slots, sources), 0) < counts[...], targets[...], -1)
    codes = jnp.concatenate([codes] * (128 // slots), axis=0)
    codes = jnp.where(iota(codes.shape, 0) // slots == place[2] % (128 // slots), codes, 0)
    row = codes.astype(F32).T
    sent = []
    for i in range(parts):
        large[i].wait()
        for s in range(i * step, (i + 1) * step):
            out[17 * s : 17 * s + 8, :] = partials[s, :, :128]
            out[17 * s + 8 : 17 * s + 16, :] = partials[s, :, 128:]
            out[17 * s + 16 : 17 * s + 17, :] = row[s : s + 1, :]
        span = slice(17 * step * i, 17 * step * (i + 1))
        sent.append(pltpu.make_async_copy(out.at[span], out_hbm.at[span], out_sems.at[i]))
        sent[-1].start()
    for copy in sent:
        copy.wait()


def unpack(payload):
    sources = payload.shape[0] // 17
    left, right, codes = [], [], []
    for g in range(sources // 16):
        row = jnp.zeros((1, 128), F32)
        for s in range(16 * g, 16 * g + 16):
            left.append(payload[17 * s : 17 * s + 8, :])
            right.append(payload[17 * s + 8 : 17 * s + 16, :])
            row = row + payload[17 * s + 16 : 17 * s + 17, :]
        codes.append(row)
    values = jnp.concatenate([jnp.concatenate(left, axis=0), jnp.concatenate(right, axis=0)], axis=1)
    return halves(values), jnp.concatenate(codes, axis=1).astype(jnp.int32)


def hot_of(code, rows, u):
    return (code == iota((rows, code.shape[1]), 0) * 4 + u).astype(F32).astype(BF16)


def rows_hot(chosen, rows):
    return (chosen[:, 0:1] == iota((chosen.shape[0], rows), 1)).astype(F32).astype(BF16)


def assemble_kernel(payload, front, own, matrix_out, pivots_out):
    (high, low), code = unpack(payload)
    rows = front.shape[0]
    pivot_hot = rows_hot(own, rows)
    for u in range(4):
        cols = slice(u * B, (u + 1) * B)
        hot = hot_of(code, rows, u)
        tile = front[:, cols] + (dot(hot, high) + dot(hot, low))
        matrix_out[:, cols] = tile
        pivots_out[:, cols] = pick(pivot_hot, tile)


def front_kernel(front, give, out):
    keep = give.shape[0]
    hot = rows_hot(give, front.shape[0])
    for u in range(4):
        out[u * keep : (u + 1) * keep, :] = pick(hot, front[:, u * B : (u + 1) * B])


def lead_kernel(payload, front_rows, give, send_first, send_rest):
    (high, low), code = unpack(payload)
    keep = give.shape[0]
    chosen = give[:, 0:1] * 4
    hot = jnp.concatenate([(chosen + u == code).astype(F32) for u in range(4)], axis=0).astype(BF16)
    sums = front_rows[...] + (dot(hot, high) + dot(hot, low))
    for i in range(send_first.shape[0] // keep):
        send_first[i * keep : (i + 1) * keep, :] = sums[:keep]
    for u in range(1, 4):
        send_rest[:, (u - 1) * B : u * B] = sums[u * keep : (u + 1) * keep]


def tile_kernel(payload, front, first_out):
    (high, low), code = unpack(payload)
    hot = hot_of(code, front.shape[0], 0)
    first_out[...] = front[...] + (dot(hot, high) + dot(hot, low))


def tiles_kernel(payload, front, rest_out, done_out):
    done_out[...] = jnp.zeros_like(done_out)
    (high, low), code = unpack(payload)
    for u in range(1, 4):
        cols = slice(u * B, (u + 1) * B)
        hot = hot_of(code, front.shape[0], u)
        rest_out[:, cols.start - B : cols.stop - B] = front[:, cols] + (dot(hot, high) + dot(hot, low))


def join_kernel(tiles_done, sort_done, a0, a1, a2, a3, out):
    size = a0.shape[0]
    for i, a in enumerate((a0, a1, a2, a3)):
        out[i * size : (i + 1) * size, :] = a[...]


def sort_first_kernel(r_done, slot, gathered, out, done_out):
    done_out[...] = jnp.zeros_like(done_out)
    out[...] = pick(slot[...], gathered[...])


def inverse_of(diag):
    eye = iota((B, B), 0) == iota((B, B), 1)
    only = jnp.where(eye, diag, 0.0)
    by_row = 1.0 / jnp.sum(only, axis=1, keepdims=True)
    by_col = 1.0 / jnp.sum(only, axis=0, keepdims=True)
    two = jnp.where(eye, 2.0, 0.0)
    x = by_row * (two - diag * by_col)
    xs = halves(x)
    return dot3(xs, halves(two - dot3(halves(diag), xs)))


def panel_kernel(place, w_own, w_other, r_own, r_other, active, half_out, tile_out):
    even = place[1] % 2 == 0
    w0 = jnp.where(even, w_own[...], w_other[...])
    w1 = jnp.where(even, w_other[...], w_own[...])
    r0 = jnp.where(even, r_own[...], r_other[...])
    r1 = jnp.where(even, r_other[...], r_own[...])
    act0 = active[0][:, 0:1]
    act1 = active[1][:, 0:1]
    inv0 = halves(inverse_of(w0[:B]))
    m0w = dot3(halves(w0[B:]), inv0)
    m0w_s = halves(m0w)
    p01 = halves(w1[:B])
    inv1 = halves(inverse_of(w1[B:] - dot3(m0w_s, p01)))
    m0 = dot3(halves(r0), inv0)
    m0a = jnp.where(act0 > 0, m0, 0.0)
    r1 = r1 - dot3(halves(m0a), p01)
    m1 = dot3(halves(r1), inv1)
    n1 = jnp.where(act1 > 0, m1, 0.0)
    n0 = m0a - dot3(halves(n1), m0w_s)
    half_out[...] = jnp.where(even, n0, n1)
    tile_out[...] = jnp.where(even, jnp.where(act0 > 0, m0, r0), jnp.where(act1 > 0, m1, r1))


def update_kernel(place, matrix, pivots, n_own, n_other, tile, out):
    even = place[1] % 2 == 0
    n0 = halves(jnp.where(even, n_own[...], n_other[...]))
    n1 = halves(jnp.where(even, n_other[...], n_own[...]))
    for u in range(4):
        cols = slice(u * B, (u + 1) * B)
        new = matrix[:, cols] - (
            dot3(n0, halves(pivots[:B, cols])) + dot3(n1, halves(pivots[B:, cols]))
        )
        if u == 0:
            new = jnp.where(place[1] < 2, tile[...], new)
        out[:, cols] = new


def finish_kernel(
    place, n_early, n_late, o_early, o_late, tile_hbm, first_hbm, w_first_hbm, rest_hbm, xy_hbm,
    a0, a1, a2, a3, out_hbm, n_own, n_other, first, w_first, tile, rest, xy, w_rest, out, sems
):
    q = place[1]
    even = q % 2 == 0
    copy = pltpu.make_async_copy
    for early, first_of, second_of, target, at in (
        ((q < 3) | (q == 7), n_early, n_late, n_own, 0),
        ((q < 2) | (q == 3) | (q == 6), o_early, o_late, n_other, 1),
    ):

        @pl.when(early)
        def _():
            copy(first_of, target, sems.at[at]).start()

        @pl.when(jnp.logical_not(early))
        def _():
            copy(second_of, target, sems.at[at]).start()

    size = a0.shape[0]
    moves = [
        copy(xy_hbm, xy, sems.at[2]),
        copy(w_first_hbm, w_first, sems.at[3]),
        copy(first_hbm, first, sems.at[4]),
        copy(tile_hbm, tile, sems.at[5]),
        copy(a0, w_rest.at[:size], sems.at[6]),
        copy(a1, w_rest.at[size : 2 * size], sems.at[7]),
        copy(a2, w_rest.at[2 * size : 3 * size], sems.at[8]),
        copy(a3, w_rest.at[3 * size :], sems.at[9]),
        copy(rest_hbm, rest, sems.at[10]),
    ]
    for move in moves:
        move.start()
    copy(n_early, n_own, sems.at[0]).wait()
    copy(o_early, n_other, sems.at[1]).wait()
    h0, l0 = halves(jnp.where(even, n_own[...], n_other[...]))
    h1, l1 = halves(jnp.where(even, n_other[...], n_own[...]))
    rows = first.shape[0]
    half = out.shape[1]
    block = half // 2
    moves[0].wait()
    n_high = jnp.concatenate([h0, h1], axis=1)
    n_low = jnp.concatenate([l0, l1], axis=1)
    hot = xy[...]
    high = dot(n_high, hot).astype(BF16)
    low = dot(n_low, hot).astype(BF16)
    for move in moves[1:4]:
        move.wait()
    new = first[...] - dot3((n_high, n_low), halves(w_first[...]))
    new = jnp.where(q < 2, tile[...], new)
    for t in range(rows // half):
        out[t, :, 0, :] = new[t * half : (t + 1) * half]
    for move in moves[4:]:
        move.wait()
    w = [halves(w_rest[:, u * B : (u + 1) * B]) for u in range(3)]
    sent = []
    for i in range(rows // block):
        t, at = i * block // half, i * block % half
        span = slice(i * block, (i + 1) * block)
        for u in range(1, 4):
            cols = slice((u - 1) * B, u * B)
            out[t, at : at + block, u, :] = rest[span, cols] - dot3((high[span], low[span]), w[u - 1])
        done = copy(out.at[t, at : at + block], out_hbm.at[t, at : at + block], sems.at[11 + i])
        done.start()
        sent.append(done)
    for done in sent:
        done.wait()


def call(kernel, outs, n_in, scalars=1, outs_in_smem=0, flops=0, moved=0):
    specs = jax.tree.map(lambda _: VM, outs)
    if outs_in_smem:
        specs = specs[:-outs_in_smem] + (SM,) * outs_in_smem
    return pl.pallas_call(
        kernel,
        out_shape=outs,
        in_specs=[SM] * scalars + [VM] * (n_in - scalars),
        out_specs=specs,
        cost_estimate=pl.CostEstimate(flops=flops, bytes_accessed=moved, transcendentals=0),
        **PARAMS,
    )


def shaped(*shape, dtype=F32):
    return jax.ShapeDtypeStruct(shape, dtype)


def core_swap(x):
    return lax.ppermute(x, "pcol", [(i, i ^ 1) for i in range(lax.axis_size("pcol"))])


def shift_x(step):
    return [(p, p // 4 * 4 + (p + step) % 4) for p in range(16)]


def shift_y(step):
    return [(p, (p + 4 * step) % 16) for p in range(16)]


def ring(x, shift):
    return [x] + [lax.ppermute(x, "prow", shift(step)) for step in (1, -1, 2)]


def spread_z(x, z):
    one = lax.ppermute(x, "pcol", [(0, 2), (1, 3)])
    three = lax.ppermute(x, "pcol", [(0, 6), (1, 7)])
    two = lax.ppermute(x, "pcol", [(0, 4), (1, 5)])
    return jnp.where(z == 0, x, jnp.where(z == 1, one, jnp.where(z == 2, two, three)))


def body(front, partials, targets, counts, local_picks, level_picks, order):
    rows = front.shape[0] * front.shape[1]
    cols = front.shape[2] * front.shape[3]
    p = lax.axis_index("prow")
    q = lax.axis_index("pcol")
    me = p * lax.axis_size("pcol") + q
    place = jnp.stack([p, q, me]).astype(jnp.int32)
    sources = partials.shape[1]
    slots = partials.shape[2]

    payload = pl.pallas_call(
        pack_kernel,
        out_shape=shaped(sources * 17, 128),
        in_specs=[SM, HBM, HBM, HBM],
        out_specs=HBM,
        scratch_shapes=[
            pltpu.VMEM((sources, slots, B), F32),
            pltpu.VMEM((slots, sources), jnp.int32),
            pltpu.VMEM((1, sources), jnp.int32),
            pltpu.VMEM((sources * 17, 128), F32),
            pltpu.SemaphoreType.DMA((10,)),
            pltpu.SemaphoreType.DMA((8,)),
        ],
        cost_estimate=pl.CostEstimate(flops=10**6, bytes_accessed=2 * 10**6, transcendentals=0),
        **ALONE,
    )(place, partials[0], targets[0].T, counts).reshape(sources * 17, 1, 128)
    payload = lax.all_to_all(payload, ("prow", "pcol"), 0, 0, tiled=True).reshape(sources * 17, 128)

    copies = lax.axis_size("prow") * KEEP
    hots = shaped(2 * B, copies, dtype=BF16)
    own, active, give, slot, xy, fits = call(
        index_kernel,
        (
            shaped(2 * B, 128, dtype=jnp.int32),
            shaped(2, rows, 128),
            shaped(KEEP, 128, dtype=jnp.int32),
            hots,
            hots,
            shaped(1, dtype=jnp.int32),
        ),
        4,
        outs_in_smem=1,
        flops=10**9,
        moved=10**6,
    )(place, local_picks, level_picks, order)
    front, own = lax.optimization_barrier((front, own))
    flat = front.reshape(rows, cols)
    share_rows = 2 * B // lax.axis_size("prow")

    front_rows = call(front_kernel, shaped(4 * KEEP, B), 2, scalars=0, flops=10**8, moved=3 * 10**6)(flat, give)

    send_first, send_rest = call(
        lead_kernel, (shaped(copies, B), shaped(KEEP, cols - B)), 3, scalars=0, flops=10**8, moved=2 * 10**6
    )(payload, front_rows, give)
    w_first = lax.all_to_all(send_first, "prow", 0, 0, tiled=True)
    whole = lambda *shape: pl.BlockSpec(shape, lambda i: (0, 0))
    first = pl.pallas_call(
        tile_kernel,
        out_shape=shaped(rows, B),
        grid=(1,),
        in_specs=[whole(*payload.shape), whole(rows, B)],
        out_specs=whole(rows, B),
        cost_estimate=pl.CostEstimate(flops=10**9, bytes_accessed=2 * 10**6, transcendentals=0),
        **PARAMS,
    )(payload, flat)
    r_other = core_swap(first)
    rest, done = call(
        tiles_kernel,
        (shaped(rows, cols - B), shaped(8, 128)),
        2,
        scalars=0,
        flops=4 * 10**9,
        moved=6 * 10**6,
    )(payload, flat)
    w_first, sorted_ = call(
        sort_first_kernel, (shaped(2 * B, B), shaped(8, 128)), 3, scalars=0, flops=10**8, moved=10**6
    )(r_other, slot, w_first)
    joined = call(join_kernel, shaped(4 * KEEP, cols - B), 6, scalars=0, moved=10**6)(
        done, sorted_, *ring(send_rest, shift_x)
    )
    w_parts = ring(joined, shift_y)

    def panels(w_first, first, r_other, active, place, joined):
        w_other = core_swap(w_first)
        half, tile = call(
            panel_kernel, (shaped(rows, B), shaped(rows, B)), 6, flops=2 * 10**9, moved=4 * 10**6
        )(place, w_first, w_other, first, r_other, active)
        q = place[1]
        step = lax.ppermute(half, "pcol", [(0, 2), (1, 7)])
        n_early = jnp.where((q == 2) | (q == 7), step, half)
        n_late = lax.ppermute(n_early, "pcol", [(1, 3), (0, 6), (2, 4), (7, 5)])
        o_early = lax.ppermute(n_early, "pcol", [(0, 1), (1, 0), (2, 3), (7, 6)])
        o_late = lax.ppermute(n_late, "pcol", [(3, 2), (6, 7), (4, 5), (5, 4)])
        return n_early, n_late, o_early, o_late, tile

    def nothing(w_first, first, r_other, active, place, joined):
        return (jnp.zeros((rows, B), F32),) * 5

    parts = lax.cond(fits[0] == 1, panels, nothing, w_first, first, r_other, active, place, joined)

    def finish(payload, flat, own, active, place, *arrays):
        return pl.pallas_call(
            finish_kernel,
            out_shape=shaped(*front.shape),
            in_specs=[SM] + [HBM] * 13,
            out_specs=HBM,
            scratch_shapes=[
                pltpu.VMEM((rows, B), F32),
                pltpu.VMEM((rows, B), F32),
                pltpu.VMEM((rows, B), F32),
                pltpu.VMEM((2 * B, B), F32),
                pltpu.VMEM((rows, B), F32),
                pltpu.VMEM((rows, cols - B), F32),
                pltpu.VMEM((2 * B, copies), BF16),
                pltpu.VMEM((copies, cols - B), F32),
                pltpu.VMEM(front.shape, F32),
                pltpu.SemaphoreType.DMA((15,)),
            ],
            cost_estimate=pl.CostEstimate(flops=4 * 10**9, bytes_accessed=8 * 10**6, transcendentals=0),
            **ALONE,
        )(place, *arrays)

    def add_up(payload, flat, own, active, place, *arrays):
        matrix, pivots = call(
            assemble_kernel, (shaped(rows, cols), shaped(2 * B, cols)), 3, scalars=0, flops=4 * 10**9, moved=8 * 10**6
        )(payload, flat, own)
        r_own = matrix[:, :B]
        r_other = core_swap(r_own)
        share = lax.all_to_all(pivots, "prow", 0, 0, tiled=True).reshape(-1, share_rows, cols).sum(axis=0)
        pivots = lax.all_to_all(jnp.tile(share, (lax.axis_size("prow"), 1)), "prow", 0, 0, tiled=True)
        w_own = pivots[:, :B]
        w_other = core_swap(w_own)
        half, tile = call(
            panel_kernel, (shaped(rows, B), shaped(rows, B)), 6, flops=2 * 10**9, moved=4 * 10**6
        )(place, w_own, w_other, r_own, r_other, active)
        n_own = spread_z(half, place[1] // 2)
        n_other = core_swap(n_own)
        out = call(update_kernel, shaped(rows, cols), 6, flops=2 * 10**9, moved=8 * 10**6)(
            place, matrix, pivots, n_own, n_other, tile
        )
        return out.reshape(front.shape)

    return lax.cond(
        fits[0] == 1,
        finish,
        add_up,
        payload,
        flat,
        own,
        active,
        place,
        *parts,
        first,
        w_first,
        rest,
        xy,
        *w_parts,
    )


def solution(mesh):
    placed = (
        P(None, "prow", None, "pcol"),
        P(("prow", "pcol"), None, None, None),
        P(("prow", "pcol"), None, None),
        P(("prow", "pcol"), None),
        P(),
        P(),
        P(),
    )
    return jax.shard_map(
        body, mesh=mesh, in_specs=placed, out_specs=P(None, "prow", None, "pcol"), check_vma=False
    )
```

```python
import functools

import jax
import jax.numpy as jnp
from jax import lax
from jax.experimental import pallas as pl
from jax.experimental.pallas import tpu as pltpu
from jax.sharding import PartitionSpec as P

F32 = jnp.float32
BF16 = jnp.bfloat16
VM = pl.BlockSpec(memory_space=pltpu.VMEM)
HBM = pl.BlockSpec(memory_space=pltpu.HBM)
SM = pl.BlockSpec(memory_space=pltpu.SMEM)
B = 256
KEEP = 48
PARAMS = dict(compiler_params=pltpu.CompilerParams(vmem_limit_bytes=14 * 1024 * 1024))

ALONE = dict(compiler_params=pltpu.CompilerParams(vmem_limit_bytes=63 * 1024 * 1024))


def iota(shape, dim):
    return lax.broadcasted_iota(jnp.int32, shape, dim)


def dot(a, b):
    return jnp.dot(a, b, preferred_element_type=F32)


def halves(x):
    high = x.astype(BF16)
    return high, (x - high.astype(F32)).astype(BF16)


def dot3(a, b):
    ah, al = a
    bh, bl = b
    return dot(ah, bh) + (dot(ah, bl) + dot(al, bh))


def pick(onehot, x):
    high, low = halves(x)
    return dot(onehot, high) + dot(onehot, low)


def lookup(table, d, pos):
    n = pos.shape[1]
    hot = (iota((B, n), 0) == pos).astype(F32).astype(BF16)
    high = table // 256
    low = table - high * 256
    both = jnp.concatenate([high, low], axis=0).astype(F32).astype(BF16)
    got = dot(both, hot).astype(jnp.int32)
    rows = table.shape[0]
    values = got[:rows] * 256 + got[rows:]
    return jnp.sum(jnp.where(iota((rows, n), 0) == d, values, 0), axis=0, keepdims=True)


def turn(apart):
    apart = apart & 3
    return jnp.where(apart == 0, 0, jnp.where(apart == 1, 2, jnp.where(apart == 2, 3, 1)))


def index_kernel(place, local_picks, level_picks, order, own_out, active_out, give_out, slot_out, xy_out, fits_out):
    rows = active_out.shape[1]
    keep = give_out.shape[0]
    p = place[0]
    retired = jnp.zeros((rows, 1), F32)
    owners, locals_ = [], []
    for k in range(order.shape[0]):
        pos = order[k : k + 1, :]
        d = jnp.zeros_like(pos)
        for level in range(level_picks.shape[1] - 1, -1, -1):
            j = lookup(level_picks[k, level], d, pos)
            bit = 1 << level
            d = (d & ~bit) | jnp.where(j >= B, bit, 0)
            pos = j & (B - 1)
        r = lookup(local_picks[k], d, pos)
        own = jnp.where(d == p, r, -1)
        own_out[k * B : (k + 1) * B, :] = jnp.broadcast_to(own, (128, B)).T
        hit = (iota((rows, B), 0) == own).astype(F32)
        retired = jnp.maximum(retired, jnp.max(hit, axis=1, keepdims=True))
        active_out[k] = jnp.broadcast_to(1.0 - retired, (rows, 128))
        owners.append(d)
        locals_.append(r)
    d = jnp.concatenate(owners, axis=1)
    r = jnp.concatenate(locals_, axis=1)
    n = d.shape[1]
    d_col = jnp.broadcast_to(d, (128, n)).T[:, 0:1]
    before = (d_col == d) & (iota((n, n), 0) < iota((n, n), 1))
    rank = jnp.sum(before.astype(jnp.int32), axis=0, keepdims=True)
    fits_out[0] = (jnp.max(rank) < keep).astype(jnp.int32)
    slot_out[...] = rows_hot(jnp.broadcast_to(d * keep + rank, (128, n)).T, slot_out.shape[1])
    across = turn(d - p)
    down = turn((d >> 2) - (p >> 2))
    xy_out[...] = rows_hot(jnp.broadcast_to((down * 4 + across) * keep + rank, (128, n)).T, xy_out.shape[1])
    mine = (iota((keep, n), 0) == rank) & (d == p)
    give = jnp.sum(jnp.where(mine, r + 2, 0), axis=1, keepdims=True) - 2
    give_out[...] = jnp.broadcast_to(give, (keep, 128))


def pack_kernel(place, partials_hbm, targets_hbm, counts_hbm, out_hbm, partials, targets, counts, out, sems, out_sems):
    slots, sources = targets.shape
    parts = sems.shape[0] - 2
    step = sources // parts
    small = [
        pltpu.make_async_copy(targets_hbm, targets, sems.at[parts]),
        pltpu.make_async_copy(counts_hbm, counts, sems.at[parts + 1]),
    ]
    large = [
        pltpu.make_async_copy(
            partials_hbm.at[i * step : (i + 1) * step], partials.at[i * step : (i + 1) * step], sems.at[i]
        )
        for i in range(parts)
    ]
    for copy in small + large:
        copy.start()
    for copy in small:
        copy.wait()
    codes = jnp.where(iota((slots, sources), 0) < counts[...], targets[...], -1)
    codes = jnp.concatenate([codes] * (128 // slots), axis=0)
    codes = jnp.where(iota(codes.shape, 0) // slots == place[2] % (128 // slots), codes, 0)
    row = codes.astype(F32).T
    sent = []
    for i in range(parts):
        large[i].wait()
        for s in range(i * step, (i + 1) * step):
            out[17 * s : 17 * s + 8, :] = partials[s, :, :128]
            out[17 * s + 8 : 17 * s + 16, :] = partials[s, :, 128:]
            out[17 * s + 16 : 17 * s + 17, :] = row[s : s + 1, :]
        span = slice(17 * step * i, 17 * step * (i + 1))
        sent.append(pltpu.make_async_copy(out.at[span], out_hbm.at[span], out_sems.at[i]))
        sent[-1].start()
    for copy in sent:
        copy.wait()


def unpack(payload):
    sources = payload.shape[0] // 17
    left, right, codes = [], [], []
    for g in range(sources // 16):
        row = jnp.zeros((1, 128), F32)
        for s in range(16 * g, 16 * g + 16):
            left.append(payload[17 * s : 17 * s + 8, :])
            right.append(payload[17 * s + 8 : 17 * s + 16, :])
            row = row + payload[17 * s + 16 : 17 * s + 17, :]
        codes.append(row)
    values = jnp.concatenate([jnp.concatenate(left, axis=0), jnp.concatenate(right, axis=0)], axis=1)
    return halves(values), jnp.concatenate(codes, axis=1).astype(jnp.int32)


def hot_of(code, rows, u):
    return (code == iota((rows, code.shape[1]), 0) * 4 + u).astype(F32).astype(BF16)


def rows_hot(chosen, rows):
    return (chosen[:, 0:1] == iota((chosen.shape[0], rows), 1)).astype(F32).astype(BF16)


def assemble_kernel(payload, front, own, matrix_out, pivots_out):
    (high, low), code = unpack(payload)
    rows = front.shape[0]
    pivot_hot = rows_hot(own, rows)
    for u in range(4):
        cols = slice(u * B, (u + 1) * B)
        hot = hot_of(code, rows, u)
        tile = front[:, cols] + (dot(hot, high) + dot(hot, low))
        matrix_out[:, cols] = tile
        pivots_out[:, cols] = pick(pivot_hot, tile)


def front_kernel(front, give, out):
    keep = give.shape[0]
    hot = rows_hot(give, front.shape[0])
    for u in range(4):
        out[u * keep : (u + 1) * keep, :] = pick(hot, front[:, u * B : (u + 1) * B])


def lead_kernel(payload, front_rows, give, send_first, send_rest):
    (high, low), code = unpack(payload)
    keep = give.shape[0]
    chosen = give[:, 0:1] * 4
    hot = jnp.concatenate([(chosen + u == code).astype(F32) for u in range(4)], axis=0).astype(BF16)
    sums = front_rows[...] + (dot(hot, high) + dot(hot, low))
    for i in range(send_first.shape[0] // keep):
        send_first[i * keep : (i + 1) * keep, :] = sums[:keep]
    for u in range(1, 4):
        send_rest[:, (u - 1) * B : u * B] = sums[u * keep : (u + 1) * keep]


def tile_kernel(payload, front, first_out):
    (high, low), code = unpack(payload)
    hot = hot_of(code, front.shape[0], 0)
    first_out[...] = front[...] + (dot(hot, high) + dot(hot, low))


def tiles_kernel(payload, front, rest_out, done_out):
    done_out[...] = jnp.zeros_like(done_out)
    (high, low), code = unpack(payload)
    for u in range(1, 4):
        cols = slice(u * B, (u + 1) * B)
        hot = hot_of(code, front.shape[0], u)
        rest_out[:, cols.start - B : cols.stop - B] = front[:, cols] + (dot(hot, high) + dot(hot, low))


def join_kernel(tiles_done, sort_done, a0, a1, a2, a3, out):
    size = a0.shape[0]
    for i, a in enumerate((a0, a1, a2, a3)):
        out[i * size : (i + 1) * size, :] = a[...]


def sort_first_kernel(r_done, slot, gathered, out, done_out):
    done_out[...] = jnp.zeros_like(done_out)
    out[...] = pick(slot[...], gathered[...])


def inverse_of(diag):
    eye = iota((B, B), 0) == iota((B, B), 1)
    only = jnp.where(eye, diag, 0.0)
    by_row = 1.0 / jnp.sum(only, axis=1, keepdims=True)
    by_col = 1.0 / jnp.sum(only, axis=0, keepdims=True)
    two = jnp.where(eye, 2.0, 0.0)
    x = by_row * (two - diag * by_col)
    xs = halves(x)
    return dot3(xs, halves(two - dot3(halves(diag), xs)))


def panel_kernel(place, w_own, w_other, r_own, r_other, active, half_out, tile_out):
    even = place[1] % 2 == 0
    w0 = jnp.where(even, w_own[...], w_other[...])
    w1 = jnp.where(even, w_other[...], w_own[...])
    r0 = jnp.where(even, r_own[...], r_other[...])
    r1 = jnp.where(even, r_other[...], r_own[...])
    act0 = active[0][:, 0:1]
    act1 = active[1][:, 0:1]
    inv0 = halves(inverse_of(w0[:B]))
    m0w = dot3(halves(w0[B:]), inv0)
    m0w_s = halves(m0w)
    p01 = halves(w1[:B])
    inv1 = halves(inverse_of(w1[B:] - dot3(m0w_s, p01)))
    m0 = dot3(halves(r0), inv0)
    m0a = jnp.where(act0 > 0, m0, 0.0)
    r1 = r1 - dot3(halves(m0a), p01)
    m1 = dot3(halves(r1), inv1)
    n1 = jnp.where(act1 > 0, m1, 0.0)
    n0 = m0a - dot3(halves(n1), m0w_s)
    half_out[...] = jnp.where(even, n0, n1)
    tile_out[...] = jnp.where(even, jnp.where(act0 > 0, m0, r0), jnp.where(act1 > 0, m1, r1))


def update_kernel(place, matrix, pivots, n_own, n_other, tile, out):
    even = place[1] % 2 == 0
    n0 = halves(jnp.where(even, n_own[...], n_other[...]))
    n1 = halves(jnp.where(even, n_other[...], n_own[...]))
    for u in range(4):
        cols = slice(u * B, (u + 1) * B)
        new = matrix[:, cols] - (
            dot3(n0, halves(pivots[:B, cols])) + dot3(n1, halves(pivots[B:, cols]))
        )
        if u == 0:
            new = jnp.where(place[1] < 2, tile[...], new)
        out[:, cols] = new


def finish_kernel(
    place, n_early, n_late, o_early, o_late, tile_hbm, first_hbm, w_first_hbm, rest_hbm, xy_hbm,
    a0, a1, a2, a3, out_hbm, n_own, n_other, first, w_first, tile, rest, xy, w_rest, out, sems
):
    q = place[1]
    even = q % 2 == 0
    copy = pltpu.make_async_copy
    for early, first_of, second_of, target, at in (
        ((q < 3) | (q == 7), n_early, n_late, n_own, 0),
        ((q < 2) | (q == 3) | (q == 6), o_early, o_late, n_other, 1),
    ):

        @pl.when(early)
        def _():
            copy(first_of, target, sems.at[at]).start()

        @pl.when(jnp.logical_not(early))
        def _():
            copy(second_of, target, sems.at[at]).start()

    size = a0.shape[0]
    moves = [
        copy(xy_hbm, xy, sems.at[2]),
        copy(w_first_hbm, w_first, sems.at[3]),
        copy(first_hbm, first, sems.at[4]),
        copy(a0, w_rest.at[:size], sems.at[6]),
        copy(a1, w_rest.at[size : 2 * size], sems.at[7]),
        copy(a2, w_rest.at[2 * size : 3 * size], sems.at[8]),
        copy(a3, w_rest.at[3 * size :], sems.at[9]),
        copy(rest_hbm, rest, sems.at[10]),
    ]
    for move in moves[:2] + moves[3:]:
        move.start()

    @pl.when(q < 2)
    def _():
        copy(tile_hbm, first, sems.at[4]).start()

    @pl.when(q >= 2)
    def _():
        moves[2].start()

    copy(n_early, n_own, sems.at[0]).wait()
    copy(o_early, n_other, sems.at[1]).wait()
    h0, l0 = halves(jnp.where(even, n_own[...], n_other[...]))
    h1, l1 = halves(jnp.where(even, n_other[...], n_own[...]))
    rows = first.shape[0]
    half = out.shape[1]
    block = half // 2
    moves[0].wait()
    n_high = jnp.concatenate([h0, h1], axis=1)
    n_low = jnp.concatenate([l0, l1], axis=1)
    hot = xy[...]
    high = dot(n_high, hot).astype(BF16)
    low = dot(n_low, hot).astype(BF16)
    for move in moves[1:3]:
        move.wait()
    new = first[...] - jnp.where(q < 2, 0.0, dot3((n_high, n_low), halves(w_first[...])))
    for t in range(rows // half):
        out[t, :, 0, :] = new[t * half : (t + 1) * half]
    for move in moves[3:]:
        move.wait()
    w = [halves(w_rest[:, u * B : (u + 1) * B]) for u in range(3)]
    sent = []
    for i in range(rows // block):
        t, at = i * block // half, i * block % half
        span = slice(i * block, (i + 1) * block)
        for u in range(1, 4):
            cols = slice((u - 1) * B, u * B)
            out[t, at : at + block, u, :] = rest[span, cols] - dot3((high[span], low[span]), w[u - 1])
        done = copy(out.at[t, at : at + block], out_hbm.at[t, at : at + block], sems.at[11 + i])
        done.start()
        sent.append(done)
    for done in sent:
        done.wait()


def call(kernel, outs, n_in, scalars=1, outs_in_smem=0, flops=0, moved=0):
    specs = jax.tree.map(lambda _: VM, outs)
    if outs_in_smem:
        specs = specs[:-outs_in_smem] + (SM,) * outs_in_smem
    return pl.pallas_call(
        kernel,
        out_shape=outs,
        in_specs=[SM] * scalars + [VM] * (n_in - scalars),
        out_specs=specs,
        cost_estimate=pl.CostEstimate(flops=flops, bytes_accessed=moved, transcendentals=0),
        **PARAMS,
    )


def shaped(*shape, dtype=F32):
    return jax.ShapeDtypeStruct(shape, dtype)


def core_swap(x):
    return lax.ppermute(x, "pcol", [(i, i ^ 1) for i in range(lax.axis_size("pcol"))])


def shift_x(step):
    return [(p, p // 4 * 4 + (p + step) % 4) for p in range(16)]


def shift_y(step):
    return [(p, (p + 4 * step) % 16) for p in range(16)]


def ring(x, shift):
    return [x] + [lax.ppermute(x, "prow", shift(step)) for step in (1, -1, 2)]


def spread_z(x, z):
    one = lax.ppermute(x, "pcol", [(0, 2), (1, 3)])
    three = lax.ppermute(x, "pcol", [(0, 6), (1, 7)])
    two = lax.ppermute(x, "pcol", [(0, 4), (1, 5)])
    return jnp.where(z == 0, x, jnp.where(z == 1, one, jnp.where(z == 2, two, three)))


def body(front, partials, targets, counts, local_picks, level_picks, order):
    rows = front.shape[0] * front.shape[1]
    cols = front.shape[2] * front.shape[3]
    p = lax.axis_index("prow")
    q = lax.axis_index("pcol")
    me = p * lax.axis_size("pcol") + q
    place = jnp.stack([p, q, me]).astype(jnp.int32)
    sources = partials.shape[1]
    slots = partials.shape[2]

    payload = pl.pallas_call(
        pack_kernel,
        out_shape=shaped(sources * 17, 128),
        in_specs=[SM, HBM, HBM, HBM],
        out_specs=HBM,
        scratch_shapes=[
            pltpu.VMEM((sources, slots, B), F32),
            pltpu.VMEM((slots, sources), jnp.int32),
            pltpu.VMEM((1, sources), jnp.int32),
            pltpu.VMEM((sources * 17, 128), F32),
            pltpu.SemaphoreType.DMA((10,)),
            pltpu.SemaphoreType.DMA((8,)),
        ],
        cost_estimate=pl.CostEstimate(flops=10**6, bytes_accessed=2 * 10**6, transcendentals=0),
        **ALONE,
    )(place, partials[0], targets[0].T, counts).reshape(sources * 17, 1, 128)
    payload = lax.all_to_all(payload, ("prow", "pcol"), 0, 0, tiled=True).reshape(sources * 17, 128)

    copies = lax.axis_size("prow") * KEEP
    hots = shaped(2 * B, copies, dtype=BF16)
    own, active, give, slot, xy, fits = call(
        index_kernel,
        (
            shaped(2 * B, 128, dtype=jnp.int32),
            shaped(2, rows, 128),
            shaped(KEEP, 128, dtype=jnp.int32),
            hots,
            hots,
            shaped(1, dtype=jnp.int32),
        ),
        4,
        outs_in_smem=1,
        flops=10**9,
        moved=10**6,
    )(place, local_picks, level_picks, order)
    front, own = lax.optimization_barrier((front, own))
    flat = front.reshape(rows, cols)
    share_rows = 2 * B // lax.axis_size("prow")

    front_rows = call(front_kernel, shaped(4 * KEEP, B), 2, scalars=0, flops=10**8, moved=3 * 10**6)(flat, give)

    send_first, send_rest = call(
        lead_kernel, (shaped(copies, B), shaped(KEEP, cols - B)), 3, scalars=0, flops=10**8, moved=2 * 10**6
    )(payload, front_rows, give)
    w_first = lax.all_to_all(send_first, "prow", 0, 0, tiled=True)
    whole = lambda *shape: pl.BlockSpec(shape, lambda i: (0, 0))
    first = pl.pallas_call(
        tile_kernel,
        out_shape=shaped(rows, B),
        grid=(1,),
        in_specs=[whole(*payload.shape), whole(rows, B)],
        out_specs=whole(rows, B),
        cost_estimate=pl.CostEstimate(flops=10**9, bytes_accessed=2 * 10**6, transcendentals=0),
        **PARAMS,
    )(payload, flat)
    r_other = core_swap(first)
    rest, done = call(
        tiles_kernel,
        (shaped(rows, cols - B), shaped(8, 128)),
        2,
        scalars=0,
        flops=4 * 10**9,
        moved=6 * 10**6,
    )(payload, flat)
    w_first, sorted_ = call(
        sort_first_kernel, (shaped(2 * B, B), shaped(8, 128)), 3, scalars=0, flops=10**8, moved=10**6
    )(r_other, slot, w_first)
    joined = call(join_kernel, shaped(4 * KEEP, cols - B), 6, scalars=0, moved=10**6)(
        done, sorted_, *ring(send_rest, shift_x)
    )
    w_parts = ring(joined, shift_y)

    def panels(w_first, first, r_other, active, place, joined):
        w_other = core_swap(w_first)
        half, tile = call(
            panel_kernel, (shaped(rows, B), shaped(rows, B)), 6, flops=2 * 10**9, moved=4 * 10**6
        )(place, w_first, w_other, first, r_other, active)
        q = place[1]
        step = lax.ppermute(half, "pcol", [(0, 2), (1, 7)])
        n_early = jnp.where((q == 2) | (q == 7), step, half)
        n_late = lax.ppermute(n_early, "pcol", [(1, 3), (0, 6), (2, 4), (7, 5)])
        o_early = lax.ppermute(n_early, "pcol", [(0, 1), (1, 0), (2, 3), (7, 6)])
        o_late = lax.ppermute(n_late, "pcol", [(3, 2), (6, 7), (4, 5), (5, 4)])
        return n_early, n_late, o_early, o_late, tile

    def nothing(w_first, first, r_other, active, place, joined):
        return (jnp.zeros((rows, B), F32),) * 5

    parts = lax.cond(fits[0] == 1, panels, nothing, w_first, first, r_other, active, place, joined)

    def finish(payload, flat, own, active, place, *arrays):
        return pl.pallas_call(
            finish_kernel,
            out_shape=shaped(*front.shape),
            in_specs=[SM] + [HBM] * 13,
            out_specs=HBM,
            scratch_shapes=[
                pltpu.VMEM((rows, B), F32),
                pltpu.VMEM((rows, B), F32),
                pltpu.VMEM((rows, B), F32),
                pltpu.VMEM((2 * B, B), F32),
                pltpu.VMEM((rows, B), F32),
                pltpu.VMEM((rows, cols - B), F32),
                pltpu.VMEM((2 * B, copies), BF16),
                pltpu.VMEM((copies, cols - B), F32),
                pltpu.VMEM(front.shape, F32),
                pltpu.SemaphoreType.DMA((15,)),
            ],
            cost_estimate=pl.CostEstimate(flops=4 * 10**9, bytes_accessed=8 * 10**6, transcendentals=0),
            **ALONE,
        )(place, *arrays)

    def add_up(payload, flat, own, active, place, *arrays):
        matrix, pivots = call(
            assemble_kernel, (shaped(rows, cols), shaped(2 * B, cols)), 3, scalars=0, flops=4 * 10**9, moved=8 * 10**6
        )(payload, flat, own)
        r_own = matrix[:, :B]
        r_other = core_swap(r_own)
        share = lax.all_to_all(pivots, "prow", 0, 0, tiled=True).reshape(-1, share_rows, cols).sum(axis=0)
        pivots = lax.all_to_all(jnp.tile(share, (lax.axis_size("prow"), 1)), "prow", 0, 0, tiled=True)
        w_own = pivots[:, :B]
        w_other = core_swap(w_own)
        half, tile = call(
            panel_kernel, (shaped(rows, B), shaped(rows, B)), 6, flops=2 * 10**9, moved=4 * 10**6
        )(place, w_own, w_other, r_own, r_other, active)
        n_own = spread_z(half, place[1] // 2)
        n_other = core_swap(n_own)
        out = call(update_kernel, shaped(rows, cols), 6, flops=2 * 10**9, moved=8 * 10**6)(
            place, matrix, pivots, n_own, n_other, tile
        )
        return out.reshape(front.shape)

    return lax.cond(
        fits[0] == 1,
        finish,
        add_up,
        payload,
        flat,
        own,
        active,
        place,
        *parts,
        first,
        w_first,
        rest,
        xy,
        *w_parts,
    )


def solution(mesh):
    placed = (
        P(None, "prow", None, "pcol"),
        P(("prow", "pcol"), None, None, None),
        P(("prow", "pcol"), None, None),
        P(("prow", "pcol"), None),
        P(),
        P(),
        P(),
    )
    return jax.shard_map(
        body, mesh=mesh, in_specs=placed, out_specs=P(None, "prow", None, "pcol"), check_vma=False
    )
```
